32 devices in a mesh: dp: 4 (over y, core), seq: 2 (over x), mp: 4 (over z).
Axes of the slice: x: 2, y: 2, z: 4, core: 2. Of those that a mesh axis runs over, the one named last changes fastest.
Arguments:
- tokens: bfloat16 [8, 4096, 768], P('dp', 'seq'), may hold values from -6 to 6
- places: int32 [8, 4096], P('dp', 'seq'), may hold values from 0 to 4095, as said below
- w_qkv: bfloat16 [3, 768, 768], P(None, ('dp', 'seq'), 'mp'), may hold values from -0.21875 to 0.21875
- b_qkv: bfloat16 [3, 12, 64], P(None, 'mp', ('dp', 'seq')), may hold values from -3 to 3
- w_dense: bfloat16 [768, 768], P('mp', ('dp', 'seq')), may hold values from -6 to 6
- b_dense: bfloat16 [768], P(('dp', 'seq')), may hold values from -3 to 3
- w_up: bfloat16 [768, 3072], P(('dp', 'seq'), 'mp'), may hold values from -0.21875 to 0.21875
- b_up: bfloat16 [24, 128], P('mp', ('dp', 'seq')), may hold values from -3 to 3
- w_down: bfloat16 [3072, 768], P('mp', ('dp', 'seq')), may hold values from -0.109375 to 0.109375
- b_down: bfloat16 [768], P(('dp', 'seq')), may hold values from -3 to 3
- norm1_gain: bfloat16 [768], P(('dp', 'seq')), may hold values from 0.5 to 1.5
- norm1_bias: bfloat16 [768], P(('dp', 'seq')), may hold values from -2 to 2
- norm2_gain: bfloat16 [768], P(('dp', 'seq')), may hold values from 0.5 to 1.5
- norm2_bias: bfloat16 [768], P(('dp', 'seq')), may hold values from -2 to 2
- out_grad: bfloat16 [8, 4096, 768], P('dp', 'seq'), may hold values from -6 to 6
Outputs:
- mixed: bfloat16 [8, 4096, 768], P('dp', 'seq')
- grad_tokens: bfloat16 [8, 4096, 768], P('dp', 'seq')
- grad_w_qkv: float32 [3, 768, 768], P(None, ('dp', 'seq'), 'mp')
- grad_b_qkv: float32 [3, 12, 64], P(None, 'mp', ('dp', 'seq'))
- grad_w_dense: float32 [768, 768], P('mp', ('dp', 'seq'))
- grad_b_dense: float32 [768], P(('dp', 'seq'))
- grad_w_up: float32 [768, 3072], P(('dp', 'seq'), 'mp')
- grad_b_up: float32 [24, 128], P('mp', ('dp', 'seq'))
- grad_w_down: float32 [3072, 768], P('mp', ('dp', 'seq'))
- grad_b_down: float32 [768], P(('dp', 'seq'))
- grad_norm1_gain: float32 [768], P(('dp', 'seq'))
- grad_norm1_bias: float32 [768], P(('dp', 'seq'))
- grad_norm2_gain: float32 [768], P(('dp', 'seq'))
- grad_norm2_bias: float32 [768], P(('dp', 'seq'))
The draws below stay inside these ranges and needn't reach their ends.
Inputs may be any that keep to these rules, and one draw needn't show every extreme that they name: Each row places[s] is a permutation of the positions of one sequence. The 2048 stored tokens of a sequence on one index of seq are two runs of 1024 consecutive positions in increasing order: run t and run 2 * 2 - 1 - t of the sequence, with t different for every index of seq and drawn per sequence.
All inputs are finite; a program needn't handle non-finite values.
Results may differ from the reference program's by a relative error of at most 0.011.
Values may be sent and summed in bfloat16 or wider, within the bound.
No kernel may reach another device: no remote copies, remote signals or barrier semaphores. Data moves between devices by JAX's collectives and lax.ppermute only.
A program may use at most 512 MiB of HBM per device.

```python
import jax
import jax.numpy as jnp
from jax import lax

D = 768
H = 12
HD = 64
FF = 3072
ROT = 16
LEN = 4096
SEG = 2048
SEQS = 8


def draw_places(key, part):
    key = jax.random.fold_in(key, 11)
    shard_count = LEN // SEG
    block_len = SEG // 2
    row_ids = jnp.arange(LEN, dtype=jnp.int32)
    device = row_ids // SEG
    offset = row_ids % SEG
    upper_half = offset // block_len
    within = offset % block_len

    def one_sequence(seq_key):
        block_order = jax.random.permutation(seq_key, shard_count).astype(jnp.int32)
        chosen = block_order[device]
        block_index = jnp.where(upper_half == 0, chosen, 2 * shard_count - 1 - chosen)
        return (block_index * block_len + within).astype(jnp.int32)
    seq_keys = jax.random.split(key, SEQS)
    return jax.vmap(one_sequence)(seq_keys)


def level_of(stream_key, dims, shards, least, high):
    factor_of, own = 1.0, jax.random.fold_in(stream_key, 6)
    for position, shards_of in shards:
        steps = jnp.exp(jax.random.uniform(jax.random.fold_in(own, position), (shards_of,), jnp.float32, least / len(shards), high / len(shards)))
        factor_of = factor_of * jnp.repeat(steps, dims[position] // shards_of).reshape([-1 if axis == position else 1 for axis in range(len(dims))])
    return factor_of


def gaussian(stream_key, dims, scale, reach, cuts=(), kind=jnp.bfloat16):
    loudness = level_of(stream_key, dims, cuts, -0.22, 0.18) if cuts else 1.0
    drawn = jax.random.normal(stream_key, dims, jnp.float32) * scale * loudness
    return jnp.minimum(jnp.maximum(drawn, -reach), reach).astype(kind)


def setup_inputs(seed: int = 0) -> dict:
    seeds = jax.random.split(jax.random.key(seed), 16)
    tokens = gaussian(seeds[0], (SEQS, LEN, D), 1.0, 6.0, ((0, 4), (1, 2)))
    places = draw_places(jax.random.fold_in(seeds[15], 71), 0)
    w_qkv = gaussian(seeds[2], (3, D, D), D ** -0.5, 0.21875, ((1, 8), (2, 4)))
    b_qkv = gaussian(seeds[3], (3, H, HD), 0.5, 3.0, ((1, 4), (2, 8)))
    w_dense = gaussian(seeds[4], (D, D), (max(1, 2 * D // LEN)) ** -0.5, 6.0, ((0, 4), (1, 8)))
    b_dense = gaussian(seeds[5], (D,), 0.5, 3.0, ((0, 8),))
    w_up = gaussian(seeds[6], (D, FF), D ** -0.5, 0.21875, ((0, 8), (1, 4)))
    b_up = gaussian(seeds[7], (FF // 128, 128), 0.5, 3.0, ((0, 4), (1, 8)))
    w_down = gaussian(seeds[8], (FF, D), FF ** -0.5, 0.109375, ((0, 4), (1, 8)))
    b_down = gaussian(seeds[9], (D,), 0.5, 3.0, ((0, 8),))
    norm1_gain = jnp.clip(1.0 + 0.1 * jax.random.normal(seeds[10], (D,), jnp.float32), 0.5, 1.5).astype(jnp.bfloat16)
    norm1_bias = gaussian(seeds[11], (D,), 0.3, 2.0, ((0, 8),))
    norm2_gain = jnp.clip(1.0 + 0.1 * jax.random.normal(seeds[12], (D,), jnp.float32), 0.5, 1.5).astype(jnp.bfloat16)
    norm2_bias = gaussian(seeds[13], (D,), 0.3, 2.0, ((0, 8),))
    out_grad = gaussian(seeds[14], (SEQS, LEN, D), 1.0, 6.0, ((0, 4), (1, 2)))
    return {"tokens": tokens, "places": places, "w_qkv": w_qkv, "b_qkv": b_qkv, "w_dense": w_dense, "b_dense": b_dense, "w_up": w_up, "b_up": b_up, "w_down": w_down, "b_down": b_down, "norm1_gain": norm1_gain, "norm1_bias": norm1_bias, "norm2_gain": norm2_gain, "norm2_bias": norm2_bias, "out_grad": out_grad}


@jax.custom_vjp
def low(v):
    return lax.optimization_barrier(v.astype(jnp.bfloat16)).astype(jnp.float32)

@jax.custom_vjp
def low_back(v):
    return v

def low_keep(v):
    return (low(v), None)

def low_pass(kept, grad):
    return (grad,)

def back_keep(v):
    return (v, None)

def back_low(kept, grad):
    return (low(grad),)
low.defvjp(low_keep, low_pass)
low_back.defvjp(back_keep, back_low)
norm_eps = 1e-05
masked_value = -1e+30

def layer_norm(values, gain, shift):
    centre = lax.optimization_barrier(jnp.mean(values, axis=-1, keepdims=True))
    deviate = values - centre
    spread = lax.optimization_barrier(jnp.mean(deviate * deviate, axis=-1, keepdims=True))
    return deviate * lax.rsqrt(spread + norm_eps) * gain + shift

def rotate(values, positions):
    half_dims = ROT // 2
    frequency = jnp.power(jnp.float32(10000.0), -2.0 * jnp.arange(half_dims, dtype=jnp.float32) / ROT)
    angles = positions.astype(jnp.float32)[:, None] * frequency[None, :]
    cosines = jnp.concatenate([jnp.cos(angles), jnp.cos(angles)], axis=-1)[:, None, :]
    sine_part = jnp.concatenate([jnp.sin(angles), jnp.sin(angles)], axis=-1)[:, None, :]
    leading = values[..., :ROT]
    turned = jnp.concatenate([-leading[..., half_dims:], leading[..., :half_dims]], axis=-1)
    return jnp.concatenate([leading * cosines + turned * sine_part, values[..., ROT:]], axis=-1)

def attention_block(query_block, block_places, keys, values, key_places):
    scores = jnp.einsum('qhd,khd->hqk', query_block, keys, precision=lax.Precision.HIGHEST) * HD ** (-0.5)
    scores = low_back(scores)
    visible = key_places[None, None, :] <= block_places[None, :, None]
    scores = jnp.where(visible, scores, masked_value)
    row_max = lax.optimization_barrier(jnp.max(scores, axis=-1, keepdims=True))
    log_total = row_max + jnp.log(lax.optimization_barrier(jnp.sum(jnp.exp(scores - row_max), axis=-1, keepdims=True)))
    soft_low = low(jnp.exp(scores - log_total))
    return jnp.einsum('hqk,khd->qhd', soft_low, values, precision=lax.Precision.HIGHEST)

def one_sequence(x_seq, seq_places, weights):
    qkv_w, qkv_b, dense_w, dense_b, up_w, up_b, down_w, down_b, gain_one, shift_one, gain_two, shift_two = weights
    norm_one = low(layer_norm(x_seq, gain_one, shift_one))
    norm_two = low(layer_norm(x_seq, gain_two, shift_two))
    projected = jnp.einsum('td,ide->ite', norm_one, qkv_w, precision=lax.Precision.HIGHEST) + qkv_b.reshape(3, 1, D)
    projected = low_back(projected).reshape(3, LEN, H, HD)
    queries = low(rotate(projected[0], seq_places))
    keys = low(rotate(projected[1], seq_places))
    values = low(projected[2])
    rows_block = min(512, LEN)

    def block_attention(pair):
        return attention_block(pair[0], pair[1], keys, values, seq_places)
    attended = lax.map(jax.checkpoint(block_attention), (queries.reshape(LEN // rows_block, rows_block, H, HD), seq_places.reshape(LEN // rows_block, rows_block)))
    attended = low(low_back(attended.reshape(LEN, D)))
    hidden_pre = low_back(jnp.dot(norm_two, up_w, precision=lax.Precision.HIGHEST, preferred_element_type=jnp.float32) + up_b.reshape(FF))
    activated = low(jax.nn.gelu(hidden_pre, approximate=False))
    attn_part = jnp.dot(attended, dense_w, precision=lax.Precision.HIGHEST, preferred_element_type=jnp.float32) + dense_b
    mlp_part = jnp.dot(activated, down_w, precision=lax.Precision.HIGHEST, preferred_element_type=jnp.float32) + down_b
    return x_seq + attn_part + mlp_part

def reference(tokens, places, w_qkv, b_qkv, w_dense, b_dense, w_up, b_up, w_down, b_down, norm1_gain, norm1_bias, norm2_gain, norm2_bias, out_grad):
    params = tuple((param.astype(jnp.float32) for param in (w_qkv, b_qkv, w_dense, b_dense, w_up, b_up, w_down, b_down, norm1_gain, norm1_bias, norm2_gain, norm2_bias)))
    inputs = tokens.astype(jnp.float32)

    def forward(x_all, *weights):

        def per_sequence(carry, pair):
            return (carry, one_sequence(pair[0], pair[1], weights))
        carry_out, result = lax.scan(per_sequence, jnp.zeros((), jnp.float32), (x_all, places))
        return result
    mixed, pullback = jax.vjp(forward, inputs, *params)
    grads = pullback(out_grad.astype(jnp.float32))
    return (mixed.astype(jnp.bfloat16), grads[0].astype(jnp.bfloat16), grads[1], grads[2], grads[3], grads[4], grads[5], grads[6], grads[7], grads[8], grads[9], grads[10], grads[11], grads[12])
```

```python
import functools

import jax
import jax.numpy as jnp
from jax import lax
from jax.experimental import pallas as pl
from jax.experimental.pallas import tpu as pltpu
from jax.sharding import Mesh
from jax.sharding import PartitionSpec as P

HD = 64
ROT = 16
LANES = 128
F32 = jnp.float32
BF16 = jnp.bfloat16
LOG2E = 1.4426950408889634
norm_eps = 1e-05
masked_value = -1e30
vmem_bytes = 60 * 2**20

NN = (((1,), (0,)), ((), ()))
NT = (((1,), (1,)), ((), ()))
TN = (((0,), (0,)), ((), ()))


def dot(left, right, dims):
    return lax.dot_general(left, right, dims, preferred_element_type=F32)


def normalise(rows):
    centre = jnp.mean(rows, axis=-1, keepdims=True)
    deviate = rows - centre
    spread = jnp.mean(deviate * deviate, axis=-1, keepdims=True)
    scale = lax.rsqrt(spread + norm_eps)
    return deviate * scale, scale


def turn(chunk, cosines, sine_low, sine_high):
    half = ROT // 2
    return (
        chunk * cosines
        + pltpu.roll(chunk, LANES - half, 1) * sine_low
        + pltpu.roll(chunk, half, 1) * sine_high
    )


def whole(shape):
    return pl.BlockSpec(shape, lambda *_: (0,) * len(shape))


def params(**kwargs):
    return pltpu.CompilerParams(vmem_limit_bytes=vmem_bytes, **kwargs)


def front_kernel(
    which, x_ref, dy_ref, w_ref, wb_ref, dense_ref, gain_ref, shift_ref, cos_ref, low_ref, high_ref,
    q_ref, kv_ref, do_ref,
):
    half = q_ref.shape[1]
    xhat, _ = normalise(x_ref[0].astype(F32))
    normed = (xhat * gain_ref[...] + shift_ref[...]).astype(BF16)
    proj = dot(normed, w_ref[...], NN) + wb_ref[...]
    cosines, low, high = cos_ref[...], low_ref[...], high_ref[...]
    for j in range(half // LANES):
        at = slice(j * LANES, (j + 1) * LANES)
        query = turn(proj[:, at], cosines, low, high).astype(BF16)
        q_ref[:, at] = query * BF16(HD**-0.5)
        key = proj[:, half + j * LANES : half + (j + 1) * LANES]
        kv_ref[:, at] = turn(key, cosines, low, high).astype(BF16)
    kv_ref[:, half:] = proj[:, 2 * half :].astype(BF16)
    do_ref[...] = dot(dy_ref[0], dense_ref[...], NN).astype(BF16)


def front(which, x, dy, w, wb, dense, gain, shift, tables):
    _, rows, width = x.shape
    half = dense.shape[1]
    step = min(512, rows)
    chosen = pl.BlockSpec((1, step, width), lambda i, which: (which[0], i, 0))
    by_row = lambda cols: pl.BlockSpec((step, cols), lambda i, *_: (i, 0))
    return pl.pallas_call(
        front_kernel,
        grid_spec=pltpu.PrefetchScalarGridSpec(
            num_scalar_prefetch=1,
            grid=(rows // step,),
            in_specs=[chosen, chosen, whole(w.shape), whole(wb.shape), whole(dense.shape),
                      whole(gain.shape), whole(shift.shape)] + [by_row(LANES)] * 3,
            out_specs=[by_row(half), by_row(2 * half), by_row(half)],
        ),
        out_shape=[
            jax.ShapeDtypeStruct((rows, half), BF16),
            jax.ShapeDtypeStruct((rows, 2 * half), BF16),
            jax.ShapeDtypeStruct((rows, half), BF16),
        ],
        compiler_params=params(),
        cost_estimate=pl.CostEstimate(
            flops=2 * rows * width * 4 * half, bytes_accessed=12 * rows * width, transcendentals=0
        ),
        name="front",
    )(which, x, dy, w, wb, dense, gain, shift, *tables)


def feed_kernel(
    which, x_ref, dy_ref, up_ref, upb_ref, down_ref, gain_ref, shift_ref, gain_col, shift_col,
    part_ref, dx_ref, gup_ref, gdown_ref, vec_ref, gupb_ref,
    up_acc, down_acc, sum_acc, dy_acc,
):
    step = pl.program_id(0)

    @pl.when(step == 0)
    def _():
        up_acc[...] = jnp.zeros_like(up_acc)
        down_acc[...] = jnp.zeros_like(down_acc)
        sum_acc[...] = jnp.zeros_like(sum_acc)
        dy_acc[...] = jnp.zeros_like(dy_acc)

    xhat, _ = normalise(x_ref[0].astype(F32))
    dy = dy_ref[0]
    normed = (xhat * gain_ref[...] + shift_ref[...]).astype(BF16)
    hidden = dot(normed, up_ref[...], NN) + upb_ref[...]
    share = 0.5 * (1.0 + lax.erf(hidden * F32(0.5**0.5)))
    act = (hidden * share).astype(BF16)
    slope = share + hidden * (jnp.exp(hidden * hidden * -0.5) * F32(0.3989422804014327))
    part_ref[...] = dot(act, down_ref[...], NT).astype(part_ref.dtype)
    grad = dot(dy, down_ref[...], NN) * slope
    grad_low = grad.astype(BF16)
    dx_ref[...] = (dot(grad_low, up_ref[...], NT) * gain_ref[...]).astype(dx_ref.dtype)
    up_acc[...] += dot(xhat.astype(BF16), grad_low, TN)
    down_acc[...] += dot(dy, act, TN)
    sum_acc[...] += jnp.sum(grad_low.astype(F32), axis=0, keepdims=True)
    dy_acc[...] += jnp.sum(dy.astype(F32), axis=0, keepdims=True)

    @pl.when(step == pl.num_programs(0) - 1)
    def _():
        sums = sum_acc[...]
        raw = up_acc[...]
        up = up_ref[...].astype(F32)
        gup_ref[...] = (raw * gain_col[...] + shift_col[...] * sums).astype(gup_ref.dtype)
        gdown_ref[...] = down_acc[...].astype(gdown_ref.dtype)
        gupb_ref[...] = sums
        lane = lax.broadcasted_iota(jnp.int32, vec_ref.shape, 1)
        gain_grad = jnp.sum(raw * up, axis=1, keepdims=True)
        shift_grad = jnp.sum(up * sums, axis=1, keepdims=True)
        dy_col = jnp.transpose(jnp.broadcast_to(dy_acc[...], (LANES, dy_acc.shape[1])))
        vec_ref[...] = jnp.where(
            lane == 0, dy_col * 0.5,
            jnp.where(lane == 3, gain_grad, jnp.where(lane == 4, shift_grad, 0.0)),
        )


def feed(which, x, dy, up, upb, down, gain, shift, gain_col, shift_col):
    _, rows, width = x.shape
    units = up.shape[1]
    step = min(256, rows)
    chosen = pl.BlockSpec((1, step, width), lambda i, which: (which[0], i, 0))
    by_row = pl.BlockSpec((step, width), lambda i, *_: (i, 0))
    return pl.pallas_call(
        feed_kernel,
        grid_spec=pltpu.PrefetchScalarGridSpec(
            num_scalar_prefetch=1,
            grid=(rows // step,),
            in_specs=[chosen, chosen, whole(up.shape), whole(upb.shape), whole(down.shape),
                      whole(gain.shape), whole(shift.shape), whole(gain_col.shape), whole(shift_col.shape)],
            out_specs=[by_row, by_row, whole((width, units)), whole((width, units)),
                       whole((width, LANES)), whole((1, units))],
            scratch_shapes=[pltpu.VMEM((width, units), F32), pltpu.VMEM((width, units), F32),
                            pltpu.VMEM((1, units), F32), pltpu.VMEM((1, width), F32)],
        ),
        out_shape=[
            jax.ShapeDtypeStruct((rows, width), BF16),
            jax.ShapeDtypeStruct((rows, width), BF16),
            jax.ShapeDtypeStruct((width, units), BF16),
            jax.ShapeDtypeStruct((width, units), BF16),
            jax.ShapeDtypeStruct((width, LANES), F32),
            jax.ShapeDtypeStruct((1, units), F32),
        ],
        compiler_params=params(),
        cost_estimate=pl.CostEstimate(
            flops=12 * rows * width * units, bytes_accessed=24 * width * units, transcendentals=2 * rows * units
        ),
        name="feed",
    )(which, x, dy, up, upb, down, gain, shift, gain_col, shift_col)


def lane_fold(values, combine):
    total = values[:, :LANES]
    for j in range(1, values.shape[1] // LANES):
        total = combine(total, values[:, j * LANES : (j + 1) * LANES])
    return total


def attention_kernel(
    runs, slots, q_ref, g_ref, k_ref, v_ref, o_ref, dq_ref, dk_ref, dv_ref,
    score_ref, soft_ref, acc_ref, *, block, per_run,
):
    step = pl.program_id(1)

    @pl.when(step == 0)
    def _():
        dk_ref[...] = jnp.zeros_like(dk_ref)
        dv_ref[...] = jnp.zeros_like(dv_ref)

    full = runs[step // per_run] * per_run + step % per_run
    lane = lax.broadcasted_iota(jnp.int32, (block, LANES), 1)
    heads = (lane < HD, lane >= HD)
    both_q, both_g = q_ref[...], g_ref[...]
    queries = [jnp.where(mine, both_q, jnp.zeros_like(both_q)) for mine in heads]
    grads = [jnp.where(mine, both_g, jnp.zeros_like(both_g)) for mine in heads]

    def rows_of(at):
        start = (slots[at // per_run] * per_run + at % per_run) * block
        return pl.ds(pl.multiple_of(start, block), block)

    def score(at, tops, masked):
        keys = k_ref[rows_of(at), :]
        out = []
        for h in range(2):
            scores = dot(queries[h], keys, NT)
            if masked:
                row = lax.broadcasted_iota(jnp.int32, (block, block), 0)
                col = lax.broadcasted_iota(jnp.int32, (block, block), 1)
                scores = jnp.where(col <= row, scores, masked_value)
            score_ref[h, at] = scores
            out.append(jnp.maximum(tops[h], lane_fold(scores, jnp.maximum)))
        return tuple(out)

    least = jnp.full((block, LANES), masked_value, F32)
    tops = lax.fori_loop(0, full, lambda at, carry: score(at, carry, False), (least, least))
    tops = score(full, tops, True)
    tops = [jnp.max(top, axis=1, keepdims=True) * F32(LOG2E) for top in tops]

    acc_ref[...] = jnp.zeros_like(acc_ref)

    def weigh(at, totals):
        values = v_ref[rows_of(at), :]
        out = []
        for h in range(2):
            soft = jnp.exp2(score_ref[h, at] * F32(LOG2E) - tops[h])
            out.append(totals[h] + lane_fold(soft, jnp.add))
            soft_low = soft.astype(BF16)
            soft_ref[h, at] = soft_low
            acc_ref[h] += dot(soft_low, values, NN)
        return tuple(out)

    nought = jnp.zeros((block, LANES), F32)
    totals = lax.fori_loop(0, full + 1, weigh, (nought, nought))
    shares = [1.0 / jnp.sum(total, axis=1, keepdims=True) for total in totals]
    attended = jnp.where(heads[0], acc_ref[0] * shares[0], acc_ref[1] * shares[1])
    o_ref[...] = attended.astype(o_ref.dtype)
    product = attended * both_g.astype(F32)
    row_terms = [
        jnp.sum(jnp.where(heads[h], product, 0.0), axis=1, keepdims=True) * shares[h] for h in range(2)
    ]
    scaled = [(grads[h].astype(F32) * shares[h]).astype(BF16) for h in range(2)]

    acc_ref[...] = jnp.zeros_like(acc_ref)

    def back(at, carry):
        there = rows_of(at)
        keys, values = k_ref[there, :], v_ref[there, :]
        key_terms, value_terms = [], []
        for h in range(2):
            soft_low = soft_ref[h, at]
            grad_soft = dot(scaled[h], values, NT)
            grad_score = (soft_low.astype(F32) * (grad_soft - row_terms[h])).astype(BF16)
            acc_ref[h] += dot(grad_score, keys, NN)
            key_terms.append(dot(grad_score, queries[h], TN))
            value_terms.append(dot(soft_low, scaled[h], TN))
        dk_ref[there, :] += key_terms[0] + key_terms[1]
        dv_ref[there, :] += value_terms[0] + value_terms[1]
        return carry

    lax.fori_loop(0, full + 1, back, 0)
    dq_ref[...] = (jnp.where(heads[0], acc_ref[0], acc_ref[1]) * F32(HD**-0.5)).astype(dq_ref.dtype)


def attention(runs, slots, q, g, kv):
    rows, width = q.shape
    keys = kv.shape[0]
    run_rows = rows // 2
    block = min(512, run_rows)
    per_run = run_rows // block
    pairs = width // LANES
    by_query = pl.BlockSpec((block, LANES), lambda p, i, *_: (i, p))
    return pl.pallas_call(
        functools.partial(attention_kernel, block=block, per_run=per_run),
        grid_spec=pltpu.PrefetchScalarGridSpec(
            num_scalar_prefetch=2,
            grid=(pairs, rows // block),
            in_specs=[
                by_query,
                by_query,
                pl.BlockSpec((keys, LANES), lambda p, i, *_: (0, p)),
                pl.BlockSpec((keys, LANES), lambda p, i, *_: (0, pairs + p)),
            ],
            out_specs=[
                by_query,
                by_query,
                pl.BlockSpec((keys, LANES), lambda p, i, *_: (0, p)),
                pl.BlockSpec((keys, LANES), lambda p, i, *_: (0, p)),
            ],
            scratch_shapes=[
                pltpu.VMEM((2, keys // block, block, block), F32),
                pltpu.VMEM((2, keys // block, block, block), BF16),
                pltpu.VMEM((2, block, LANES), F32),
            ],
        ),
        out_shape=[
            jax.ShapeDtypeStruct((rows, width), BF16),
            jax.ShapeDtypeStruct((rows, width), BF16),
            jax.ShapeDtypeStruct((keys, width), F32),
            jax.ShapeDtypeStruct((keys, width), F32),
        ],
        compiler_params=params(),
        cost_estimate=pl.CostEstimate(
            flops=24 * rows * keys * width, bytes_accessed=24 * keys * width,
            transcendentals=rows * keys * pairs,
        ),
        name="attention",
    )(runs, slots, q, g, kv, kv)


def back_kernel(
    dq_ref, own_k, own_v, got_ref, w_ref, gain_ref, dx_in, cos_ref, low_ref, high_ref, dproj_ref, dx_ref
):
    half = dq_ref.shape[1]
    cosines, low, high = cos_ref[...], low_ref[...], high_ref[...]
    for j in range(half // LANES):
        at = slice(j * LANES, (j + 1) * LANES)
        query = dq_ref[:, at].astype(F32)
        dproj_ref[:, at] = turn(query, cosines, -low, -high).astype(BF16)
        key = own_k[:, at] + got_ref[:, at].astype(F32)
        dproj_ref[:, half + j * LANES : half + (j + 1) * LANES] = turn(key, cosines, -low, -high).astype(BF16)
    dproj_ref[:, 2 * half :] = (own_v[...] + got_ref[:, half:].astype(F32)).astype(BF16)
    summed = dot(dproj_ref[...], w_ref[...], NT) * gain_ref[...] + dx_in[...].astype(F32)
    dx_ref[...] = summed.astype(dx_ref.dtype)


def back(dq, dk, dv, got, w, gain, dx_part, tables):
    rows, half = dq.shape
    width = w.shape[0]
    step = min(512, rows)
    by_row = lambda cols: pl.BlockSpec((step, cols), lambda i: (i, 0))
    return pl.pallas_call(
        back_kernel,
        grid=(rows // step,),
        in_specs=[by_row(half), by_row(half), by_row(half), by_row(2 * half), whole(w.shape),
                  whole(gain.shape), by_row(width)] + [by_row(LANES)] * 3,
        out_specs=[by_row(3 * half), by_row(width)],
        out_shape=[
            jax.ShapeDtypeStruct((rows, 3 * half), BF16),
            jax.ShapeDtypeStruct((rows, width), BF16),
        ],
        compiler_params=params(),
        cost_estimate=pl.CostEstimate(
            flops=6 * rows * width * half, bytes_accessed=12 * rows * width, transcendentals=0
        ),
        name="back",
    )(dq, dk, dv, got, w, gain, dx_part, *tables)


def weight_kernel(
    which, x_ref, dy_ref, dproj_ref, o_ref, w_ref, gain_col, shift_col,
    gqkv_ref, gdense_ref, vec_ref, gb_ref, acc, dense_acc, sum_acc,
):
    step = pl.program_id(0)

    @pl.when(step == 0)
    def _():
        acc[...] = jnp.zeros_like(acc)
        dense_acc[...] = jnp.zeros_like(dense_acc)
        sum_acc[...] = jnp.zeros_like(sum_acc)

    xhat, _ = normalise(x_ref[0].astype(F32))
    dproj = dproj_ref[...]
    acc[...] += dot(xhat.astype(BF16), dproj, TN)
    dense_acc[...] += dot(dy_ref[0], o_ref[...], TN)
    sum_acc[...] += jnp.sum(dproj.astype(F32), axis=0, keepdims=True)

    @pl.when(step == pl.num_programs(0) - 1)
    def _():
        sums, raw, w = sum_acc[...], acc[...], w_ref[...].astype(F32)
        gqkv_ref[...] = (raw * gain_col[...] + shift_col[...] * sums).astype(gqkv_ref.dtype)
        gdense_ref[...] = dense_acc[...].astype(gdense_ref.dtype)
        gb_ref[...] = sums
        lane = lax.broadcasted_iota(jnp.int32, vec_ref.shape, 1)
        gain_grad = jnp.sum(raw * w, axis=1, keepdims=True)
        shift_grad = jnp.sum(w * sums, axis=1, keepdims=True)
        vec_ref[...] = jnp.where(lane == 1, gain_grad, jnp.where(lane == 2, shift_grad, 0.0))


def weight_grads(which, x, dy, dproj, o, w, gain_col, shift_col):
    _, rows, width = x.shape
    half = o.shape[1]
    step = min(512, rows)
    chosen = pl.BlockSpec((1, step, width), lambda i, which: (which[0], i, 0))
    by_row = lambda cols: pl.BlockSpec((step, cols), lambda i, *_: (i, 0))
    return pl.pallas_call(
        weight_kernel,
        grid_spec=pltpu.PrefetchScalarGridSpec(
            num_scalar_prefetch=1,
            grid=(rows // step,),
            in_specs=[chosen, chosen, by_row(3 * half), by_row(half), whole(w.shape),
                      whole(gain_col.shape), whole(shift_col.shape)],
            out_specs=[whole((width, 3 * half)), whole((width, half)), whole((width, LANES)), whole((1, 3 * half))],
            scratch_shapes=[pltpu.VMEM((width, 3 * half), F32), pltpu.VMEM((width, half), F32),
                            pltpu.VMEM((1, 3 * half), F32)],
        ),
        out_shape=[
            jax.ShapeDtypeStruct((width, 3 * half), BF16),
            jax.ShapeDtypeStruct((width, half), BF16),
            jax.ShapeDtypeStruct((width, LANES), F32),
            jax.ShapeDtypeStruct((1, 3 * half), F32),
        ],
        compiler_params=params(),
        cost_estimate=pl.CostEstimate(
            flops=8 * rows * width * half, bytes_accessed=12 * rows * width, transcendentals=0
        ),
        name="weight_grads",
    )(which, x, dy, dproj, o, w, gain_col, shift_col)


def norm_back_kernel(which, x_ref, dy_ref, kept_ref, got_ref, out_ref):
    xhat, scale = normalise(x_ref[0].astype(F32))
    grad = kept_ref[...].astype(F32) + got_ref[...].astype(F32)
    centre = jnp.mean(grad, axis=-1, keepdims=True)
    along = jnp.mean(grad * xhat, axis=-1, keepdims=True)
    out_ref[...] = (dy_ref[0].astype(F32) + scale * (grad - centre - xhat * along)).astype(out_ref.dtype)


def norm_back(which, x, dy, kept, got):
    rows, width = got.shape
    step = min(512, rows)
    blocks = rows // step
    chosen = pl.BlockSpec((1, step, width), lambda i, which: (which[0], which[1] * blocks + i, 0))
    return pl.pallas_call(
        norm_back_kernel,
        grid_spec=pltpu.PrefetchScalarGridSpec(
            num_scalar_prefetch=1,
            grid=(blocks,),
            in_specs=[chosen, chosen,
                      pl.BlockSpec((step, width), lambda i, which: (which[1] * blocks + i, 0)),
                      pl.BlockSpec((step, width), lambda i, *_: (i, 0))],
            out_specs=pl.BlockSpec((step, width), lambda i, *_: (i, 0)),
        ),
        out_shape=jax.ShapeDtypeStruct((rows, width), BF16),
        compiler_params=params(),
        cost_estimate=pl.CostEstimate(
            flops=20 * rows * width, bytes_accessed=10 * rows * width, transcendentals=0
        ),
        name="norm_back",
    )(which, x, dy, kept, got)


def swap(values, axis):
    return lax.ppermute(values, axis, [(0, 1), (1, 0)])


def rotation_tables(positions):
    half = ROT // 2
    frequency = jnp.power(F32(10000.0), -2.0 * jnp.arange(half, dtype=F32) / ROT)
    angles = frequency[:, None] * positions.astype(F32)[None, :]
    cosines, sines = lax.optimization_barrier((jnp.cos(angles), jnp.sin(angles)))
    cosines, sines = cosines.T, sines.T
    rows = positions.shape[0]
    rest = jnp.zeros((rows, HD - ROT), F32)
    blank = jnp.zeros((rows, half), F32)
    per_head = (
        jnp.concatenate([cosines, cosines, rest + 1.0], axis=1),
        jnp.concatenate([-sines, blank, rest], axis=1),
        jnp.concatenate([blank, sines, rest], axis=1),
    )
    return tuple(jnp.tile(table, (1, LANES // HD)) for table in per_head)


def body(
    tokens, places, w_qkv, b_qkv, w_dense, b_dense, w_up, b_up, w_down, b_down,
    norm1_gain, norm1_bias, norm2_gain, norm2_bias, out_grad, *, seq_size, owners,
):
    _, rows, width = tokens.shape
    share = width // owners
    heads = b_qkv.shape[1]
    cols = heads * HD
    units = w_up.shape[1]
    splits = ("dp", "seq", "mh")
    side, part = lax.axis_index("mh"), lax.axis_index("ml")
    which = jnp.stack([side, part]).astype(jnp.int32)

    def column(vector):
        vector = vector.reshape(-1)
        return jnp.pad(vector, (0, share - vector.shape[0]))[:, None]

    small = jnp.concatenate(
        [column(v) for v in (b_dense, b_down, norm1_gain, norm1_bias, norm2_gain, norm2_bias, b_qkv, b_up)],
        axis=1,
    )
    small = jnp.pad(small, ((0, 0), (0, LANES - small.shape[1])))
    first = jnp.concatenate([w_qkv.transpose(1, 0, 2).reshape(share, 3 * cols), w_dense.T, small], axis=1)
    second = jnp.concatenate([w_up, w_down.T], axis=1)
    first = lax.all_gather(first, splits, axis=0, tiled=True).reshape(owners, 2, share, -1)
    second = lax.all_gather(second, splits, axis=0, tiled=True).reshape(owners, 2, share, -1)

    def laid(pack, start, count):
        piece = pack[:, :, :, start : start + count].transpose(0, 2, 1, 3)
        return piece.reshape(width, 2, count)

    qkv_w = laid(first, 0, 3 * cols).reshape(width, 2, 3, cols).transpose(0, 2, 1, 3).reshape(width, 6 * cols)
    dense_w = laid(first, 3 * cols, cols).reshape(width, 2 * cols)
    up_w = laid(second, 0, units).reshape(width, 2 * units)
    down_w = laid(second, units, units).reshape(width, 2 * units)
    small = first[:, :, :, 4 * cols :].astype(F32)
    vectors = small[:, 0].reshape(width, LANES)
    piece = HD // owners
    qkv_b = small[:, :, : 3 * heads * piece, 6].reshape(owners, 2, 3, heads, piece)
    qkv_b = qkv_b.transpose(2, 1, 3, 0, 4).reshape(1, 6 * cols)
    up_rows, up_cols = b_up.shape
    up_b = small[:, :, :, 7].reshape(owners, 2, up_rows, up_cols).transpose(1, 2, 0, 3).reshape(1, 2 * units)
    row_of = lambda index: vectors[:, index].reshape(1, width)
    column_of = lambda index: vectors[:, index].reshape(width, 1)

    my_places = lax.dynamic_index_in_dim(places, side, 0, keepdims=False)
    run_rows = rows // 2
    runs = jnp.stack([my_places[0], my_places[run_rows]]) // run_rows
    if seq_size == 2:
        all_runs = jnp.concatenate([runs, swap(runs, "seq")])
    else:
        all_runs = lax.all_gather(runs, "seq", axis=0, tiled=True)
    order = jnp.arange(2 * seq_size, dtype=jnp.int32)
    slots = jnp.sum(jnp.where(all_runs[None, :] == order[:, None], order[None, :], 0), axis=1)
    tables = rotation_tables(my_places)

    q, kv, grad_o = front(which, tokens, out_grad, qkv_w, qkv_b, dense_w, row_of(2), row_of(3), tables)
    if seq_size == 2:
        kv_all = jnp.concatenate([kv, swap(kv, "seq")], axis=0)
    else:
        kv_all = lax.all_gather(kv, "seq", axis=0, tiled=True)

    mlp_part, mlp_dx, grad_up, grad_down, mlp_vectors, grad_up_b = feed(
        which, tokens, out_grad, up_w, up_b, down_w, row_of(4), row_of(5), column_of(4), column_of(5)
    )

    def spread(grad):
        return grad.reshape(owners, share, 2, -1).transpose(0, 2, 1, 3)

    def scatter(pack):
        return lax.psum_scatter(
            pack.reshape(owners * 2 * share, -1), splits, scatter_dimension=0, tiled=True
        )

    owned_second = scatter(jnp.concatenate([spread(grad_up), spread(grad_down)], axis=3))

    attended, dq, dk, dv = attention(runs, slots, q, grad_o, kv_all)

    half_rows = rows // 2

    def half_of(array, index):
        return lax.dynamic_slice_in_dim(array, index * half_rows, half_rows, axis=0)

    def branch_sum(index):
        product = lax.dot_general(half_of(attended, index), dense_w, NT, preferred_element_type=F32)
        return product + half_of(mlp_part, index).astype(F32)

    got_mixed = swap(branch_sum(1 - part).astype(BF16), "ml")
    my_tokens = lax.dynamic_slice(tokens, (side, part * half_rows, 0), (1, half_rows, width))[0]
    mixed = branch_sum(part) + got_mixed.astype(F32) + my_tokens.astype(F32) + row_of(0) + row_of(1)
    mixed = lax.all_gather(mixed.astype(BF16), ("mh", "ml"), axis=0, tiled=True).reshape(tokens.shape)

    if seq_size == 2:
        got = swap(jnp.concatenate([dk[rows:], dv[rows:]], axis=1).astype(BF16), "seq")
        dk, dv = dk[:rows], dv[:rows]
    else:
        got = lax.psum_scatter(
            jnp.concatenate([dk, dv], axis=1).astype(BF16), "seq", scatter_dimension=0, tiled=True
        )
        dk = dv = jnp.zeros(dq.shape, F32)
    dproj, dx = back(dq, dk, dv, got, qkv_w, row_of(2), mlp_dx, tables)
    got_dx = swap(half_of(dx, 1 - part), "ml")
    input_grad = norm_back(which, tokens, out_grad, dx, got_dx)
    input_grad = lax.all_gather(input_grad, ("mh", "ml"), axis=0, tiled=True).reshape(tokens.shape)

    grad_qkv, grad_dense, qkv_vectors, grad_qkv_b = weight_grads(
        which, tokens, out_grad, dproj, attended, qkv_w, column_of(2), column_of(3)
    )

    vector_grads = (mlp_vectors + qkv_vectors)[:, :5].reshape(owners, 1, share, 5)
    vector_grads = jnp.broadcast_to(vector_grads, (owners, 2, share, 5))
    bias_qkv = grad_qkv_b.reshape(3, 2, heads, owners, piece).transpose(3, 1, 0, 2, 4)
    bias_qkv = bias_qkv.reshape(owners, 2, 3 * heads * piece)
    bias_qkv = jnp.pad(bias_qkv, ((0, 0), (0, 0), (0, share - 3 * heads * piece)))[..., None]
    bias_up = grad_up_b.reshape(2, up_rows, owners, up_cols).transpose(2, 0, 1, 3).reshape(owners, 2, share, 1)
    tail = jnp.concatenate([vector_grads, bias_qkv, bias_up], axis=3)
    tail = jnp.pad(tail, ((0, 0), (0, 0), (0, 0), (0, LANES - 7))).astype(BF16)
    grad_qkv = grad_qkv.reshape(owners, share, 3, 2, cols).transpose(0, 3, 1, 2, 4)
    grad_qkv = grad_qkv.reshape(owners, 2, share, 3 * cols)
    owned_first = scatter(jnp.concatenate([grad_qkv, spread(grad_dense), tail], axis=3)).astype(F32)
    owned_second = owned_second.astype(F32)

    vectors = owned_first[:, 4 * cols :]
    norms = vectors[:, :5]
    norms = norms + swap(norms, "ml")
    bias_grad = norms[:, 0]
    return (
        mixed,
        input_grad,
        owned_first[:, : 3 * cols].reshape(share, 3, cols).transpose(1, 0, 2),
        vectors[: 3 * heads * piece, 5].reshape(b_qkv.shape),
        owned_first[:, 3 * cols : 4 * cols].T,
        bias_grad,
        owned_second[:, :units],
        vectors[:, 6].reshape(b_up.shape),
        owned_second[:, units:].T,
        bias_grad,
        norms[:, 1],
        norms[:, 2],
        norms[:, 3],
        norms[:, 4],
    )


def solution(mesh):
    dp, seq, mp = (mesh.shape[axis] for axis in ("dp", "seq", "mp"))
    split = Mesh(mesh.devices.reshape(dp, seq, 2, mp // 2), ("dp", "seq", "mh", "ml"))
    mp, owner = ("mh", "ml"), ("dp", "seq")
    row = P("dp", "seq", None)
    vector = P(owner)
    weights = (
        P(None, owner, mp), P(None, mp, owner), P(mp, owner), vector, P(owner, mp), P(mp, owner),
        P(mp, owner), vector, vector, vector, vector, vector,
    )
    return jax.shard_map(
        functools.partial(body, seq_size=seq, owners=dp * seq),
        mesh=split,
        in_specs=(row, P("dp", "seq")) + weights + (row,),
        out_specs=(row, row) + weights,
        check_vma=False,
    )
```

```python
import functools

import jax
import jax.numpy as jnp
from jax import lax
from jax.experimental import pallas as pl
from jax.experimental.pallas import tpu as pltpu
from jax.sharding import Mesh
from jax.sharding import PartitionSpec as P

HD = 64
ROT = 16
LANES = 128
F32 = jnp.float32
BF16 = jnp.bfloat16
LOG2E = 1.4426950408889634
norm_eps = 1e-05
masked_value = -1e30
vmem_bytes = 60 * 2**20

NN = (((1,), (0,)), ((), ()))
NT = (((1,), (1,)), ((), ()))
TN = (((0,), (0,)), ((), ()))


def dot(left, right, dims):
    return lax.dot_general(left, right, dims, preferred_element_type=F32)


def normalise(rows):
    centre = jnp.mean(rows, axis=-1, keepdims=True)
    deviate = rows - centre
    spread = jnp.mean(deviate * deviate, axis=-1, keepdims=True)
    scale = lax.rsqrt(spread + norm_eps)
    return deviate * scale, scale


def turn(chunk, cosines, sine_low, sine_high):
    half = ROT // 2
    return (
        chunk * cosines
        + pltpu.roll(chunk, LANES - half, 1) * sine_low
        + pltpu.roll(chunk, half, 1) * sine_high
    )


def whole(shape):
    return pl.BlockSpec(shape, lambda *_: (0,) * len(shape))


def params(**kwargs):
    return pltpu.CompilerParams(vmem_limit_bytes=vmem_bytes, **kwargs)


def place_first_kernel(where, one_ref, two_ref, qkv_ref, dense_ref, small_ref):
    cols = one_ref.shape[-1] // 2
    near = where[0] == 0
    one = [one_ref[0, j] for j in range(2)]
    two = [two_ref[0, j] for j in range(2)]
    one = (jnp.where(near, one[0], one[1]), jnp.where(near, one[1], one[0]))
    two = (jnp.where(near, two[0], two[1]), jnp.where(near, two[1], two[0]))
    pieces = [one[j][:, i * cols : (i + 1) * cols] for i in range(2) for j in range(2)]
    pieces += [two[j][:, :cols] for j in range(2)]
    qkv_ref[...] = jnp.concatenate(pieces, axis=1)
    dense_ref[...] = jnp.concatenate([two[j][:, cols : 2 * cols] for j in range(2)], axis=1)
    small_ref[...] = jnp.concatenate([two[j][:, 2 * cols :] for j in range(2)], axis=1).astype(F32)


def place_second_kernel(where, one_ref, two_ref, up_ref, down_ref):
    near = where[0] == 0
    for ref, out in ((one_ref, up_ref), (two_ref, down_ref)):
        units = ref.shape[-1]
        out[:, :units] = jnp.where(near, ref[0, 0], ref[0, 1])
        out[:, units:] = jnp.where(near, ref[0, 1], ref[0, 0])


def place(kernel, where, one, two, widths, types):
    owners, _, share, _ = one.shape

    def spec(array, low, high):
        def index(i, where):
            bits = i ^ where[1]
            upper, lower, across = bits // 4, (bits // 2) % 2, bits % 2
            near, far = (across, upper) if low == "seq" else (upper, across)
            return (lower * 4 + far * 2 + near, 0, 0, 0)

        return pl.BlockSpec((1,) + array.shape[1:], index)

    return pl.pallas_call(
        kernel,
        grid_spec=pltpu.PrefetchScalarGridSpec(
            num_scalar_prefetch=1,
            grid=(owners,),
            in_specs=[spec(one, "seq", "dp"), spec(two, "dp", "seq")],
            out_specs=[pl.BlockSpec((share, width), lambda i, *_: (i, 0)) for width in widths],
        ),
        out_shape=[jax.ShapeDtypeStruct((owners * share, width), kind) for width, kind in zip(widths, types)],
        compiler_params=params(),
        cost_estimate=pl.CostEstimate(flops=0, bytes_accessed=8 * one.size, transcendentals=0),
        name="place",
    )(where, one, two)


def front_kernel(
    which, x_ref, dy_ref, w_ref, wb_ref, dense_ref, gain_ref, shift_ref, cos_ref, low_ref, high_ref,
    q_ref, kv_ref, do_ref,
):
    half = q_ref.shape[1]
    xhat, _ = normalise(x_ref[0].astype(F32))
    normed = (xhat * gain_ref[...] + shift_ref[...]).astype(BF16)
    proj = dot(normed, w_ref[...], NN) + wb_ref[...]
    cosines, low, high = cos_ref[...], low_ref[...], high_ref[...]
    for j in range(half // LANES):
        at = slice(j * LANES, (j + 1) * LANES)
        query = turn(proj[:, at], cosines, low, high).astype(BF16)
        q_ref[:, at] = query * BF16(HD**-0.5)
        key = proj[:, half + j * LANES : half + (j + 1) * LANES]
        kv_ref[:, at] = turn(key, cosines, low, high).astype(BF16)
    kv_ref[:, half:] = proj[:, 2 * half :].astype(BF16)
    do_ref[...] = dot(dy_ref[0], dense_ref[...], NN).astype(BF16)


def front(which, x, dy, w, wb, dense, gain, shift, tables):
    _, rows, width = x.shape
    half = dense.shape[1]
    step = min(512, rows)
    chosen = pl.BlockSpec((1, step, width), lambda i, which: (which[0], i, 0))
    by_row = lambda cols: pl.BlockSpec((step, cols), lambda i, *_: (i, 0))
    return pl.pallas_call(
        front_kernel,
        grid_spec=pltpu.PrefetchScalarGridSpec(
            num_scalar_prefetch=1,
            grid=(rows // step,),
            in_specs=[chosen, chosen, whole(w.shape), whole(wb.shape), whole(dense.shape),
                      whole(gain.shape), whole(shift.shape)] + [by_row(LANES)] * 3,
            out_specs=[by_row(half), by_row(2 * half), by_row(half)],
        ),
        out_shape=[
            jax.ShapeDtypeStruct((rows, half), BF16),
            jax.ShapeDtypeStruct((rows, 2 * half), BF16),
            jax.ShapeDtypeStruct((rows, half), BF16),
        ],
        compiler_params=params(),
        cost_estimate=pl.CostEstimate(
            flops=2 * rows * width * 4 * half, bytes_accessed=12 * rows * width, transcendentals=0
        ),
        name="front",
    )(which, x, dy, w, wb, dense, gain, shift, *tables)


def feed_kernel(
    which, x_ref, dy_ref, up_ref, upb_ref, down_ref, gain_ref, shift_ref, gain_col, shift_col,
    part_ref, dx_ref, gup_ref, gdown_ref, vec_ref, gupb_ref,
    up_acc, down_acc, sum_acc, dy_acc,
):
    step = pl.program_id(0)

    @pl.when(step == 0)
    def _():
        up_acc[...] = jnp.zeros_like(up_acc)
        down_acc[...] = jnp.zeros_like(down_acc)
        sum_acc[...] = jnp.zeros_like(sum_acc)
        dy_acc[...] = jnp.zeros_like(dy_acc)

    xhat, _ = normalise(x_ref[0].astype(F32))
    dy = dy_ref[0]
    normed = (xhat * gain_ref[...] + shift_ref[...]).astype(BF16)
    hidden = dot(normed, up_ref[...], NN) + upb_ref[...]
    share = 0.5 * (1.0 + lax.erf(hidden * F32(0.5**0.5)))
    act = (hidden * share).astype(BF16)
    slope = share + hidden * (jnp.exp(hidden * hidden * -0.5) * F32(0.3989422804014327))
    part_ref[...] = dot(act, down_ref[...], NT).astype(part_ref.dtype)
    grad = dot(dy, down_ref[...], NN) * slope
    grad_low = grad.astype(BF16)
    dx_ref[...] = (dot(grad_low, up_ref[...], NT) * gain_ref[...]).astype(dx_ref.dtype)
    up_acc[...] += dot(xhat.astype(BF16), grad_low, TN)
    down_acc[...] += dot(dy, act, TN)
    sum_acc[...] += jnp.sum(grad_low.astype(F32), axis=0, keepdims=True)
    dy_acc[...] += jnp.sum(dy.astype(F32), axis=0, keepdims=True)

    @pl.when(step == pl.num_programs(0) - 1)
    def _():
        sums = sum_acc[...]
        raw = up_acc[...]
        up = up_ref[...].astype(F32)
        gup_ref[...] = (raw * gain_col[...] + shift_col[...] * sums).astype(gup_ref.dtype)
        gdown_ref[...] = down_acc[...].astype(gdown_ref.dtype)
        gupb_ref[...] = sums
        lane = lax.broadcasted_iota(jnp.int32, vec_ref.shape, 1)
        gain_grad = jnp.sum(raw * up, axis=1, keepdims=True)
        shift_grad = jnp.sum(up * sums, axis=1, keepdims=True)
        dy_col = jnp.transpose(jnp.broadcast_to(dy_acc[...], (LANES, dy_acc.shape[1])))
        vec_ref[...] = jnp.where(
            lane == 0, dy_col * 0.5,
            jnp.where(lane == 3, gain_grad, jnp.where(lane == 4, shift_grad, 0.0)),
        )


def feed(which, x, dy, up, upb, down, gain, shift, gain_col, shift_col):
    _, rows, width = x.shape
    units = up.shape[1]
    step = min(256, rows)
    chosen = pl.BlockSpec((1, step, width), lambda i, which: (which[0], i, 0))
    by_row = pl.BlockSpec((step, width), lambda i, *_: (i, 0))
    return pl.pallas_call(
        feed_kernel,
        grid_spec=pltpu.PrefetchScalarGridSpec(
            num_scalar_prefetch=1,
            grid=(rows // step,),
            in_specs=[chosen, chosen, whole(up.shape), whole(upb.shape), whole(down.shape),
                      whole(gain.shape), whole(shift.shape), whole(gain_col.shape), whole(shift_col.shape)],
            out_specs=[by_row, by_row, whole((width, units)), whole((width, units)),
                       whole((width, LANES)), whole((1, units))],
            scratch_shapes=[pltpu.VMEM((width, units), F32), pltpu.VMEM((width, units), F32),
                            pltpu.VMEM((1, units), F32), pltpu.VMEM((1, width), F32)],
        ),
        out_shape=[
            jax.ShapeDtypeStruct((rows, width), BF16),
            jax.ShapeDtypeStruct((rows, width), BF16),
            jax.ShapeDtypeStruct((width, units), BF16),
            jax.ShapeDtypeStruct((width, units), BF16),
            jax.ShapeDtypeStruct((width, LANES), F32),
            jax.ShapeDtypeStruct((1, units), F32),
        ],
        compiler_params=params(),
        cost_estimate=pl.CostEstimate(
            flops=12 * rows * width * units, bytes_accessed=24 * width * units, transcendentals=2 * rows * units
        ),
        name="feed",
    )(which, x, dy, up, upb, down, gain, shift, gain_col, shift_col)


def lane_fold(values, combine):
    total = values[:, :LANES]
    for j in range(1, values.shape[1] // LANES):
        total = combine(total, values[:, j * LANES : (j + 1) * LANES])
    return total


def attention_kernel(runs, slots, q_ref, g_ref, *refs, block, per_run, parts, first, carried):
    k_parts, v_parts, refs = refs[:parts], refs[parts : 2 * parts], refs[2 * parts :]
    if carried:
        dk_in, dv_in, refs = refs[0], refs[1], refs[2:]
    o_ref, dq_ref, dk_ref, dv_ref, k_ref, v_ref, score_ref, soft_ref, acc_ref = refs
    step = pl.program_id(1)

    @pl.when(step == 0)
    def _():
        for j in range(parts):
            there = pl.ds(j * k_parts[j].shape[0], k_parts[j].shape[0])
            k_ref[there, :] = k_parts[j][...]
            v_ref[there, :] = v_parts[j][...]
        dk_ref[...] = dk_in[...] if carried else jnp.zeros_like(dk_ref)
        dv_ref[...] = dv_in[...] if carried else jnp.zeros_like(dv_ref)

    step = step + first
    full = runs[step // per_run] * per_run + step % per_run
    lane = lax.broadcasted_iota(jnp.int32, (block, LANES), 1)
    heads = (lane < HD, lane >= HD)
    both_q, both_g = q_ref[...], g_ref[...]
    queries = [jnp.where(mine, both_q, jnp.zeros_like(both_q)) for mine in heads]
    grads = [jnp.where(mine, both_g, jnp.zeros_like(both_g)) for mine in heads]

    def rows_of(at):
        start = (slots[at // per_run] * per_run + at % per_run) * block
        return pl.ds(pl.multiple_of(start, block), block)

    def score(at, tops, masked):
        keys = k_ref[rows_of(at), :]
        out = []
        for h in range(2):
            scores = dot(queries[h], keys, NT)
            if masked:
                row = lax.broadcasted_iota(jnp.int32, (block, block), 0)
                col = lax.broadcasted_iota(jnp.int32, (block, block), 1)
                scores = jnp.where(col <= row, scores, masked_value)
            score_ref[h, at] = scores
            out.append(jnp.maximum(tops[h], lane_fold(scores, jnp.maximum)))
        return tuple(out)

    least = jnp.full((block, LANES), masked_value, F32)
    tops = lax.fori_loop(0, full, lambda at, carry: score(at, carry, False), (least, least))
    tops = score(full, tops, True)
    tops = [jnp.max(top, axis=1, keepdims=True) * F32(LOG2E) for top in tops]

    acc_ref[...] = jnp.zeros_like(acc_ref)

    def weigh(at, totals):
        values = v_ref[rows_of(at), :]
        out = []
        for h in range(2):
            soft = jnp.exp2(score_ref[h, at] * F32(LOG2E) - tops[h])
            out.append(totals[h] + lane_fold(soft, jnp.add))
            soft_low = soft.astype(BF16)
            soft_ref[h, at] = soft_low
            acc_ref[h] += dot(soft_low, values, NN)
        return tuple(out)

    nought = jnp.zeros((block, LANES), F32)
    totals = lax.fori_loop(0, full + 1, weigh, (nought, nought))
    shares = [1.0 / jnp.sum(total, axis=1, keepdims=True) for total in totals]
    attended = jnp.where(heads[0], acc_ref[0] * shares[0], acc_ref[1] * shares[1])
    o_ref[...] = attended.astype(o_ref.dtype)
    product = attended * both_g.astype(F32)
    row_terms = [
        jnp.sum(jnp.where(heads[h], product, 0.0), axis=1, keepdims=True) * shares[h] for h in range(2)
    ]
    scaled = [(grads[h].astype(F32) * shares[h]).astype(BF16) for h in range(2)]

    acc_ref[...] = jnp.zeros_like(acc_ref)

    def back(at, carry):
        there = rows_of(at)
        keys, values = k_ref[there, :], v_ref[there, :]
        key_terms, value_terms = [], []
        for h in range(2):
            soft_low = soft_ref[h, at]
            grad_soft = dot(scaled[h], values, NT)
            grad_score = (soft_low.astype(F32) * (grad_soft - row_terms[h])).astype(BF16)
            acc_ref[h] += dot(grad_score, keys, NN)
            key_terms.append(dot(grad_score, queries[h], TN))
            value_terms.append(dot(soft_low, scaled[h], TN))
        dk_ref[there, :] += key_terms[0] + key_terms[1]
        dv_ref[there, :] += value_terms[0] + value_terms[1]
        return carry

    lax.fori_loop(0, full + 1, back, 0)
    dq_ref[...] = (jnp.where(heads[0], acc_ref[0], acc_ref[1]) * F32(HD**-0.5)).astype(dq_ref.dtype)


def attention(runs, slots, q, g, kv_parts, first=0, last=None, carry=None, pair=None):
    rows, width = q.shape
    keys = sum(kv.shape[0] for kv in kv_parts)
    run_rows = rows // 2
    block = min(512, run_rows)
    per_run = run_rows // block
    first, last = (0, rows // block) if last is None else (first * per_run, last * per_run)
    pairs = width // LANES
    count, base = (pairs, 0) if pair is None else (1, pair)
    done = (last - first) * block
    by_query = pl.BlockSpec((block, LANES), lambda p, i, *_: (first + i, base + p))
    by_key = [pl.BlockSpec((kv.shape[0], LANES), lambda p, i, *_: (0, base + p)) for kv in kv_parts]
    by_value = [pl.BlockSpec((kv.shape[0], LANES), lambda p, i, *_: (0, pairs + base + p)) for kv in kv_parts]
    of_query = pl.BlockSpec((block, LANES), lambda p, i, *_: (i, p))
    of_key = pl.BlockSpec((keys, LANES), lambda p, i, *_: (0, p))
    from_key = pl.BlockSpec((keys, LANES), lambda p, i, *_: (0, base + p))
    carry = () if carry is None else tuple(carry)
    kernel = functools.partial(
        attention_kernel, block=block, per_run=per_run, parts=len(kv_parts), first=first, carried=bool(carry)
    )
    return pl.pallas_call(
        kernel,
        grid_spec=pltpu.PrefetchScalarGridSpec(
            num_scalar_prefetch=2,
            grid=(count, last - first),
            in_specs=[by_query, by_query, *by_key, *by_value] + [from_key] * len(carry),
            out_specs=[of_query, of_query, of_key, of_key],
            scratch_shapes=[
                pltpu.VMEM((keys, LANES), BF16),
                pltpu.VMEM((keys, LANES), BF16),
                pltpu.VMEM((2, keys // block, block, block), F32),
                pltpu.VMEM((2, keys // block, block, block), BF16),
                pltpu.VMEM((2, block, LANES), F32),
            ],
        ),
        out_shape=[
            jax.ShapeDtypeStruct((done, count * LANES), BF16),
            jax.ShapeDtypeStruct((done, count * LANES), BF16),
            jax.ShapeDtypeStruct((keys, count * LANES), F32),
            jax.ShapeDtypeStruct((keys, count * LANES), F32),
        ],
        compiler_params=params(),
        cost_estimate=pl.CostEstimate(
            flops=40 * done * keys * count * LANES, bytes_accessed=24 * keys * width,
            transcendentals=done * keys * count,
        ),
        name="attention",
    )(runs, slots, q, g, *kv_parts, *kv_parts, *carry)


def back_kernel(
    dq_ref, own_k, own_v, got_ref, w_ref, gain_ref, dx_in, cos_ref, low_ref, high_ref, dproj_ref, dx_ref
):
    half = dq_ref.shape[1]
    cosines, low, high = cos_ref[...], low_ref[...], high_ref[...]
    for j in range(half // LANES):
        at = slice(j * LANES, (j + 1) * LANES)
        query = dq_ref[:, at].astype(F32)
        dproj_ref[:, at] = turn(query, cosines, -low, -high).astype(BF16)
        key = own_k[:, at] + got_ref[:, at].astype(F32)
        dproj_ref[:, half + j * LANES : half + (j + 1) * LANES] = turn(key, cosines, -low, -high).astype(BF16)
    dproj_ref[:, 2 * half :] = (own_v[...] + got_ref[:, half:].astype(F32)).astype(BF16)
    summed = dot(dproj_ref[...], w_ref[...], NT) * gain_ref[...] + dx_in[...].astype(F32)
    dx_ref[...] = summed.astype(dx_ref.dtype)


def back(dq, dk, dv, got, w, gain, dx_part, tables):
    rows, half = dq.shape
    width = w.shape[0]
    step = min(512, rows)
    by_row = lambda cols: pl.BlockSpec((step, cols), lambda i: (i, 0))
    return pl.pallas_call(
        back_kernel,
        grid=(rows // step,),
        in_specs=[by_row(half), by_row(half), by_row(half), by_row(2 * half), whole(w.shape),
                  whole(gain.shape), by_row(width)] + [by_row(LANES)] * 3,
        out_specs=[by_row(3 * half), by_row(width)],
        out_shape=[
            jax.ShapeDtypeStruct((rows, 3 * half), BF16),
            jax.ShapeDtypeStruct((rows, width), BF16),
        ],
        compiler_params=params(),
        cost_estimate=pl.CostEstimate(
            flops=6 * rows * width * half, bytes_accessed=12 * rows * width, transcendentals=0
        ),
        name="back",
    )(dq, dk, dv, got, w, gain, dx_part, *tables)


def weight_kernel(
    which, x_ref, dy_ref, dproj_ref, o_ref, w_ref, gain_col, shift_col,
    gqkv_ref, gdense_ref, vec_ref, gb_ref, acc, dense_acc, sum_acc,
):
    step = pl.program_id(0)

    @pl.when(step == 0)
    def _():
        acc[...] = jnp.zeros_like(acc)
        dense_acc[...] = jnp.zeros_like(dense_acc)
        sum_acc[...] = jnp.zeros_like(sum_acc)

    xhat, _ = normalise(x_ref[0].astype(F32))
    dproj = dproj_ref[...]
    acc[...] += dot(xhat.astype(BF16), dproj, TN)
    dense_acc[...] += dot(dy_ref[0], o_ref[...], TN)
    sum_acc[...] += jnp.sum(dproj.astype(F32), axis=0, keepdims=True)

    @pl.when(step == pl.num_programs(0) - 1)
    def _():
        sums, raw, w = sum_acc[...], acc[...], w_ref[...].astype(F32)
        gqkv_ref[...] = (raw * gain_col[...] + shift_col[...] * sums).astype(gqkv_ref.dtype)
        gdense_ref[...] = dense_acc[...].astype(gdense_ref.dtype)
        gb_ref[...] = sums
        lane = lax.broadcasted_iota(jnp.int32, vec_ref.shape, 1)
        gain_grad = jnp.sum(raw * w, axis=1, keepdims=True)
        shift_grad = jnp.sum(w * sums, axis=1, keepdims=True)
        vec_ref[...] = jnp.where(lane == 1, gain_grad, jnp.where(lane == 2, shift_grad, 0.0))


def weight_grads(which, x, dy, dproj, o, w, gain_col, shift_col):
    _, rows, width = x.shape
    half = o.shape[1]
    step = min(512, rows)
    chosen = pl.BlockSpec((1, step, width), lambda i, which: (which[0], i, 0))
    by_row = lambda cols: pl.BlockSpec((step, cols), lambda i, *_: (i, 0))
    return pl.pallas_call(
        weight_kernel,
        grid_spec=pltpu.PrefetchScalarGridSpec(
            num_scalar_prefetch=1,
            grid=(rows // step,),
            in_specs=[chosen, chosen, by_row(3 * half), by_row(half), whole(w.shape),
                      whole(gain_col.shape), whole(shift_col.shape)],
            out_specs=[whole((width, 3 * half)), whole((width, half)), whole((width, LANES)), whole((1, 3 * half))],
            scratch_shapes=[pltpu.VMEM((width, 3 * half), F32), pltpu.VMEM((width, half), F32),
                            pltpu.VMEM((1, 3 * half), F32)],
        ),
        out_shape=[
            jax.ShapeDtypeStruct((width, 3 * half), BF16),
            jax.ShapeDtypeStruct((width, half), BF16),
            jax.ShapeDtypeStruct((width, LANES), F32),
            jax.ShapeDtypeStruct((1, 3 * half), F32),
        ],
        compiler_params=params(),
        cost_estimate=pl.CostEstimate(
            flops=8 * rows * width * half, bytes_accessed=12 * rows * width, transcendentals=0
        ),
        name="weight_grads",
    )(which, x, dy, dproj, o, w, gain_col, shift_col)


def norm_back_kernel(which, x_ref, dy_ref, kept_ref, got_ref, out_ref):
    xhat, scale = normalise(x_ref[0].astype(F32))
    grad = kept_ref[...].astype(F32) + got_ref[...].astype(F32)
    centre = jnp.mean(grad, axis=-1, keepdims=True)
    along = jnp.mean(grad * xhat, axis=-1, keepdims=True)
    out_ref[...] = (dy_ref[0].astype(F32) + scale * (grad - centre - xhat * along)).astype(out_ref.dtype)


def norm_back(which, x, dy, kept, got):
    rows, width = got.shape
    step = min(512, rows)
    blocks = rows // step
    chosen = pl.BlockSpec((1, step, width), lambda i, which: (which[0], which[1] * blocks + i, 0))
    return pl.pallas_call(
        norm_back_kernel,
        grid_spec=pltpu.PrefetchScalarGridSpec(
            num_scalar_prefetch=1,
            grid=(blocks,),
            in_specs=[chosen, chosen,
                      pl.BlockSpec((step, width), lambda i, which: (which[1] * blocks + i, 0)),
                      pl.BlockSpec((step, width), lambda i, *_: (i, 0))],
            out_specs=pl.BlockSpec((step, width), lambda i, *_: (i, 0)),
        ),
        out_shape=jax.ShapeDtypeStruct((rows, width), BF16),
        compiler_params=params(),
        cost_estimate=pl.CostEstimate(
            flops=20 * rows * width, bytes_accessed=10 * rows * width, transcendentals=0
        ),
        name="norm_back",
    )(which, x, dy, kept, got)


def swap(values, axis):
    return lax.ppermute(values, axis, [(0, 1), (1, 0)])


def across(values, bit):
    return lax.ppermute(values, "dp", [(i, i ^ bit) for i in range(4)])


def gather_half(values, seq_first):
    values = jnp.concatenate([values[None], swap(values, "mh")[None]], axis=0)
    steps = [lambda v: swap(v, "seq"), lambda v: across(v, 2)]
    for step in steps if seq_first else steps[::-1]:
        values = jnp.concatenate([values, step(values)], axis=0)
    values = jnp.concatenate([values, across(values, 1)], axis=0)
    return values.reshape(8, 2, *values.shape[1:])


def line_gather(mine, index):
    axes, count = ("mh", "ml"), 4
    up = [(i, i + 1) for i in range(count - 1)]
    down = [(i + 1, i) for i in range(count - 1)]
    from_below, from_above = [mine], [mine]
    for _ in range(count - 1):
        from_below.append(lax.ppermute(from_below[-1], axes, up))
        from_above.append(lax.ppermute(from_above[-1], axes, down))
    out = jnp.zeros((count,) + mine.shape, mine.dtype)
    out = lax.dynamic_update_index_in_dim(out, mine, index, 0)
    for back in (2, 1, 3):
        piece = jnp.where(index >= back, from_below[back], from_above[count - back])
        out = lax.dynamic_update_index_in_dim(out, piece, (index - back) % count, 0)
    return out


def rotation_tables(positions):
    half = ROT // 2
    frequency = jnp.power(F32(10000.0), -2.0 * jnp.arange(half, dtype=F32) / ROT)
    angles = frequency[:, None] * positions.astype(F32)[None, :]
    cosines, sines = lax.optimization_barrier((jnp.cos(angles), jnp.sin(angles)))
    cosines, sines = cosines.T, sines.T
    rows = positions.shape[0]
    rest = jnp.zeros((rows, HD - ROT), F32)
    blank = jnp.zeros((rows, half), F32)
    per_head = (
        jnp.concatenate([cosines, cosines, rest + 1.0], axis=1),
        jnp.concatenate([-sines, blank, rest], axis=1),
        jnp.concatenate([blank, sines, rest], axis=1),
    )
    return tuple(jnp.tile(table, (1, LANES // HD)) for table in per_head)


def body(
    tokens, places, w_qkv, b_qkv, w_dense, b_dense, w_up, b_up, w_down, b_down,
    norm1_gain, norm1_bias, norm2_gain, norm2_bias, out_grad, *, seq_size, owners,
):
    _, rows, width = tokens.shape
    share = width // owners
    heads = b_qkv.shape[1]
    cols = heads * HD
    units = w_up.shape[1]
    side, part = lax.axis_index("mh"), lax.axis_index("ml")
    index = 2 * side + part
    owner = lax.axis_index("dp") * seq_size + lax.axis_index("seq")
    which = jnp.stack([side, part]).astype(jnp.int32)
    where = jnp.stack([side, owner]).astype(jnp.int32)

    def column(vector):
        vector = vector.reshape(-1)
        return jnp.pad(vector, (0, share - vector.shape[0]))[:, None]

    small = jnp.concatenate(
        [column(v) for v in (b_dense, b_down, norm1_gain, norm1_bias, norm2_gain, norm2_bias, b_qkv, b_up)],
        axis=1,
    )
    small = jnp.pad(small, ((0, 0), (0, LANES - small.shape[1])))
    one = w_qkv[:2].transpose(1, 0, 2).reshape(share, 2 * cols)
    two = jnp.concatenate([w_qkv[2], w_dense.T, small], axis=1)
    three, four = w_up, w_down.T
    first_widths, second_widths = (6 * cols, 2 * cols, 2 * LANES), (2 * units, 2 * units)
    if owners == 8 and seq_size == 2:
        one, two = gather_half(one, True), gather_half(two, False)
        qkv_w, dense_w, small = place(place_first_kernel, where, one, two, first_widths, (BF16, BF16, F32))
        three, four = lax.optimization_barrier((three, four, one, two))[:2]
        three, four = gather_half(three, True), gather_half(four, False)
        up_w, down_w = place(place_second_kernel, where, three, four, second_widths, (BF16, BF16))
    else:

        def gather(values):
            values = lax.all_gather(values, ("dp", "seq", "mh"), axis=0, tiled=True)
            return values.reshape(owners, 2, share, -1).transpose(0, 2, 1, 3).reshape(width, 2, -1)

        one, two, three, four = gather(one), gather(two), gather(three), gather(four)
        qkv_w = jnp.concatenate([one[:, :, :cols], one[:, :, cols:], two[:, :, :cols]], axis=1)
        qkv_w, dense_w = qkv_w.reshape(width, 6 * cols), two[:, :, cols : 2 * cols].reshape(width, 2 * cols)
        small = two[:, :, 2 * cols :].reshape(width, 2 * LANES).astype(F32)
        up_w, down_w = three.reshape(width, 2 * units), four.reshape(width, 2 * units)
    vectors = small[:, :8]
    piece = HD // owners
    biases = small.reshape(owners, share, 2, LANES)
    qkv_b = biases[:, : 3 * heads * piece, :, 6].reshape(owners, 3, heads, piece, 2)
    qkv_b = qkv_b.transpose(1, 4, 2, 0, 3).reshape(1, 6 * cols)
    up_rows, up_cols = b_up.shape
    up_b = biases[..., 7].reshape(owners, up_rows, up_cols, 2).transpose(3, 1, 0, 2).reshape(1, 2 * units)
    by_row = vectors.T
    row_of = lambda at: by_row[at].reshape(1, width)
    column_of = lambda at: vectors[:, at].reshape(width, 1)

    my_places = lax.dynamic_index_in_dim(places, side, 0, keepdims=False)
    run_rows = rows // 2
    runs = jnp.stack([my_places[0], my_places[run_rows]]) // run_rows
    if seq_size == 2:
        all_runs = jnp.concatenate([runs, swap(runs, "seq")])
    else:
        all_runs = lax.all_gather(runs, "seq", axis=0, tiled=True)
    order = jnp.arange(2 * seq_size, dtype=jnp.int32)
    slots = jnp.sum(jnp.where(all_runs[None, :] == order[:, None], order[None, :], 0), axis=1)
    tables = rotation_tables(my_places)

    q, kv, grad_o = front(which, tokens, out_grad, qkv_w, qkv_b, dense_w, row_of(2), row_of(3), tables)
    if seq_size == 2:
        kv_parts = (kv, swap(kv, "seq"))
    else:
        kv_parts = (lax.all_gather(kv, "seq", axis=0, tiled=True),)

    mlp_part, mlp_dx, grad_up, grad_down, mlp_vectors, grad_up_b = feed(
        which, tokens, out_grad, up_w, up_b, down_w, row_of(4), row_of(5), column_of(4), column_of(5)
    )
    q, mlp_part = lax.optimization_barrier((q, mlp_part))

    quarter = rows // 4

    def mixed_of(run, attended):
        def branch_sum(at):
            there = lax.dynamic_slice_in_dim(attended, at * quarter, quarter, axis=0)
            other = lax.dynamic_slice_in_dim(mlp_part, run * run_rows + at * quarter, quarter, axis=0)
            return lax.dot_general(there, dense_w, NT, preferred_element_type=F32) + other.astype(F32)

        got = swap(branch_sum(1 - part).astype(BF16), "ml")
        mine = lax.dynamic_slice(tokens, (side, run * run_rows + part * quarter, 0), (1, quarter, width))[0]
        return (branch_sum(part) + got.astype(F32) + mine.astype(F32) + row_of(0) + row_of(1)).astype(BF16)

    o_early, dq_early, dk, dv = attention(runs, slots, q, grad_o, kv_parts, 0, 1)
    mixed_early = lax.all_gather(mixed_of(0, o_early), ("mh", "ml"), axis=0, tiled=True)
    o_late, dq_late, dk, dv = attention(runs, slots, q, grad_o, kv_parts, 1, 2, (dk, dv))
    mixed_late = line_gather(mixed_of(1, o_late), index)
    mixed = jnp.concatenate(
        [mixed_early.reshape(2, run_rows, width), mixed_late.reshape(2, run_rows, width)], axis=1
    )

    if seq_size == 2:
        got = swap(jnp.concatenate([dk[rows:], dv[rows:]], axis=1).astype(BF16), "seq")
    else:
        got = lax.psum_scatter(
            jnp.concatenate([dk, dv], axis=1).astype(BF16), "seq", scatter_dimension=0, tiled=True
        )
        dk = dv = jnp.zeros(q.shape, F32)
    dq = jnp.concatenate([dq_early, dq_late], axis=0)
    dproj, dx = back(dq, dk, dv, got, qkv_w, row_of(2), mlp_dx, tables)
    half_rows = rows // 2
    got_dx = swap(lax.dynamic_slice_in_dim(dx, (1 - part) * half_rows, half_rows, axis=0), "ml")
    input_grad = line_gather(norm_back(which, tokens, out_grad, dx, got_dx), index).reshape(tokens.shape)

    attended = jnp.concatenate([o_early, o_late], axis=0)
    grad_qkv, grad_dense, qkv_vectors, grad_qkv_b = weight_grads(
        which, tokens, out_grad, dproj, attended, qkv_w, column_of(2), column_of(3)
    )

    def scatter(grads):
        return lax.psum_scatter(grads, ("dp", "seq"), scatter_dimension=0, tiled=True)

    def settle(sums):
        sums = sums.astype(F32)
        mine = lax.dynamic_index_in_dim(sums, side, 1, keepdims=False)
        other = lax.dynamic_index_in_dim(sums, 1 - side, 1, keepdims=False)
        return mine + swap(other.astype(BF16), "mh").astype(F32)

    owned_up = settle(scatter(grad_up).reshape(share, 2, units))
    owned_down = settle(scatter(grad_down).reshape(share, 2, units))
    vector_grads = (mlp_vectors + qkv_vectors)[:, None, :5]
    vector_grads = jnp.broadcast_to(vector_grads, (width, 2, 5))
    bias_qkv = grad_qkv_b.reshape(3, 2, heads, owners, piece).transpose(3, 0, 2, 4, 1)
    bias_qkv = bias_qkv.reshape(owners, 3 * heads * piece, 2)
    bias_qkv = jnp.pad(bias_qkv, ((0, 0), (0, share - 3 * heads * piece), (0, 0))).reshape(width, 2, 1)
    bias_up = grad_up_b.reshape(2, up_rows, owners, up_cols).transpose(2, 1, 3, 0).reshape(width, 2, 1)
    tail = jnp.concatenate([vector_grads, bias_qkv, bias_up], axis=2)
    tail = jnp.pad(tail, ((0, 0), (0, 0), (0, LANES // 2 - 7))).astype(BF16).reshape(width, LANES)
    first = scatter(jnp.concatenate([grad_qkv, grad_dense, tail], axis=1))
    owned_qkv = first[:, : 6 * cols].reshape(share, 3, 2, cols).transpose(0, 2, 1, 3).reshape(share, 2, 3 * cols)
    owned_dense = first[:, 6 * cols : 8 * cols].reshape(share, 2, cols)
    owned_tail = first[:, 8 * cols :].reshape(share, 2, LANES // 2)
    owned = settle(jnp.concatenate([owned_qkv, owned_dense, owned_tail], axis=2))
    vectors = owned[:, 4 * cols :]
    norms = vectors[:, :5]
    norms = norms + swap(norms, "ml")
    bias_grad = norms[:, 0]
    return (
        mixed,
        input_grad,
        owned[:, : 3 * cols].reshape(share, 3, cols).transpose(1, 0, 2),
        vectors[: 3 * heads * piece, 5].reshape(b_qkv.shape),
        owned[:, 3 * cols : 4 * cols].T,
        bias_grad,
        owned_up,
        vectors[:, 6].reshape(b_up.shape),
        owned_down.T,
        bias_grad,
        norms[:, 1],
        norms[:, 2],
        norms[:, 3],
        norms[:, 4],
    )


def solution(mesh):
    dp, seq, mp = (mesh.shape[axis] for axis in ("dp", "seq", "mp"))
    split = Mesh(mesh.devices.reshape(dp, seq, 2, mp // 2), ("dp", "seq", "mh", "ml"))
    mp, owner = ("mh", "ml"), ("dp", "seq")
    row = P("dp", "seq", None)
    vector = P(owner)
    weights = (
        P(None, owner, mp), P(None, mp, owner), P(mp, owner), vector, P(owner, mp), P(mp, owner),
        P(mp, owner), vector, vector, vector, vector, vector,
    )
    return jax.shard_map(
        functools.partial(body, seq_size=seq, owners=dp * seq),
        mesh=split,
        in_specs=(row, P("dp", "seq")) + weights + (row,),
        out_specs=(row, row) + weights,
        check_vma=False,
    )
```

```python
import functools

import jax
import jax.numpy as jnp
from jax import lax
from jax.experimental import pallas as pl
from jax.experimental.pallas import tpu as pltpu
from jax.sharding import Mesh
from jax.sharding import PartitionSpec as P

HD = 64
ROT = 16
LANES = 128
F32 = jnp.float32
BF16 = jnp.bfloat16
LOG2E = 1.4426950408889634
norm_eps = 1e-05
masked_value = -1e30
vmem_bytes = 60 * 2**20

NN = (((1,), (0,)), ((), ()))
NT = (((1,), (1,)), ((), ()))
TN = (((0,), (0,)), ((), ()))


def dot(left, right, dims):
    return lax.dot_general(left, right, dims, preferred_element_type=F32)


def normalise(rows):
    centre = jnp.mean(rows, axis=-1, keepdims=True)
    deviate = rows - centre
    spread = jnp.mean(deviate * deviate, axis=-1, keepdims=True)
    scale = lax.rsqrt(spread + norm_eps)
    return deviate * scale, scale


def turn(chunk, cosines, sine_low, sine_high):
    half = ROT // 2
    return (
        chunk * cosines
        + pltpu.roll(chunk, LANES - half, 1) * sine_low
        + pltpu.roll(chunk, half, 1) * sine_high
    )


def whole(shape):
    return pl.BlockSpec(shape, lambda *_: (0,) * len(shape))


def params(**kwargs):
    return pltpu.CompilerParams(vmem_limit_bytes=vmem_bytes, **kwargs)


def place_first_kernel(where, one_ref, two_ref, qkv_ref, dense_ref, small_ref):
    cols = one_ref.shape[-1] // 2
    near = where[0] == 0
    one = [one_ref[0, j] for j in range(2)]
    two = [two_ref[0, j] for j in range(2)]
    one = (jnp.where(near, one[0], one[1]), jnp.where(near, one[1], one[0]))
    two = (jnp.where(near, two[0], two[1]), jnp.where(near, two[1], two[0]))
    pieces = [one[j][:, i * cols : (i + 1) * cols] for i in range(2) for j in range(2)]
    pieces += [two[j][:, :cols] for j in range(2)]
    qkv_ref[...] = jnp.concatenate(pieces, axis=1)
    dense_ref[...] = jnp.concatenate([two[j][:, cols : 2 * cols] for j in range(2)], axis=1)
    small_ref[...] = jnp.concatenate([two[j][:, 2 * cols :] for j in range(2)], axis=1).astype(F32)


def place_second_kernel(where, one_ref, two_ref, up_ref, down_ref):
    near = where[0] == 0
    for ref, out in ((one_ref, up_ref), (two_ref, down_ref)):
        units = ref.shape[-1]
        out[:, :units] = jnp.where(near, ref[0, 0], ref[0, 1])
        out[:, units:] = jnp.where(near, ref[0, 1], ref[0, 0])


def place(kernel, where, one, two, widths, types):
    owners, _, share, _ = one.shape

    def spec(array, low, high):
        def index(i, where):
            bits = i ^ where[1]
            upper, lower, across = bits // 4, (bits // 2) % 2, bits % 2
            near, far = (across, upper) if low == "seq" else (upper, across)
            return (lower * 4 + far * 2 + near, 0, 0, 0)

        return pl.BlockSpec((1,) + array.shape[1:], index)

    return pl.pallas_call(
        kernel,
        grid_spec=pltpu.PrefetchScalarGridSpec(
            num_scalar_prefetch=1,
            grid=(owners,),
            in_specs=[spec(one, "seq", "dp"), spec(two, "dp", "seq")],
            out_specs=[pl.BlockSpec((share, width), lambda i, *_: (i, 0)) for width in widths],
        ),
        out_shape=[jax.ShapeDtypeStruct((owners * share, width), kind) for width, kind in zip(widths, types)],
        compiler_params=params(),
        cost_estimate=pl.CostEstimate(flops=0, bytes_accessed=8 * one.size, transcendentals=0),
        name="place",
    )(where, one, two)


def front_kernel(
    which, x_ref, dy_ref, w_ref, wb_ref, dense_ref, gain_ref, shift_ref, cos_ref, low_ref, high_ref,
    q_ref, kv_ref, do_ref,
):
    half = q_ref.shape[1]
    xhat, _ = normalise(x_ref[0].astype(F32))
    normed = (xhat * gain_ref[...] + shift_ref[...]).astype(BF16)
    proj = dot(normed, w_ref[...], NN) + wb_ref[...]
    cosines, low, high = cos_ref[...], low_ref[...], high_ref[...]
    for j in range(half // LANES):
        at = slice(j * LANES, (j + 1) * LANES)
        query = turn(proj[:, at], cosines, low, high).astype(BF16)
        q_ref[:, at] = query * BF16(HD**-0.5)
        key = proj[:, half + j * LANES : half + (j + 1) * LANES]
        kv_ref[:, at] = turn(key, cosines, low, high).astype(BF16)
    kv_ref[:, half:] = proj[:, 2 * half :].astype(BF16)
    do_ref[...] = dot(dy_ref[0], dense_ref[...], NN).astype(BF16)


def front(which, x, dy, w, wb, dense, gain, shift, tables):
    _, rows, width = x.shape
    half = dense.shape[1]
    step = min(512, rows)
    chosen = pl.BlockSpec((1, step, width), lambda i, which: (which[0], i, 0))
    by_row = lambda cols: pl.BlockSpec((step, cols), lambda i, *_: (i, 0))
    return pl.pallas_call(
        front_kernel,
        grid_spec=pltpu.PrefetchScalarGridSpec(
            num_scalar_prefetch=1,
            grid=(rows // step,),
            in_specs=[chosen, chosen, whole(w.shape), whole(wb.shape), whole(dense.shape),
                      whole(gain.shape), whole(shift.shape)] + [by_row(LANES)] * 3,
            out_specs=[by_row(half), by_row(2 * half), by_row(half)],
        ),
        out_shape=[
            jax.ShapeDtypeStruct((rows, half), BF16),
            jax.ShapeDtypeStruct((rows, 2 * half), BF16),
            jax.ShapeDtypeStruct((rows, half), BF16),
        ],
        compiler_params=params(),
        cost_estimate=pl.CostEstimate(
            flops=2 * rows * width * 4 * half, bytes_accessed=12 * rows * width, transcendentals=0
        ),
        name="front",
    )(which, x, dy, w, wb, dense, gain, shift, *tables)


def feed_kernel(
    which, x_ref, dy_ref, up_ref, upb_ref, down_ref, gain_ref, shift_ref, gain_col, shift_col,
    part_ref, dx_ref, gup_ref, gdown_ref, vec_ref, gupb_ref,
    up_acc, down_acc, sum_acc, dy_acc,
):
    step = pl.program_id(0)

    @pl.when(step == 0)
    def _():
        up_acc[...] = jnp.zeros_like(up_acc)
        down_acc[...] = jnp.zeros_like(down_acc)
        sum_acc[...] = jnp.zeros_like(sum_acc)
        dy_acc[...] = jnp.zeros_like(dy_acc)

    xhat, _ = normalise(x_ref[0].astype(F32))
    dy = dy_ref[0]
    normed = (xhat * gain_ref[...] + shift_ref[...]).astype(BF16)
    hidden = dot(normed, up_ref[...], NN) + upb_ref[...]
    share = 0.5 * (1.0 + lax.erf(hidden * F32(0.5**0.5)))
    act = (hidden * share).astype(BF16)
    slope = share + hidden * (jnp.exp(hidden * hidden * -0.5) * F32(0.3989422804014327))
    part_ref[...] = dot(act, down_ref[...], NT).astype(part_ref.dtype)
    grad = dot(dy, down_ref[...], NN) * slope
    grad_low = grad.astype(BF16)
    dx_ref[...] = (dot(grad_low, up_ref[...], NT) * gain_ref[...]).astype(dx_ref.dtype)
    up_acc[...] += dot(xhat.astype(BF16), grad_low, TN)
    down_acc[...] += dot(dy, act, TN)
    sum_acc[...] += jnp.sum(grad_low.astype(F32), axis=0, keepdims=True)
    dy_acc[...] += jnp.sum(dy.astype(F32), axis=0, keepdims=True)

    @pl.when(step == pl.num_programs(0) - 1)
    def _():
        sums = sum_acc[...]
        raw = up_acc[...]
        up = up_ref[...].astype(F32)
        gup_ref[...] = (raw * gain_col[...] + shift_col[...] * sums).astype(gup_ref.dtype)
        gdown_ref[...] = down_acc[...].astype(gdown_ref.dtype)
        gupb_ref[...] = sums
        lane = lax.broadcasted_iota(jnp.int32, vec_ref.shape, 1)
        gain_grad = jnp.sum(raw * up, axis=1, keepdims=True)
        shift_grad = jnp.sum(up * sums, axis=1, keepdims=True)
        dy_col = jnp.transpose(jnp.broadcast_to(dy_acc[...], (LANES, dy_acc.shape[1])))
        vec_ref[...] = jnp.where(
            lane == 0, dy_col * 0.5,
            jnp.where(lane == 3, gain_grad, jnp.where(lane == 4, shift_grad, 0.0)),
        )


def feed(which, x, dy, up, upb, down, gain, shift, gain_col, shift_col):
    _, rows, width = x.shape
    units = up.shape[1]
    step = min(256, rows)
    chosen = pl.BlockSpec((1, step, width), lambda i, which: (which[0], i, 0))
    by_row = pl.BlockSpec((step, width), lambda i, *_: (i, 0))
    return pl.pallas_call(
        feed_kernel,
        grid_spec=pltpu.PrefetchScalarGridSpec(
            num_scalar_prefetch=1,
            grid=(rows // step,),
            in_specs=[chosen, chosen, whole(up.shape), whole(upb.shape), whole(down.shape),
                      whole(gain.shape), whole(shift.shape), whole(gain_col.shape), whole(shift_col.shape)],
            out_specs=[by_row, by_row, whole((width, units)), whole((width, units)),
                       whole((width, LANES)), whole((1, units))],
            scratch_shapes=[pltpu.VMEM((width, units), F32), pltpu.VMEM((width, units), F32),
                            pltpu.VMEM((1, units), F32), pltpu.VMEM((1, width), F32)],
        ),
        out_shape=[
            jax.ShapeDtypeStruct((rows, width), BF16),
            jax.ShapeDtypeStruct((rows, width), BF16),
            jax.ShapeDtypeStruct((width, units), BF16),
            jax.ShapeDtypeStruct((width, units), BF16),
            jax.ShapeDtypeStruct((width, LANES), F32),
            jax.ShapeDtypeStruct((1, units), F32),
        ],
        compiler_params=params(),
        cost_estimate=pl.CostEstimate(
            flops=12 * rows * width * units, bytes_accessed=24 * width * units, transcendentals=2 * rows * units
        ),
        name="feed",
    )(which, x, dy, up, upb, down, gain, shift, gain_col, shift_col)


def lane_fold(values, combine):
    total = values[:, :LANES]
    for j in range(1, values.shape[1] // LANES):
        total = combine(total, values[:, j * LANES : (j + 1) * LANES])
    return total


def pick_heads(both, heads):
    return [jnp.where(mine, both, jnp.zeros_like(both)) for mine in heads]


def attend_kernel(info, slots, q_ref, g_ref, dense_ref, prior_ref, *refs, block, run_rows, parts, run):
    k_parts, v_parts, refs = refs[:parts], refs[parts : 2 * parts], refs[2 * parts :]
    o_ref, stat_ref, send_ref, keep_ref, k_ref, v_ref, score_ref, acc_ref, branch_ref = refs
    per_run = run_rows // block
    pair, place_in_run = pl.program_id(0), pl.program_id(1)
    full = info[run]

    @pl.when((pair == 0) & (place_in_run == 0))
    def _():
        branch_ref[...] = prior_ref[...].astype(F32)

    @pl.when(place_in_run == 0)
    def _():
        at = 0
        for j in range(parts):
            there = pl.ds(at, k_parts[j].shape[0])
            k_ref[there, :] = k_parts[j][...]
            v_ref[there, :] = v_parts[j][...]
            at += k_parts[j].shape[0]

    lane = lax.broadcasted_iota(jnp.int32, (block, LANES), 1)
    heads = (lane < HD, lane >= HD)

    def rows_of(at, count):
        return pl.ds(pl.multiple_of(slots[at] * run_rows, run_rows), count)

    def one_block(within):
        queries = pick_heads(q_ref[...], heads)
        seen = (within + 1) * block

        def score(at, tops, last):
            count = seen if last else run_rows
            keys = k_ref[rows_of(at, count), :]
            out = []
            for h in range(2):
                scores = dot(queries[h], keys, NT)
                if last:
                    row = lax.broadcasted_iota(jnp.int32, (block, count), 0)
                    col = lax.broadcasted_iota(jnp.int32, (block, count), 1)
                    scores = jnp.where(col <= row + within * block, scores, masked_value)
                score_ref[h, at, :, :count] = scores
                out.append(jnp.maximum(tops[h], lane_fold(scores, jnp.maximum)))
            return tuple(out)

        least = jnp.full((block, LANES), masked_value, F32)
        tops = lax.fori_loop(0, full, lambda at, carry: score(at, carry, False), (least, least))
        tops = score(full, tops, True)
        tops = [jnp.max(top, axis=1, keepdims=True) * F32(LOG2E) for top in tops]

        acc_ref[...] = jnp.zeros_like(acc_ref)

        def weigh(at, totals, last):
            count = seen if last else run_rows
            values = v_ref[rows_of(at, count), :]
            out = []
            for h in range(2):
                soft = jnp.exp2(score_ref[h, at, :, :count] * F32(LOG2E) - tops[h])
                out.append(totals[h] + lane_fold(soft, jnp.add))
                acc_ref[h] += dot(soft.astype(BF16), values, NN)
            return tuple(out)

        nought = jnp.zeros((block, LANES), F32)
        totals = lax.fori_loop(0, full, lambda at, carry: weigh(at, carry, False), (nought, nought))
        totals = weigh(full, totals, True)
        totals = [jnp.sum(total, axis=1, keepdims=True) for total in totals]
        attended = jnp.where(heads[0], acc_ref[0] / totals[0], acc_ref[1] / totals[1])
        o_ref[...] = attended.astype(o_ref.dtype)
        mine = pl.ds(within * block, block)
        branch_ref[mine, :] += dot(attended.astype(BF16), dense_ref[...], NT)
        product = attended * g_ref[...].astype(F32)
        row_terms = [jnp.sum(jnp.where(mine, product, 0.0), axis=1, keepdims=True) for mine in heads]
        logs = [tops[h] + jnp.log2(totals[h]) for h in range(2)]
        stats = jnp.where(lane == 0, logs[0], jnp.where(lane == 1, logs[1], 0.0))
        stats = jnp.where(lane == 2, row_terms[0], jnp.where(lane == 3, row_terms[1], stats))
        stat_ref[...] = jnp.transpose(stats)[:8]

    for within in range(per_run):
        pl.when(place_in_run == within)(functools.partial(one_block, within))

    @pl.when((pair == pl.num_programs(0) - 1) & (place_in_run == per_run - 1))
    def _():
        half = run_rows // 2
        send_ref[...] = branch_ref[pl.ds(pl.multiple_of((1 - info[2]) * half, half), half), :].astype(BF16)
        keep_ref[...] = branch_ref[pl.ds(pl.multiple_of(info[2] * half, half), half), :]


def attend(info, slots, q, g, kv_parts, dense, prior, run):
    rows, width = q.shape
    model = dense.shape[0]
    keys = sum(kv.shape[0] for kv in kv_parts)
    run_rows = rows // 2
    block = min(512, run_rows)
    per_run = run_rows // block
    pairs = width // LANES
    by_query = pl.BlockSpec((block, LANES), lambda p, i, *_: (run * per_run + i, p))
    by_key = [pl.BlockSpec((kv.shape[0], LANES), lambda p, i, *_: (0, p)) for kv in kv_parts]
    by_value = [pl.BlockSpec((kv.shape[0], LANES), lambda p, i, *_: (0, pairs + p)) for kv in kv_parts]
    kernel = functools.partial(attend_kernel, block=block, run_rows=run_rows, parts=len(kv_parts), run=run)
    return pl.pallas_call(
        kernel,
        grid_spec=pltpu.PrefetchScalarGridSpec(
            num_scalar_prefetch=2,
            grid=(pairs, per_run),
            in_specs=[
                by_query, by_query,
                pl.BlockSpec((model, LANES), lambda p, i, *_: (0, p)),
                pl.BlockSpec((run_rows, model), lambda p, i, *_: (run, 0)),
                *by_key, *by_value,
            ],
            out_specs=[
                pl.BlockSpec((block, LANES), lambda p, i, *_: (i, p)),
                pl.BlockSpec((8, block), lambda p, i, *_: (p, i)),
                whole((run_rows // 2, model)),
                whole((run_rows // 2, model)),
            ],
            scratch_shapes=[
                pltpu.VMEM((keys, LANES), BF16),
                pltpu.VMEM((keys, LANES), BF16),
                pltpu.VMEM((2, keys // run_rows, block, run_rows), F32),
                pltpu.VMEM((2, block, LANES), F32),
                pltpu.VMEM((run_rows, model), F32),
            ],
        ),
        out_shape=[
            jax.ShapeDtypeStruct((run_rows, width), BF16),
            jax.ShapeDtypeStruct((8 * pairs, run_rows), F32),
            jax.ShapeDtypeStruct((run_rows // 2, model), BF16),
            jax.ShapeDtypeStruct((run_rows // 2, model), F32),
        ],
        compiler_params=params(),
        cost_estimate=pl.CostEstimate(
            flops=24 * run_rows * keys * width, bytes_accessed=12 * keys * width,
            transcendentals=run_rows * keys * pairs,
        ),
        name="attend",
    )(info, slots, q, g, dense, prior, *kv_parts, *kv_parts)


def attend_back_kernel(info, slots, q_ref, g_ref, stat_ref, *refs, block, run_rows, parts, home):
    k_parts, v_parts, refs = refs[:parts], refs[parts : 2 * parts], refs[2 * parts :]
    dq_ref, dk_out, dv_out, refs = refs[0], refs[1], refs[2], refs[3:]
    if home:
        back_ref, refs = refs[0], refs[1:]
    k_ref, v_ref, dk_ref, dv_ref, acc_ref = refs
    per_run = run_rows // block
    step = pl.program_id(0)
    full = info[step // per_run]

    @pl.when(step == 0)
    def _():
        at = 0
        for j in range(parts):
            there = pl.ds(at, k_parts[j].shape[0])
            k_ref[there, :] = k_parts[j][...]
            v_ref[there, :] = v_parts[j][...]
            at += k_parts[j].shape[0]
        dk_ref[...] = jnp.zeros_like(dk_ref)
        dv_ref[...] = jnp.zeros_like(dv_ref)

    lane = lax.broadcasted_iota(jnp.int32, (block, LANES), 1)
    heads = (lane < HD, lane >= HD)

    def rows_of(at, count):
        return pl.ds(pl.multiple_of(slots[at] * run_rows, run_rows), count)

    def one_block(within):
        queries, grads = pick_heads(q_ref[...], heads), pick_heads(g_ref[...], heads)
        stats = jnp.transpose(stat_ref[...])
        logs, row_terms = [stats[:, h : h + 1] for h in range(2)], [stats[:, 2 + h : 3 + h] for h in range(2)]
        seen = (within + 1) * block
        acc_ref[...] = jnp.zeros_like(acc_ref)

        def back(at, last):
            count = seen if last else run_rows
            there = rows_of(at, count)
            keys, values = k_ref[there, :], v_ref[there, :]
            key_terms, value_terms = [], []
            for h in range(2):
                soft = jnp.exp2(dot(queries[h], keys, NT) * F32(LOG2E) - logs[h])
                if last:
                    row = lax.broadcasted_iota(jnp.int32, (block, count), 0)
                    col = lax.broadcasted_iota(jnp.int32, (block, count), 1)
                    soft = jnp.where(col <= row + within * block, soft, 0.0)
                grad_soft = dot(grads[h], values, NT)
                grad_score = (soft * (grad_soft - row_terms[h])).astype(BF16)
                acc_ref[h] += dot(grad_score, keys, NN)
                key_terms.append(dot(grad_score, queries[h], TN))
                value_terms.append(dot(soft.astype(BF16), grads[h], TN))
            dk_ref[there, :] += key_terms[0] + key_terms[1]
            dv_ref[there, :] += value_terms[0] + value_terms[1]

        def back_whole(at, carry):
            back(at, False)
            return carry

        lax.fori_loop(0, full, back_whole, 0)
        back(full, True)
        dq_ref[...] = (jnp.where(heads[0], acc_ref[0], acc_ref[1]) * F32(HD**-0.5)).astype(dq_ref.dtype)

    for within in range(per_run):
        pl.when(step % per_run == within)(functools.partial(one_block, within))

    @pl.when(step == pl.num_programs(0) - 1)
    def _():
        own = dk_out.shape[0]
        dk_out[...] = dk_ref[:own, :]
        dv_out[...] = dv_ref[:own, :]
        if home:
            back_ref[:, :LANES] = dk_ref[home:, :].astype(BF16)
            back_ref[:, LANES:] = dv_ref[home:, :].astype(BF16)


def attend_back(info, slots, q, g, stats, kv_parts, pair, home):
    rows, width = q.shape
    keys = sum(kv.shape[0] for kv in kv_parts)
    run_rows = rows // 2
    block = min(512, run_rows)
    pairs = width // LANES
    own = home or keys
    by_query = pl.BlockSpec((block, LANES), lambda i, *_: (i, pair))
    by_key = [pl.BlockSpec((kv.shape[0], LANES), lambda i, *_: (0, pair)) for kv in kv_parts]
    by_value = [pl.BlockSpec((kv.shape[0], LANES), lambda i, *_: (0, pairs + pair)) for kv in kv_parts]
    kernel = functools.partial(
        attend_back_kernel, block=block, run_rows=run_rows, parts=len(kv_parts), home=home
    )
    out_specs = [pl.BlockSpec((block, LANES), lambda i, *_: (i, 0)), whole((own, LANES)), whole((own, LANES))]
    out_shape = [
        jax.ShapeDtypeStruct((rows, LANES), BF16),
        jax.ShapeDtypeStruct((own, LANES), F32),
        jax.ShapeDtypeStruct((own, LANES), F32),
    ]
    if home:
        out_specs.append(whole((keys - home, 2 * LANES)))
        out_shape.append(jax.ShapeDtypeStruct((keys - home, 2 * LANES), BF16))
    return pl.pallas_call(
        kernel,
        grid_spec=pltpu.PrefetchScalarGridSpec(
            num_scalar_prefetch=2,
            grid=(rows // block,),
            in_specs=[by_query, by_query, pl.BlockSpec((8, block), lambda i, *_: (pair, i)), *by_key, *by_value],
            out_specs=out_specs,
            scratch_shapes=[
                pltpu.VMEM((keys, LANES), BF16),
                pltpu.VMEM((keys, LANES), BF16),
                pltpu.VMEM((keys, LANES), F32),
                pltpu.VMEM((keys, LANES), F32),
                pltpu.VMEM((2, block, LANES), F32),
            ],
        ),
        out_shape=out_shape,
        compiler_params=params(),
        cost_estimate=pl.CostEstimate(
            flops=30 * rows * keys * LANES, bytes_accessed=12 * keys * width, transcendentals=rows * keys
        ),
        name="attend_back",
    )(info, slots, q, g, stats, *kv_parts, *kv_parts)


def back_kernel(which, dq_ref, *refs, pairs):
    own_k, refs = refs[:pairs], refs[pairs:]
    own_v, refs = refs[:pairs], refs[pairs:]
    got, refs = refs[:pairs], refs[pairs:]
    w_ref, gain_ref, dx_in, cos_ref, low_ref, high_ref, dproj_ref, send_ref, keep_ref = refs
    half = dq_ref.shape[1]
    cosines, low, high = cos_ref[...], low_ref[...], high_ref[...]
    for j in range(pairs):
        at = slice(j * LANES, (j + 1) * LANES)
        query = dq_ref[:, at].astype(F32)
        dproj_ref[:, at] = turn(query, cosines, -low, -high).astype(BF16)
        key = own_k[j][...] + got[j][:, :LANES].astype(F32)
        dproj_ref[:, half + j * LANES : half + (j + 1) * LANES] = turn(key, cosines, -low, -high).astype(BF16)
        value = own_v[j][...] + got[j][:, LANES:].astype(F32)
        dproj_ref[:, 2 * half + j * LANES : 2 * half + (j + 1) * LANES] = value.astype(BF16)
    summed = dot(dproj_ref[...], w_ref[...], NT) * gain_ref[...] + dx_in[...].astype(F32)
    mine = pl.program_id(0) % 2 == which[1]

    @pl.when(mine)
    def _():
        keep_ref[...] = summed

    @pl.when(jnp.logical_not(mine))
    def _():
        send_ref[...] = summed.astype(send_ref.dtype)


def back(which, dq, dk, dv, got, w, gain, dx_part, tables):
    rows, half = dq.shape
    width = w.shape[0]
    step = rows // 4
    pairs = len(dk)
    by_row = lambda cols: pl.BlockSpec((step, cols), lambda i, *_: (i, 0))
    by_run = pl.BlockSpec((step, width), lambda i, *_: (i // 2, 0))
    return pl.pallas_call(
        functools.partial(back_kernel, pairs=pairs),
        grid_spec=pltpu.PrefetchScalarGridSpec(
            num_scalar_prefetch=1,
            grid=(4,),
            in_specs=[by_row(half)] + [by_row(LANES)] * (2 * pairs) + [by_row(2 * LANES)] * pairs
            + [whole(w.shape), whole(gain.shape), by_row(width)] + [by_row(LANES)] * 3,
            out_specs=[by_row(3 * half), by_run, by_run],
        ),
        out_shape=[
            jax.ShapeDtypeStruct((rows, 3 * half), BF16),
            jax.ShapeDtypeStruct((rows // 2, width), BF16),
            jax.ShapeDtypeStruct((rows // 2, width), F32),
        ],
        compiler_params=params(),
        cost_estimate=pl.CostEstimate(
            flops=6 * rows * width * half, bytes_accessed=12 * rows * width, transcendentals=0
        ),
        name="back",
    )(which, dq, *dk, *dv, *got, w, gain, dx_part, *tables)


def weight_kernel(
    which, x_ref, dy_ref, dproj_ref, o_ref, w_ref, gain_col, shift_col,
    gqkv_ref, gdense_ref, vec_ref, gb_ref, acc, dense_acc, sum_acc,
):
    step = pl.program_id(0)

    @pl.when(step == 0)
    def _():
        acc[...] = jnp.zeros_like(acc)
        dense_acc[...] = jnp.zeros_like(dense_acc)
        sum_acc[...] = jnp.zeros_like(sum_acc)

    xhat, _ = normalise(x_ref[0].astype(F32))
    dproj = dproj_ref[...]
    acc[...] += dot(xhat.astype(BF16), dproj, TN)
    dense_acc[...] += dot(dy_ref[0], o_ref[...], TN)
    sum_acc[...] += jnp.sum(dproj.astype(F32), axis=0, keepdims=True)

    @pl.when(step == pl.num_programs(0) - 1)
    def _():
        sums, raw, w = sum_acc[...], acc[...], w_ref[...].astype(F32)
        gqkv_ref[...] = (raw * gain_col[...] + shift_col[...] * sums).astype(gqkv_ref.dtype)
        gdense_ref[...] = dense_acc[...].astype(gdense_ref.dtype)
        gb_ref[...] = sums
        lane = lax.broadcasted_iota(jnp.int32, vec_ref.shape, 1)
        gain_grad = jnp.sum(raw * w, axis=1, keepdims=True)
        shift_grad = jnp.sum(w * sums, axis=1, keepdims=True)
        vec_ref[...] = jnp.where(lane == 1, gain_grad, jnp.where(lane == 2, shift_grad, 0.0))


def weight_grads(which, x, dy, dproj, o, w, gain_col, shift_col):
    _, rows, width = x.shape
    half = o.shape[1]
    step = min(512, rows)
    chosen = pl.BlockSpec((1, step, width), lambda i, which: (which[0], i, 0))
    by_row = lambda cols: pl.BlockSpec((step, cols), lambda i, *_: (i, 0))
    return pl.pallas_call(
        weight_kernel,
        grid_spec=pltpu.PrefetchScalarGridSpec(
            num_scalar_prefetch=1,
            grid=(rows // step,),
            in_specs=[chosen, chosen, by_row(3 * half), by_row(half), whole(w.shape),
                      whole(gain_col.shape), whole(shift_col.shape)],
            out_specs=[whole((width, 3 * half)), whole((width, half)), whole((width, LANES)), whole((1, 3 * half))],
            scratch_shapes=[pltpu.VMEM((width, 3 * half), F32), pltpu.VMEM((width, half), F32),
                            pltpu.VMEM((1, 3 * half), F32)],
        ),
        out_shape=[
            jax.ShapeDtypeStruct((width, 3 * half), BF16),
            jax.ShapeDtypeStruct((width, half), BF16),
            jax.ShapeDtypeStruct((width, LANES), F32),
            jax.ShapeDtypeStruct((1, 3 * half), F32),
        ],
        compiler_params=params(),
        cost_estimate=pl.CostEstimate(
            flops=8 * rows * width * half, bytes_accessed=12 * rows * width, transcendentals=0
        ),
        name="weight_grads",
    )(which, x, dy, dproj, o, w, gain_col, shift_col)


def norm_back_kernel(which, x_ref, dy_ref, kept_ref, got_ref, out_ref):
    xhat, scale = normalise(x_ref[0].astype(F32))
    grad = kept_ref[...].astype(F32) + got_ref[...].astype(F32)
    centre = jnp.mean(grad, axis=-1, keepdims=True)
    along = jnp.mean(grad * xhat, axis=-1, keepdims=True)
    out_ref[...] = (dy_ref[0].astype(F32) + scale * (grad - centre - xhat * along)).astype(out_ref.dtype)


def norm_back(which, x, dy, kept, got, run):
    rows, width = got.shape
    step = min(256, rows)
    blocks = rows // step
    chosen = pl.BlockSpec(
        (1, step, width), lambda i, which: (which[0], (2 * run + which[1]) * blocks + i, 0)
    )
    return pl.pallas_call(
        norm_back_kernel,
        grid_spec=pltpu.PrefetchScalarGridSpec(
            num_scalar_prefetch=1,
            grid=(blocks,),
            in_specs=[chosen, chosen,
                      pl.BlockSpec((step, width), lambda i, *_: (run * blocks + i, 0)),
                      pl.BlockSpec((step, width), lambda i, *_: (i, 0))],
            out_specs=pl.BlockSpec((step, width), lambda i, *_: (i, 0)),
        ),
        out_shape=jax.ShapeDtypeStruct((rows, width), BF16),
        compiler_params=params(),
        cost_estimate=pl.CostEstimate(
            flops=20 * rows * width, bytes_accessed=10 * rows * width, transcendentals=0
        ),
        name="norm_back",
    )(which, x, dy, kept, got)


def lay_kernel(index, *refs):
    pieces, out, sems = refs[:-2], refs[-2], refs[-1]
    half = pieces[0].shape[0]
    copies = []
    for j, piece in enumerate(pieces):
        run, back = j // 4, j % 4
        slot = lax.rem(index[0] + (4 - back), 4)
        start = pl.multiple_of(lax.rem(slot, 2) * half, half) + run * 2 * half
        there = out.at[slot // 2, pl.ds(pl.multiple_of(start, half), half), :]
        copies.append(pltpu.make_async_copy(piece, there, sems.at[j]))
        copies[-1].start()
    for copy in copies:
        copy.wait()


def lay(index, early, late):
    half, width = early[0].shape
    anywhere = pl.BlockSpec(memory_space=pl.ANY)
    return pl.pallas_call(
        lay_kernel,
        grid_spec=pltpu.PrefetchScalarGridSpec(
            num_scalar_prefetch=1,
            grid=(),
            in_specs=[anywhere] * 8,
            out_specs=anywhere,
            scratch_shapes=[pltpu.SemaphoreType.DMA((8,))],
        ),
        out_shape=jax.ShapeDtypeStruct((2, 4 * half, width), BF16),
        cost_estimate=pl.CostEstimate(flops=0, bytes_accessed=32 * half * width, transcendentals=0),
        name="lay",
    )(index[None], *early, *late)


def swap(values, axis):
    return lax.ppermute(values, axis, [(0, 1), (1, 0)])


def across(values, bit):
    return lax.ppermute(values, "dp", [(i, i ^ bit) for i in range(4)])


def gather_half(values, seq_first):
    values = jnp.concatenate([values[None], swap(values, "mh")[None]], axis=0)
    steps = [lambda v: swap(v, "seq"), lambda v: across(v, 2)]
    for step in steps if seq_first else steps[::-1]:
        values = jnp.concatenate([values, step(values)], axis=0)
    values = jnp.concatenate([values, across(values, 1)], axis=0)
    return values.reshape(8, 2, *values.shape[1:])


def round_mp(mine):
    axes = ("mh", "ml")
    return [mine] + [lax.ppermute(mine, axes, [(i, (i + k) % 4) for i in range(4)]) for k in (1, 2, 3)]


def rotation_tables(positions):
    half = ROT // 2
    frequency = jnp.power(F32(10000.0), -2.0 * jnp.arange(half, dtype=F32) / ROT)
    angles = frequency[:, None] * positions.astype(F32)[None, :]
    cosines, sines = lax.optimization_barrier((jnp.cos(angles), jnp.sin(angles)))
    cosines, sines = cosines.T, sines.T
    rows = positions.shape[0]
    rest = jnp.zeros((rows, HD - ROT), F32)
    blank = jnp.zeros((rows, half), F32)
    per_head = (
        jnp.concatenate([cosines, cosines, rest + 1.0], axis=1),
        jnp.concatenate([-sines, blank, rest], axis=1),
        jnp.concatenate([blank, sines, rest], axis=1),
    )
    return tuple(jnp.tile(table, (1, LANES // HD)) for table in per_head)


def body(
    tokens, places, w_qkv, b_qkv, w_dense, b_dense, w_up, b_up, w_down, b_down,
    norm1_gain, norm1_bias, norm2_gain, norm2_bias, out_grad, *, seq_size, owners,
):
    _, rows, width = tokens.shape
    share = width // owners
    heads = b_qkv.shape[1]
    cols = heads * HD
    units = w_up.shape[1]
    side, part = lax.axis_index("mh"), lax.axis_index("ml")
    index = (2 * side + part).astype(jnp.int32)
    owner = lax.axis_index("dp") * seq_size + lax.axis_index("seq")
    which = jnp.stack([side, part]).astype(jnp.int32)
    where = jnp.stack([side, owner]).astype(jnp.int32)

    def column(vector):
        vector = vector.reshape(-1)
        return jnp.pad(vector, (0, share - vector.shape[0]))[:, None]

    small = jnp.concatenate(
        [column(v) for v in (b_dense, b_down, norm1_gain, norm1_bias, norm2_gain, norm2_bias, b_qkv, b_up)],
        axis=1,
    )
    small = jnp.pad(small, ((0, 0), (0, LANES - small.shape[1])))
    one = w_qkv[:2].transpose(1, 0, 2).reshape(share, 2 * cols)
    two = jnp.concatenate([w_qkv[2], w_dense.T, small], axis=1)
    three, four = w_up, w_down.T
    first_widths = (6 * cols, 2 * cols, 2 * LANES)
    if owners == 8 and seq_size == 2:
        one, two = gather_half(one, True), gather_half(two, False)
        qkv_w, dense_w, small = place(place_first_kernel, where, one, two, first_widths, (BF16, BF16, F32))
        three = jnp.concatenate([three, four], axis=1)
        other = swap(three, "mh")
        three = jnp.concatenate([jnp.where(side == 0, three, other), jnp.where(side == 0, other, three)], axis=1)
        three = lax.all_gather(three, ("dp", "seq"), axis=0, tiled=True)
        up_w = jnp.concatenate([three[:, :units], three[:, 2 * units : 3 * units]], axis=1)
        down_w = jnp.concatenate([three[:, units : 2 * units], three[:, 3 * units :]], axis=1)
    else:

        def gather(values):
            values = lax.all_gather(values, ("dp", "seq", "mh"), axis=0, tiled=True)
            return values.reshape(owners, 2, share, -1).transpose(0, 2, 1, 3).reshape(width, 2, -1)

        one, two, three, four = gather(one), gather(two), gather(three), gather(four)
        qkv_w = jnp.concatenate([one[:, :, :cols], one[:, :, cols:], two[:, :, :cols]], axis=1)
        qkv_w, dense_w = qkv_w.reshape(width, 6 * cols), two[:, :, cols : 2 * cols].reshape(width, 2 * cols)
        small = two[:, :, 2 * cols :].reshape(width, 2 * LANES).astype(F32)
        up_w, down_w = three.reshape(width, 2 * units), four.reshape(width, 2 * units)
    vectors = small[:, :8]
    piece = HD // owners
    biases = small.reshape(owners, share, 2, LANES)
    qkv_b = biases[:, : 3 * heads * piece, :, 6].reshape(owners, 3, heads, piece, 2)
    qkv_b = qkv_b.transpose(1, 4, 2, 0, 3).reshape(1, 6 * cols)
    up_rows, up_cols = b_up.shape
    up_b = biases[..., 7].reshape(owners, up_rows, up_cols, 2).transpose(3, 1, 0, 2).reshape(1, 2 * units)
    by_row = vectors.T
    row_of = lambda at: by_row[at].reshape(1, width)
    column_of = lambda at: vectors[:, at].reshape(width, 1)

    my_places = lax.dynamic_index_in_dim(places, side, 0, keepdims=False)
    run_rows = rows // 2
    runs = jnp.stack([my_places[0], my_places[run_rows]]) // run_rows
    if seq_size == 2:
        all_runs = jnp.concatenate([runs, swap(runs, "seq")])
    else:
        all_runs = lax.all_gather(runs, "seq", axis=0, tiled=True)
    order = jnp.arange(2 * seq_size, dtype=jnp.int32)
    slots = jnp.sum(jnp.where(all_runs[None, :] == order[:, None], order[None, :], 0), axis=1)
    tables = rotation_tables(my_places)

    q, kv, grad_o = front(which, tokens, out_grad, qkv_w, qkv_b, dense_w, row_of(2), row_of(3), tables)
    if seq_size == 2:
        kv_parts = (kv, swap(kv, "seq"))
    else:
        kv_parts = (lax.all_gather(kv, "seq", axis=0, tiled=True),)

    mlp_part, mlp_dx, grad_up, grad_down, mlp_vectors, grad_up_b = feed(
        which, tokens, out_grad, up_w, up_b, down_w, row_of(4), row_of(5), column_of(4), column_of(5)
    )
    info = jnp.concatenate([runs, which[1:]])
    quarter = rows // 4

    def finish(run, kept, got):
        mine = lax.dynamic_slice(tokens, (side, run * run_rows + part * quarter, 0), (1, quarter, width))[0]
        return (kept + got.astype(F32) + mine.astype(F32) + row_of(0) + row_of(1)).astype(BF16)

    o_early, stat_early, send, keep_early = attend(info, slots, q, grad_o, kv_parts, dense_w, mlp_part, 0)
    got_early = swap(send, "ml")
    q_late, send = lax.optimization_barrier((q, send))
    o_late, stat_late, send, keep_late = attend(info, slots, q_late, grad_o, kv_parts, dense_w, mlp_part, 1)
    got_late = swap(send, "ml")
    mixed_early = finish(0, keep_early, got_early)
    stats, mixed_early = lax.optimization_barrier((jnp.concatenate([stat_early, stat_late], axis=1), mixed_early))
    mixed_early = round_mp(mixed_early)

    home = rows if seq_size == 2 else 0
    dq, dk, dv, got = [], [], [], []
    q_next = q
    for pair in range(q.shape[1] // LANES):
        outs = attend_back(info, slots, q_next, grad_o, stats, kv_parts, pair, home)
        dq.append(outs[0])
        if home:
            dk.append(outs[1])
            dv.append(outs[2])
            got.append(swap(outs[3], "seq"))
            tied = outs[3]
        else:
            both = jnp.concatenate([outs[1], outs[2]], axis=1).astype(BF16)
            got.append(lax.psum_scatter(both, "seq", scatter_dimension=0, tiled=True))
            dk.append(jnp.zeros((rows, LANES), F32))
            dv.append(jnp.zeros((rows, LANES), F32))
            tied = outs[0]
        if pair == 0:
            mixed_late = finish(1, keep_late, got_late)
            q_next, _, mixed_late = lax.optimization_barrier((q, tied, mixed_late))
            mixed_late = round_mp(mixed_late)
        else:
            q_next, _ = lax.optimization_barrier((q, tied))
    mixed = lay(index, mixed_early, mixed_late)
    dq = jnp.concatenate(dq, axis=1)
    dproj, send, keep = back(which, dq, dk, dv, got, qkv_w, row_of(2), mlp_dx, tables)
    got = [swap(send[run * quarter : (run + 1) * quarter], "ml") for run in range(2)]
    input_grad = [round_mp(norm_back(which, tokens, out_grad, keep, got[run], run)) for run in range(2)]
    input_grad = lay(index, *input_grad)

    attended = jnp.concatenate([o_early, o_late], axis=0)
    grad_qkv, grad_dense, qkv_vectors, grad_qkv_b = weight_grads(
        which, tokens, out_grad, dproj, attended, qkv_w, column_of(2), column_of(3)
    )

    def scatter(grads):
        return lax.psum_scatter(grads, ("dp", "seq"), scatter_dimension=0, tiled=True)

    def settle(sums):
        sums = sums.astype(F32)
        mine = lax.dynamic_index_in_dim(sums, side, 1, keepdims=False)
        other = lax.dynamic_index_in_dim(sums, 1 - side, 1, keepdims=False)
        return mine + swap(other.astype(BF16), "mh").astype(F32)

    owned_up = settle(scatter(grad_up).reshape(share, 2, units))
    owned_down = settle(scatter(grad_down).reshape(share, 2, units))
    vector_grads = (mlp_vectors + qkv_vectors)[:, None, :5]
    vector_grads = jnp.broadcast_to(vector_grads, (width, 2, 5))
    bias_qkv = grad_qkv_b.reshape(3, 2, heads, owners, piece).transpose(3, 0, 2, 4, 1)
    bias_qkv = bias_qkv.reshape(owners, 3 * heads * piece, 2)
    bias_qkv = jnp.pad(bias_qkv, ((0, 0), (0, share - 3 * heads * piece), (0, 0))).reshape(width, 2, 1)
    bias_up = grad_up_b.reshape(2, up_rows, owners, up_cols).transpose(2, 1, 3, 0).reshape(width, 2, 1)
    tail = jnp.concatenate([vector_grads, bias_qkv, bias_up], axis=2)
    tail = jnp.pad(tail, ((0, 0), (0, 0), (0, LANES // 2 - 7))).astype(BF16).reshape(width, LANES)
    first = scatter(jnp.concatenate([grad_qkv, grad_dense, tail], axis=1))
    owned_qkv = first[:, : 6 * cols].reshape(share, 3, 2, cols).transpose(0, 2, 1, 3).reshape(share, 2, 3 * cols)
    owned_dense = first[:, 6 * cols : 8 * cols].reshape(share, 2, cols)
    owned_tail = first[:, 8 * cols :].reshape(share, 2, LANES // 2)
    owned = settle(jnp.concatenate([owned_qkv, owned_dense, owned_tail], axis=2))
    vectors = owned[:, 4 * cols :]
    norms = vectors[:, :5]
    norms = norms + swap(norms, "ml")
    bias_grad = norms[:, 0]
    return (
        mixed,
        input_grad,
        owned[:, : 3 * cols].reshape(share, 3, cols).transpose(1, 0, 2),
        vectors[: 3 * heads * piece, 5].reshape(b_qkv.shape),
        owned[:, 3 * cols : 4 * cols].T,
        bias_grad,
        owned_up,
        vectors[:, 6].reshape(b_up.shape),
        owned_down.T,
        bias_grad,
        norms[:, 1],
        norms[:, 2],
        norms[:, 3],
        norms[:, 4],
    )


def solution(mesh):
    dp, seq, mp = (mesh.shape[axis] for axis in ("dp", "seq", "mp"))
    split = Mesh(mesh.devices.reshape(dp, seq, 2, mp // 2), ("dp", "seq", "mh", "ml"))
    mp, owner = ("mh", "ml"), ("dp", "seq")
    row = P("dp", "seq", None)
    vector = P(owner)
    weights = (
        P(None, owner, mp), P(None, mp, owner), P(mp, owner), vector, P(owner, mp), P(mp, owner),
        P(mp, owner), vector, vector, vector, vector, vector,
    )
    return jax.shard_map(
        functools.partial(body, seq_size=seq, owners=dp * seq),
        mesh=split,
        in_specs=(row, P("dp", "seq")) + weights + (row,),
        out_specs=(row, row) + weights,
        check_vma=False,
    )
```

```python
import functools

import jax
import jax.numpy as jnp
from jax import lax
from jax.experimental import pallas as pl
from jax.experimental.pallas import tpu as pltpu
from jax.sharding import Mesh
from jax.sharding import PartitionSpec as P

HD = 64
ROT = 16
LANES = 128
F32 = jnp.float32
BF16 = jnp.bfloat16
LOG2E = 1.4426950408889634
norm_eps = 1e-05
masked_value = -1e30
vmem_bytes = 60 * 2**20
brief = pl.CostEstimate(flops=1, bytes_accessed=1, transcendentals=0)
long = pl.CostEstimate(flops=2**33, bytes_accessed=2**24, transcendentals=0)

NN = (((1,), (0,)), ((), ()))
NT = (((1,), (1,)), ((), ()))
TN = (((0,), (0,)), ((), ()))


def dot(left, right, dims):
    return lax.dot_general(left, right, dims, preferred_element_type=F32)


def normalise(rows):
    centre = jnp.mean(rows, axis=-1, keepdims=True)
    deviate = rows - centre
    spread = jnp.mean(deviate * deviate, axis=-1, keepdims=True)
    scale = lax.rsqrt(spread + norm_eps)
    return deviate * scale, scale


def turn(chunk, cosines, sine_low, sine_high):
    half = ROT // 2
    return (
        chunk * cosines
        + pltpu.roll(chunk, LANES - half, 1) * sine_low
        + pltpu.roll(chunk, half, 1) * sine_high
    )

longest = pl.CostEstimate(flops=2**36, bytes_accessed=2**27, transcendentals=0)


anywhere = pl.BlockSpec(memory_space=pl.ANY)


def whole(shape):
    return pl.BlockSpec(shape, lambda *_: (0,) * len(shape))


def params(**kwargs):
    return pltpu.CompilerParams(vmem_limit_bytes=vmem_bytes, **kwargs)


def place_first_kernel(where, one_ref, two_ref, qkv_ref, dense_ref, small_ref):
    cols = one_ref.shape[-1] // 2
    near = where[0] == 0
    one = [one_ref[0, j] for j in range(2)]
    two = [two_ref[0, j] for j in range(2)]
    one = (jnp.where(near, one[0], one[1]), jnp.where(near, one[1], one[0]))
    two = (jnp.where(near, two[0], two[1]), jnp.where(near, two[1], two[0]))
    pieces = [one[j][:, i * cols : (i + 1) * cols] for i in range(2) for j in range(2)]
    pieces += [two[j][:, :cols] for j in range(2)]
    qkv_ref[...] = jnp.concatenate(pieces, axis=1)
    dense_ref[...] = jnp.concatenate([two[j][:, cols : 2 * cols] for j in range(2)], axis=1)
    small_ref[...] = jnp.concatenate([two[j][:, 2 * cols :] for j in range(2)], axis=1).astype(F32)


def place_second_kernel(pack_ref, up_ref, down_ref):
    units = pack_ref.shape[-1] // 2
    for j in range(2):
        up_ref[:, j * units : (j + 1) * units] = pack_ref[0, j, :, :units]
        down_ref[:, j * units : (j + 1) * units] = pack_ref[0, j, :, units:]


def place_second(pack):
    owners, _, share, width = pack.shape
    return pl.pallas_call(
        place_second_kernel,
        grid=(owners,),
        in_specs=[pl.BlockSpec((1,) + pack.shape[1:], lambda i: (i, 0, 0, 0))],
        out_specs=[pl.BlockSpec((share, width), lambda i: (i, 0))] * 2,
        out_shape=[jax.ShapeDtypeStruct((owners * share, width), BF16)] * 2,
        compiler_params=params(),
        cost_estimate=brief,
        name="place_second",
    )(pack)


def place(kernel, where, one, two, widths, types):
    owners, _, share, _ = one.shape

    def spec(array, low, high):
        def index(i, where):
            bits = i ^ where[1]
            upper, lower, across = bits // 4, (bits // 2) % 2, bits % 2
            near, far = (across, upper) if low == "seq" else (upper, across)
            return (lower * 4 + far * 2 + near, 0, 0, 0)

        return pl.BlockSpec((1,) + array.shape[1:], index)

    return pl.pallas_call(
        kernel,
        grid_spec=pltpu.PrefetchScalarGridSpec(
            num_scalar_prefetch=1,
            grid=(owners,),
            in_specs=[spec(one, "seq", "dp"), spec(two, "dp", "seq")],
            out_specs=[pl.BlockSpec((share, width), lambda i, *_: (i, 0)) for width in widths],
        ),
        out_shape=[jax.ShapeDtypeStruct((owners * share, width), kind) for width, kind in zip(widths, types)],
        compiler_params=params(),
        cost_estimate=brief,
        name="place",
    )(where, one, two)


def front_kernel(
    which, x_ref, dy_ref, w_ref, wb_ref, dense_ref, gain_ref, shift_ref, cos_ref, low_ref, high_ref,
    q_ref, kv_ref, do_ref,
):
    half = q_ref.shape[1]
    xhat, _ = normalise(x_ref[0].astype(F32))
    normed = (xhat * gain_ref[...] + shift_ref[...]).astype(BF16)
    proj = dot(normed, w_ref[...], NN) + wb_ref[...]
    cosines, low, high = cos_ref[...], low_ref[...], high_ref[...]
    for j in range(half // LANES):
        at = slice(j * LANES, (j + 1) * LANES)
        query = turn(proj[:, at], cosines, low, high).astype(BF16)
        q_ref[:, at] = query * BF16(HD**-0.5)
        key = proj[:, half + j * LANES : half + (j + 1) * LANES]
        kv_ref[:, at] = turn(key, cosines, low, high).astype(BF16)
    kv_ref[:, half:] = proj[:, 2 * half :].astype(BF16)
    do_ref[...] = dot(dy_ref[0], dense_ref[...], NN).astype(BF16)


def front(which, x, dy, w, wb, dense, gain, shift, tables):
    _, rows, width = x.shape
    half = dense.shape[1]
    step = min(512, rows)
    chosen = pl.BlockSpec((1, step, width), lambda i, which: (which[0], i, 0))
    by_row = lambda cols: pl.BlockSpec((step, cols), lambda i, *_: (i, 0))
    return pl.pallas_call(
        front_kernel,
        grid_spec=pltpu.PrefetchScalarGridSpec(
            num_scalar_prefetch=1,
            grid=(rows // step,),
            in_specs=[chosen, chosen, whole(w.shape), whole(wb.shape), whole(dense.shape),
                      whole(gain.shape), whole(shift.shape)] + [by_row(LANES)] * 3,
            out_specs=[by_row(half), by_row(2 * half), by_row(half)],
        ),
        out_shape=[
            jax.ShapeDtypeStruct((rows, half), BF16),
            jax.ShapeDtypeStruct((rows, 2 * half), BF16),
            jax.ShapeDtypeStruct((rows, half), BF16),
        ],
        compiler_params=params(),
        cost_estimate=brief,
        name="front",
    )(which, x, dy, w, wb, dense, gain, shift, *tables)


def feed_kernel(
    which, x_ref, dy_ref, up_ref, upb_ref, down_ref, gain_ref, shift_ref, part_ref, dx_ref, act_ref, grad_ref
):
    xhat, _ = normalise(x_ref[0].astype(F32))
    normed = (xhat * gain_ref[...] + shift_ref[...]).astype(BF16)
    hidden = dot(normed, up_ref[...], NN) + upb_ref[...]
    share = 0.5 * (1.0 + lax.erf(hidden * F32(0.5**0.5)))
    act = (hidden * share).astype(BF16)
    act_ref[...] = act
    slope = share + hidden * (jnp.exp(hidden * hidden * -0.5) * F32(0.3989422804014327))
    part_ref[...] = dot(act, down_ref[...], NT).astype(part_ref.dtype)
    grad_low = (dot(dy_ref[0], down_ref[...], NN) * slope).astype(BF16)
    grad_ref[...] = grad_low
    dx_ref[...] = (dot(grad_low, up_ref[...], NT) * gain_ref[...]).astype(dx_ref.dtype)


def feed(which, x, dy, up, upb, down, gain, shift):
    _, rows, width = x.shape
    units = up.shape[1]
    step = min(256, rows)
    chosen = pl.BlockSpec((1, step, width), lambda i, which: (which[0], i, 0))
    by_row = lambda cols: pl.BlockSpec((step, cols), lambda i, *_: (i, 0))
    return pl.pallas_call(
        feed_kernel,
        grid_spec=pltpu.PrefetchScalarGridSpec(
            num_scalar_prefetch=1,
            grid=(rows // step,),
            in_specs=[chosen, chosen, whole(up.shape), whole(upb.shape), whole(down.shape),
                      whole(gain.shape), whole(shift.shape)],
            out_specs=[by_row(width), by_row(width), by_row(units), by_row(units)],
        ),
        out_shape=[
            jax.ShapeDtypeStruct((rows, width), BF16),
            jax.ShapeDtypeStruct((rows, width), BF16),
            jax.ShapeDtypeStruct((rows, units), BF16),
            jax.ShapeDtypeStruct((rows, units), BF16),
        ],
        compiler_params=params(),
        cost_estimate=brief,
        name="feed",
    )(which, x, dy, up, upb, down, gain, shift)


def feed_grads_kernel(
    which, x_ref, dy_ref, act_ref, grad_ref, up_ref, gain_col, shift_col, *refs
):
    both_ref, vec_ref, gupb_ref, up_acc, down_acc, sum_acc, dy_acc = refs[-7:]
    step = pl.program_id(0)

    @pl.when(step == 0)
    def _():
        up_acc[...] = jnp.zeros_like(up_acc)
        down_acc[...] = jnp.zeros_like(down_acc)
        sum_acc[...] = jnp.zeros_like(sum_acc)
        dy_acc[...] = jnp.zeros_like(dy_acc)

    xhat, _ = normalise(x_ref[0].astype(F32))
    dy, grad = dy_ref[0], grad_ref[...]
    up_acc[...] += dot(xhat.astype(BF16), grad, TN)
    down_acc[...] += dot(dy, act_ref[...], TN)
    sum_acc[...] += jnp.sum(grad.astype(F32), axis=0, keepdims=True)
    dy_acc[...] += jnp.sum(dy.astype(F32), axis=0, keepdims=True)

    @pl.when(step == pl.num_programs(0) - 1)
    def _():
        sums, raw = sum_acc[...], up_acc[...]
        up = up_ref[...].astype(F32)
        units = up.shape[1]
        both_ref[:, :units] = (raw * gain_col[...] + shift_col[...] * sums).astype(both_ref.dtype)
        both_ref[:, units:] = down_acc[...].astype(both_ref.dtype)
        gupb_ref[...] = sums
        lane = lax.broadcasted_iota(jnp.int32, vec_ref.shape, 1)
        gain_grad = jnp.sum(raw * up, axis=1, keepdims=True)
        shift_grad = jnp.sum(up * sums, axis=1, keepdims=True)
        dy_col = jnp.transpose(jnp.broadcast_to(dy_acc[...], (LANES, dy_acc.shape[1])))
        vec_ref[...] = jnp.where(
            lane == 0, dy_col * 0.5,
            jnp.where(lane == 3, gain_grad, jnp.where(lane == 4, shift_grad, 0.0)),
        )


def feed_grads(which, x, dy, act, grad, up, gain_col, shift_col, after=()):
    _, rows, width = x.shape
    units = up.shape[1]
    step = min(512, rows)
    chosen = pl.BlockSpec((1, step, width), lambda i, which: (which[0], i, 0))
    by_row = pl.BlockSpec((step, units), lambda i, *_: (i, 0))
    return pl.pallas_call(
        feed_grads_kernel,
        grid_spec=pltpu.PrefetchScalarGridSpec(
            num_scalar_prefetch=1,
            grid=(rows // step,),
            in_specs=[chosen, chosen, by_row, by_row, whole(up.shape),
                      whole(gain_col.shape), whole(shift_col.shape)] + [anywhere] * len(after),
            out_specs=[whole((width, 2 * units)), whole((width, LANES)), whole((1, units))],
            scratch_shapes=[pltpu.VMEM((width, units), F32), pltpu.VMEM((width, units), F32),
                            pltpu.VMEM((1, units), F32), pltpu.VMEM((1, width), F32)],
        ),
        out_shape=[
            jax.ShapeDtypeStruct((width, 2 * units), BF16),
            jax.ShapeDtypeStruct((width, LANES), F32),
            jax.ShapeDtypeStruct((1, units), F32),
        ],
        compiler_params=params(),
        cost_estimate=long,
        name="feed_grads",
    )(which, x, dy, act, grad, up, gain_col, shift_col, *after)


def lane_fold(values, combine):
    total = values[:, :LANES]
    for j in range(1, values.shape[1] // LANES):
        total = combine(total, values[:, j * LANES : (j + 1) * LANES])
    return total


def pick_heads(both, heads):
    return [jnp.where(mine, both, jnp.zeros_like(both)) for mine in heads]


def attend_kernel(info, slots, q_ref, g_ref, dense_ref, prior_ref, *refs, block, run_rows, parts, run, ties):
    k_parts, v_parts, refs = refs[:parts], refs[parts : 2 * parts], refs[2 * parts + ties :]
    o_ref, stat_ref, send_ref, keep_ref, k_ref, v_ref, score_ref, acc_ref, branch_ref = refs
    per_run = run_rows // block
    pair, place_in_run = pl.program_id(0), pl.program_id(1)
    full = info[run]

    @pl.when((pair == 0) & (place_in_run == 0))
    def _():
        branch_ref[...] = prior_ref[...].astype(F32)

    @pl.when(place_in_run == 0)
    def _():
        at = 0
        for j in range(parts):
            there = pl.ds(at, k_parts[j].shape[0])
            k_ref[there, :] = k_parts[j][...]
            v_ref[there, :] = v_parts[j][...]
            at += k_parts[j].shape[0]

    lane = lax.broadcasted_iota(jnp.int32, (block, LANES), 1)
    heads = (lane < HD, lane >= HD)

    def rows_of(at, count):
        return pl.ds(pl.multiple_of(slots[at] * run_rows, run_rows), count)

    def one_block(within):
        queries = pick_heads(q_ref[...], heads)
        seen = (within + 1) * block

        def score(at, tops, last):
            count = seen if last else run_rows
            keys = k_ref[rows_of(at, count), :]
            out = []
            for h in range(2):
                scores = dot(queries[h], keys, NT)
                if last:
                    row = lax.broadcasted_iota(jnp.int32, (block, count), 0)
                    col = lax.broadcasted_iota(jnp.int32, (block, count), 1)
                    scores = jnp.where(col <= row + within * block, scores, masked_value)
                score_ref[h, at, :, :count] = scores
                out.append(jnp.maximum(tops[h], lane_fold(scores, jnp.maximum)))
            return tuple(out)

        least = jnp.full((block, LANES), masked_value, F32)
        tops = lax.fori_loop(0, full, lambda at, carry: score(at, carry, False), (least, least))
        tops = score(full, tops, True)
        tops = [jnp.max(top, axis=1, keepdims=True) * F32(LOG2E) for top in tops]

        acc_ref[...] = jnp.zeros_like(acc_ref)

        def weigh(at, totals, last):
            count = seen if last else run_rows
            values = v_ref[rows_of(at, count), :]
            out = []
            for h in range(2):
                soft = jnp.exp2(score_ref[h, at, :, :count] * F32(LOG2E) - tops[h])
                out.append(totals[h] + lane_fold(soft, jnp.add))
                acc_ref[h] += dot(soft.astype(BF16), values, NN)
            return tuple(out)

        nought = jnp.zeros((block, LANES), F32)
        totals = lax.fori_loop(0, full, lambda at, carry: weigh(at, carry, False), (nought, nought))
        totals = weigh(full, totals, True)
        totals = [jnp.sum(total, axis=1, keepdims=True) for total in totals]
        attended = jnp.where(heads[0], acc_ref[0] / totals[0], acc_ref[1] / totals[1])
        o_ref[...] = attended.astype(o_ref.dtype)
        mine = pl.ds(within * block, block)
        branch_ref[mine, :] += dot(attended.astype(BF16), dense_ref[...], NT)
        product = attended * g_ref[...].astype(F32)
        row_terms = [jnp.sum(jnp.where(mine, product, 0.0), axis=1, keepdims=True) for mine in heads]
        logs = [tops[h] + jnp.log2(totals[h]) for h in range(2)]
        stats = jnp.where(lane == 0, logs[0], jnp.where(lane == 1, logs[1], 0.0))
        stats = jnp.where(lane == 2, row_terms[0], jnp.where(lane == 3, row_terms[1], stats))
        stat_ref[...] = jnp.transpose(stats)[:8]

    for within in range(per_run):
        pl.when(place_in_run == within)(functools.partial(one_block, within))

    @pl.when((pair == pl.num_programs(0) - 1) & (place_in_run == per_run - 1))
    def _():
        half = run_rows // 2
        send_ref[...] = branch_ref[pl.ds(pl.multiple_of((1 - info[2]) * half, half), half), :].astype(BF16)
        keep_ref[...] = branch_ref[pl.ds(pl.multiple_of(info[2] * half, half), half), :]


def attend(info, slots, q, g, kv_parts, dense, prior, run, after=()):
    rows, width = q.shape
    model = dense.shape[0]
    keys = sum(kv.shape[0] for kv in kv_parts)
    run_rows = rows // 2
    block = min(512, run_rows)
    per_run = run_rows // block
    pairs = width // LANES
    by_query = pl.BlockSpec((block, LANES), lambda p, i, *_: (run * per_run + i, p))
    by_key = [pl.BlockSpec((kv.shape[0], LANES), lambda p, i, *_: (0, p)) for kv in kv_parts]
    by_value = [pl.BlockSpec((kv.shape[0], LANES), lambda p, i, *_: (0, pairs + p)) for kv in kv_parts]
    kernel = functools.partial(
        attend_kernel, block=block, run_rows=run_rows, parts=len(kv_parts), run=run, ties=len(after)
    )
    return pl.pallas_call(
        kernel,
        grid_spec=pltpu.PrefetchScalarGridSpec(
            num_scalar_prefetch=2,
            grid=(pairs, per_run),
            in_specs=[
                by_query, by_query,
                pl.BlockSpec((model, LANES), lambda p, i, *_: (0, p)),
                pl.BlockSpec((run_rows, model), lambda p, i, *_: (run, 0)),
                *by_key, *by_value,
            ] + [anywhere] * len(after),
            out_specs=[
                pl.BlockSpec((block, LANES), lambda p, i, *_: (i, p)),
                pl.BlockSpec((8, block), lambda p, i, *_: (p, i)),
                whole((run_rows // 2, model)),
                whole((run_rows // 2, model)),
            ],
            scratch_shapes=[
                pltpu.VMEM((keys, LANES), BF16),
                pltpu.VMEM((keys, LANES), BF16),
                pltpu.VMEM((2, keys // run_rows, block, run_rows), F32),
                pltpu.VMEM((2, block, LANES), F32),
                pltpu.VMEM((run_rows, model), F32),
            ],
        ),
        out_shape=[
            jax.ShapeDtypeStruct((run_rows, width), BF16),
            jax.ShapeDtypeStruct((8 * pairs, run_rows), F32),
            jax.ShapeDtypeStruct((run_rows // 2, model), BF16),
            jax.ShapeDtypeStruct((run_rows // 2, model), F32),
        ],
        compiler_params=params(),
        cost_estimate=brief,
        name="attend",
    )(info, slots, q, g, dense, prior, *kv_parts, *kv_parts, *after)


def attend_back_kernel(info, slots, q_ref, g_ref, stat_ref, *refs, block, run_rows, parts, home, ties):
    k_parts, v_parts, refs = refs[:parts], refs[parts : 2 * parts], refs[2 * parts + ties :]
    dq_ref, dk_out, dv_out, refs = refs[0], refs[1], refs[2], refs[3:]
    if home:
        back_ref, refs = refs[0], refs[1:]
    k_ref, v_ref, dk_ref, dv_ref, acc_ref = refs
    per_run = run_rows // block
    step = pl.program_id(0)
    full = info[step // per_run]

    @pl.when(step == 0)
    def _():
        at = 0
        for j in range(parts):
            there = pl.ds(at, k_parts[j].shape[0])
            k_ref[there, :] = k_parts[j][...]
            v_ref[there, :] = v_parts[j][...]
            at += k_parts[j].shape[0]
        dk_ref[...] = jnp.zeros_like(dk_ref)
        dv_ref[...] = jnp.zeros_like(dv_ref)

    lane = lax.broadcasted_iota(jnp.int32, (block, LANES), 1)
    heads = (lane < HD, lane >= HD)

    def rows_of(at, count):
        return pl.ds(pl.multiple_of(slots[at] * run_rows, run_rows), count)

    def one_block(within):
        queries, grads = pick_heads(q_ref[...], heads), pick_heads(g_ref[...], heads)
        stats = jnp.transpose(stat_ref[...])
        logs, row_terms = [stats[:, h : h + 1] for h in range(2)], [stats[:, 2 + h : 3 + h] for h in range(2)]
        seen = (within + 1) * block
        acc_ref[...] = jnp.zeros_like(acc_ref)

        def back(at, last):
            count = seen if last else run_rows
            there = rows_of(at, count)
            keys, values = k_ref[there, :], v_ref[there, :]
            key_terms, value_terms = [], []
            for h in range(2):
                soft = jnp.exp2(dot(queries[h], keys, NT) * F32(LOG2E) - logs[h])
                if last:
                    row = lax.broadcasted_iota(jnp.int32, (block, count), 0)
                    col = lax.broadcasted_iota(jnp.int32, (block, count), 1)
                    soft = jnp.where(col <= row + within * block, soft, 0.0)
                grad_soft = dot(grads[h], values, NT)
                grad_score = (soft * (grad_soft - row_terms[h])).astype(BF16)
                acc_ref[h] += dot(grad_score, keys, NN)
                key_terms.append(dot(grad_score, queries[h], TN))
                value_terms.append(dot(soft.astype(BF16), grads[h], TN))
            dk_ref[there, :] += key_terms[0] + key_terms[1]
            dv_ref[there, :] += value_terms[0] + value_terms[1]

        def back_whole(at, carry):
            back(at, False)
            return carry

        lax.fori_loop(0, full, back_whole, 0)
        back(full, True)
        dq_ref[...] = (jnp.where(heads[0], acc_ref[0], acc_ref[1]) * F32(HD**-0.5)).astype(dq_ref.dtype)

    for within in range(per_run):
        pl.when(step % per_run == within)(functools.partial(one_block, within))

    @pl.when(step == pl.num_programs(0) - 1)
    def _():
        own = dk_out.shape[0]
        dk_out[...] = dk_ref[:own, :]
        dv_out[...] = dv_ref[:own, :]
        if home:
            back_ref[:, :LANES] = dk_ref[home:, :].astype(BF16)
            back_ref[:, LANES:] = dv_ref[home:, :].astype(BF16)


def attend_back(info, slots, q, g, stats, kv_parts, pair, home, after=()):
    rows, width = q.shape
    keys = sum(kv.shape[0] for kv in kv_parts)
    run_rows = rows // 2
    block = min(512, run_rows)
    pairs = width // LANES
    own = home or keys
    by_query = pl.BlockSpec((block, LANES), lambda i, *_: (i, pair))
    by_key = [pl.BlockSpec((kv.shape[0], LANES), lambda i, *_: (0, pair)) for kv in kv_parts]
    by_value = [pl.BlockSpec((kv.shape[0], LANES), lambda i, *_: (0, pairs + pair)) for kv in kv_parts]
    kernel = functools.partial(
        attend_back_kernel, block=block, run_rows=run_rows, parts=len(kv_parts), home=home, ties=len(after)
    )
    out_specs = [pl.BlockSpec((block, LANES), lambda i, *_: (i, 0)), whole((own, LANES)), whole((own, LANES))]
    out_shape = [
        jax.ShapeDtypeStruct((rows, LANES), BF16),
        jax.ShapeDtypeStruct((own, LANES), F32),
        jax.ShapeDtypeStruct((own, LANES), F32),
    ]
    if home:
        out_specs.append(whole((keys - home, 2 * LANES)))
        out_shape.append(jax.ShapeDtypeStruct((keys - home, 2 * LANES), BF16))
    return pl.pallas_call(
        kernel,
        grid_spec=pltpu.PrefetchScalarGridSpec(
            num_scalar_prefetch=2,
            grid=(rows // block,),
            in_specs=[by_query, by_query, pl.BlockSpec((8, block), lambda i, *_: (pair, i)), *by_key, *by_value]
            + [anywhere] * len(after),
            out_specs=out_specs,
            scratch_shapes=[
                pltpu.VMEM((keys, LANES), BF16),
                pltpu.VMEM((keys, LANES), BF16),
                pltpu.VMEM((keys, LANES), F32),
                pltpu.VMEM((keys, LANES), F32),
                pltpu.VMEM((2, block, LANES), F32),
            ],
        ),
        out_shape=out_shape,
        compiler_params=params(),
        cost_estimate=long,
        name="attend_back",
    )(info, slots, q, g, stats, *kv_parts, *kv_parts, *after)


def back_kernel(which, dq_ref, *refs, pairs):
    own_k, refs = refs[:pairs], refs[pairs:]
    own_v, refs = refs[:pairs], refs[pairs:]
    got, refs = refs[:pairs], refs[pairs:]
    w_ref, gain_ref, dx_in, cos_ref, low_ref, high_ref = refs[:6]
    dproj_ref, send_ref, keep_ref = refs[-3:]
    half = dq_ref.shape[1]
    cosines, low, high = cos_ref[...], low_ref[...], high_ref[...]
    for j in range(pairs):
        at = slice(j * LANES, (j + 1) * LANES)
        query = dq_ref[:, at].astype(F32)
        dproj_ref[:, at] = turn(query, cosines, -low, -high).astype(BF16)
        key = own_k[j][...] + got[j][:, :LANES].astype(F32)
        dproj_ref[:, half + j * LANES : half + (j + 1) * LANES] = turn(key, cosines, -low, -high).astype(BF16)
        value = own_v[j][...] + got[j][:, LANES:].astype(F32)
        dproj_ref[:, 2 * half + j * LANES : 2 * half + (j + 1) * LANES] = value.astype(BF16)
    summed = dot(dproj_ref[...], w_ref[...], NT) * gain_ref[...] + dx_in[...].astype(F32)
    mine = pl.program_id(0) % 2 == which[1]

    @pl.when(mine)
    def _():
        keep_ref[...] = summed

    @pl.when(jnp.logical_not(mine))
    def _():
        send_ref[...] = summed.astype(send_ref.dtype)


def back(which, dq, dk, dv, got, w, gain, dx_part, tables, after=()):
    rows, half = dq.shape
    width = w.shape[0]
    step = rows // 4
    pairs = len(dk)
    by_row = lambda cols: pl.BlockSpec((step, cols), lambda i, *_: (i, 0))
    by_run = pl.BlockSpec((step, width), lambda i, *_: (i // 2, 0))
    return pl.pallas_call(
        functools.partial(back_kernel, pairs=pairs),
        grid_spec=pltpu.PrefetchScalarGridSpec(
            num_scalar_prefetch=1,
            grid=(4,),
            in_specs=[by_row(half)] + [by_row(LANES)] * (2 * pairs) + [by_row(2 * LANES)] * pairs
            + [whole(w.shape), whole(gain.shape), by_row(width)] + [by_row(LANES)] * 3
            + [anywhere] * len(after),
            out_specs=[by_row(3 * half), by_run, by_run],
        ),
        out_shape=[
            jax.ShapeDtypeStruct((rows, 3 * half), BF16),
            jax.ShapeDtypeStruct((rows // 2, width), BF16),
            jax.ShapeDtypeStruct((rows // 2, width), F32),
        ],
        compiler_params=params(),
        cost_estimate=brief,
        name="back",
    )(which, dq, *dk, *dv, *got, w, gain, dx_part, *tables, *after)


def weight_kernel(
    which, x_ref, dy_ref, dproj_ref, o_ref, w_ref, gain_col, shift_col, *refs
):
    gqkv_ref, gdense_ref, vec_ref, gb_ref, acc, dense_acc, sum_acc = refs[-7:]
    step = pl.program_id(0)

    @pl.when(step == 0)
    def _():
        acc[...] = jnp.zeros_like(acc)
        dense_acc[...] = jnp.zeros_like(dense_acc)
        sum_acc[...] = jnp.zeros_like(sum_acc)

    xhat, _ = normalise(x_ref[0].astype(F32))
    dproj = dproj_ref[...]
    acc[...] += dot(xhat.astype(BF16), dproj, TN)
    dense_acc[...] += dot(dy_ref[0], o_ref[...], TN)
    sum_acc[...] += jnp.sum(dproj.astype(F32), axis=0, keepdims=True)

    @pl.when(step == pl.num_programs(0) - 1)
    def _():
        sums, raw, w = sum_acc[...], acc[...], w_ref[...].astype(F32)
        gqkv_ref[...] = (raw * gain_col[...] + shift_col[...] * sums).astype(gqkv_ref.dtype)
        gdense_ref[...] = dense_acc[...].astype(gdense_ref.dtype)
        gb_ref[...] = sums
        lane = lax.broadcasted_iota(jnp.int32, vec_ref.shape, 1)
        gain_grad = jnp.sum(raw * w, axis=1, keepdims=True)
        shift_grad = jnp.sum(w * sums, axis=1, keepdims=True)
        vec_ref[...] = jnp.where(lane == 1, gain_grad, jnp.where(lane == 2, shift_grad, 0.0))


def weight_grads(which, x, dy, dproj, o, w, gain_col, shift_col, after=()):
    _, rows, width = x.shape
    half = o.shape[1]
    step = min(512, rows)
    chosen = pl.BlockSpec((1, step, width), lambda i, which: (which[0], i, 0))
    by_row = lambda cols: pl.BlockSpec((step, cols), lambda i, *_: (i, 0))
    return pl.pallas_call(
        weight_kernel,
        grid_spec=pltpu.PrefetchScalarGridSpec(
            num_scalar_prefetch=1,
            grid=(rows // step,),
            in_specs=[chosen, chosen, by_row(3 * half), by_row(half), whole(w.shape),
                      whole(gain_col.shape), whole(shift_col.shape)] + [anywhere] * len(after),
            out_specs=[whole((width, 3 * half)), whole((width, half)), whole((width, LANES)), whole((1, 3 * half))],
            scratch_shapes=[pltpu.VMEM((width, 3 * half), F32), pltpu.VMEM((width, half), F32),
                            pltpu.VMEM((1, 3 * half), F32)],
        ),
        out_shape=[
            jax.ShapeDtypeStruct((width, 3 * half), BF16),
            jax.ShapeDtypeStruct((width, half), BF16),
            jax.ShapeDtypeStruct((width, LANES), F32),
            jax.ShapeDtypeStruct((1, 3 * half), F32),
        ],
        compiler_params=params(),
        cost_estimate=long,
        name="weight_grads",
    )(which, x, dy, dproj, o, w, gain_col, shift_col, *after)


def norm_back_kernel(which, x_ref, dy_ref, kept_ref, got_ref, *refs):
    out_ref = refs[-1]
    xhat, scale = normalise(x_ref[0].astype(F32))
    grad = kept_ref[...].astype(F32) + got_ref[...].astype(F32)
    centre = jnp.mean(grad, axis=-1, keepdims=True)
    along = jnp.mean(grad * xhat, axis=-1, keepdims=True)
    out_ref[...] = (dy_ref[0].astype(F32) + scale * (grad - centre - xhat * along)).astype(out_ref.dtype)


def norm_back(which, x, dy, kept, got, run, after=()):
    rows, width = got.shape
    step = min(256, rows)
    blocks = rows // step
    chosen = pl.BlockSpec(
        (1, step, width), lambda i, which: (which[0], (2 * run + which[1]) * blocks + i, 0)
    )
    return pl.pallas_call(
        norm_back_kernel,
        grid_spec=pltpu.PrefetchScalarGridSpec(
            num_scalar_prefetch=1,
            grid=(blocks,),
            in_specs=[chosen, chosen,
                      pl.BlockSpec((step, width), lambda i, *_: (run * blocks + i, 0)),
                      pl.BlockSpec((step, width), lambda i, *_: (i, 0))] + [anywhere] * len(after),
            out_specs=pl.BlockSpec((step, width), lambda i, *_: (i, 0)),
        ),
        out_shape=jax.ShapeDtypeStruct((rows, width), BF16),
        compiler_params=params(),
        cost_estimate=longest,
        name="norm_back",
    )(which, x, dy, kept, got, *after)


def finish_kernel(which, x_ref, kept_ref, got_ref, one_ref, two_ref, *refs):
    summed = kept_ref[...] + got_ref[...].astype(F32) + x_ref[0].astype(F32) + one_ref[...] + two_ref[...]
    refs[-1][...] = summed.astype(BF16)


def finish(which, x, kept, got, one, two, run, after=()):
    rows, width = got.shape
    step = min(256, rows)
    blocks = rows // step
    by_row = pl.BlockSpec((step, width), lambda i, *_: (i, 0))
    return pl.pallas_call(
        finish_kernel,
        grid_spec=pltpu.PrefetchScalarGridSpec(
            num_scalar_prefetch=1,
            grid=(blocks,),
            in_specs=[
                pl.BlockSpec((1, step, width), lambda i, which: (which[0], (2 * run + which[1]) * blocks + i, 0)),
                by_row, by_row, whole(one.shape), whole(two.shape),
            ] + [anywhere] * len(after),
            out_specs=by_row,
        ),
        out_shape=jax.ShapeDtypeStruct((rows, width), BF16),
        compiler_params=params(),
        cost_estimate=brief,
        name="finish",
    )(which, x, kept, got, one, two, *after)


def lay_kernel(early_ref, late_ref, *refs):
    out = refs[-1]
    run = pl.program_id(0) % 2

    @pl.when(run == 0)
    def _():
        out[0] = early_ref[...]

    @pl.when(run == 1)
    def _():
        out[0] = late_ref[...]


def lay_gathered(early, late, after=()):
    rows, width = early.shape[0] // 2, early.shape[1]
    half = pl.BlockSpec((rows, width), lambda i: (i // 2, 0))
    return pl.pallas_call(
        lay_kernel,
        grid=(4,),
        in_specs=[half, half] + [anywhere] * len(after),
        out_specs=pl.BlockSpec((1, rows, width), lambda i: (i // 2, i % 2, 0)),
        out_shape=jax.ShapeDtypeStruct((2, 2 * rows, width), BF16),
        compiler_params=params(),
        cost_estimate=brief,
        name="lay_gathered",
    )(early, late, *after)


def lay_round_kernel(index, *refs):
    out = refs[-1]
    run, slot = pl.program_id(0) // 4, pl.program_id(0) % 4
    back = (index[0] + 4 - slot) % 4
    for j in range(8):

        @pl.when((run == j // 4) & (back == j % 4))
        def _(j=j):
            out[0] = refs[j][...]


def lay_round(index, early, late):
    half, width = early[0].shape
    return pl.pallas_call(
        lay_round_kernel,
        grid_spec=pltpu.PrefetchScalarGridSpec(
            num_scalar_prefetch=1,
            grid=(8,),
            in_specs=[whole((half, width))] * 8,
            out_specs=pl.BlockSpec((1, half, width), lambda i, *_: ((i % 4) // 2, 2 * (i // 4) + i % 2, 0)),
        ),
        out_shape=jax.ShapeDtypeStruct((2, 4 * half, width), BF16),
        compiler_params=params(),
        cost_estimate=brief,
        name="lay_round",
    )(index[None], *early, *late)


def swap(values, axis):
    return lax.ppermute(values, axis, [(0, 1), (1, 0)])


def across(values, bit):
    return lax.ppermute(values, "dp", [(i, i ^ bit) for i in range(4)])


def gather_half(values, seq_first):
    values = jnp.concatenate([values[None], swap(values, "mh")[None]], axis=0)
    steps = [lambda v: swap(v, "seq"), lambda v: across(v, 2)]
    for step in steps if seq_first else steps[::-1]:
        values = jnp.concatenate([values, step(values)], axis=0)
    values = jnp.concatenate([values, across(values, 1)], axis=0)
    return values.reshape(8, 2, *values.shape[1:])


def round_mp(mine):
    axes = ("mh", "ml")
    return [mine] + [lax.ppermute(mine, axes, [(i, (i + k) % 4) for i in range(4)]) for k in (1, 2, 3)]


def rotation_tables(positions):
    half = ROT // 2
    frequency = jnp.power(F32(10000.0), -2.0 * jnp.arange(half, dtype=F32) / ROT)
    angles = frequency[:, None] * positions.astype(F32)[None, :]
    cosines, sines = lax.optimization_barrier((jnp.cos(angles), jnp.sin(angles)))
    cosines, sines = cosines.T, sines.T
    rows = positions.shape[0]
    rest = jnp.zeros((rows, HD - ROT), F32)
    blank = jnp.zeros((rows, half), F32)
    per_head = (
        jnp.concatenate([cosines, cosines, rest + 1.0], axis=1),
        jnp.concatenate([-sines, blank, rest], axis=1),
        jnp.concatenate([blank, sines, rest], axis=1),
    )
    return tuple(jnp.tile(table, (1, LANES // HD)) for table in per_head)


def body(
    tokens, places, w_qkv, b_qkv, w_dense, b_dense, w_up, b_up, w_down, b_down,
    norm1_gain, norm1_bias, norm2_gain, norm2_bias, out_grad, *, seq_size, owners,
):
    _, rows, width = tokens.shape
    share = width // owners
    heads = b_qkv.shape[1]
    cols = heads * HD
    units = w_up.shape[1]
    side, part = lax.axis_index("mh"), lax.axis_index("ml")
    index = (2 * side + part).astype(jnp.int32)
    owner = lax.axis_index("dp") * seq_size + lax.axis_index("seq")
    which = jnp.stack([side, part]).astype(jnp.int32)
    where = jnp.stack([side, owner]).astype(jnp.int32)

    def column(vector):
        vector = vector.reshape(-1)
        return jnp.pad(vector, (0, share - vector.shape[0]))[:, None]

    small = jnp.concatenate(
        [column(v) for v in (b_dense, b_down, norm1_gain, norm1_bias, norm2_gain, norm2_bias, b_qkv, b_up)],
        axis=1,
    )
    small = jnp.pad(small, ((0, 0), (0, LANES - small.shape[1])))
    one = w_qkv[:2].transpose(1, 0, 2).reshape(share, 2 * cols)
    two = jnp.concatenate([w_qkv[2], w_dense.T, small], axis=1)
    three, four = w_up, w_down.T
    first_widths = (6 * cols, 2 * cols, 2 * LANES)
    if owners == 8 and seq_size == 2:
        one, two = gather_half(one, True), gather_half(two, False)
        qkv_w, dense_w, small = place(place_first_kernel, where, one, two, first_widths, (BF16, BF16, F32))
        pack = lax.all_gather(jnp.concatenate([three, four], axis=1), ("dp", "seq", "mh"), axis=0, tiled=True)
        up_w, down_w = place_second(pack.reshape(owners, 2, share, 2 * units))
    else:

        def gather(values):
            values = lax.all_gather(values, ("dp", "seq", "mh"), axis=0, tiled=True)
            return values.reshape(owners, 2, share, -1).transpose(0, 2, 1, 3).reshape(width, 2, -1)

        one, two, three, four = gather(one), gather(two), gather(three), gather(four)
        qkv_w = jnp.concatenate([one[:, :, :cols], one[:, :, cols:], two[:, :, :cols]], axis=1)
        qkv_w, dense_w = qkv_w.reshape(width, 6 * cols), two[:, :, cols : 2 * cols].reshape(width, 2 * cols)
        small = two[:, :, 2 * cols :].reshape(width, 2 * LANES).astype(F32)
        up_w, down_w = three.reshape(width, 2 * units), four.reshape(width, 2 * units)
    vectors = small[:, :8]
    piece = HD // owners
    biases = small.reshape(owners, share, 2, LANES)
    qkv_b = biases[:, : 3 * heads * piece, :, 6].reshape(owners, 3, heads, piece, 2)
    qkv_b = qkv_b.transpose(1, 4, 2, 0, 3).reshape(1, 6 * cols)
    up_rows, up_cols = b_up.shape
    up_b = biases[..., 7].reshape(owners, up_rows, up_cols, 2).transpose(3, 1, 0, 2).reshape(1, 2 * units)
    by_row = vectors.T
    row_of = lambda at: by_row[at].reshape(1, width)
    column_of = lambda at: vectors[:, at].reshape(width, 1)

    my_places = lax.dynamic_index_in_dim(places, side, 0, keepdims=False)
    run_rows = rows // 2
    runs = jnp.stack([my_places[0], my_places[run_rows]]) // run_rows
    if seq_size == 2:
        all_runs = jnp.concatenate([runs, swap(runs, "seq")])
    else:
        all_runs = lax.all_gather(runs, "seq", axis=0, tiled=True)
    order = jnp.arange(2 * seq_size, dtype=jnp.int32)
    slots = jnp.sum(jnp.where(all_runs[None, :] == order[:, None], order[None, :], 0), axis=1)
    tables = rotation_tables(my_places)

    q, kv, grad_o = front(which, tokens, out_grad, qkv_w, qkv_b, dense_w, row_of(2), row_of(3), tables)
    if seq_size == 2:
        kv_parts = (kv, swap(kv, "seq"))
    else:
        kv_parts = (lax.all_gather(kv, "seq", axis=0, tiled=True),)

    mlp_part, mlp_dx, act, mlp_grad = feed(which, tokens, out_grad, up_w, up_b, down_w, row_of(4), row_of(5))
    info = jnp.concatenate([runs, which[1:]])
    quarter = rows // 4

    o_early, stat_early, send, keep_early = attend(info, slots, q, grad_o, kv_parts, dense_w, mlp_part, 0)
    got_early = swap(send, "ml")
    o_late, stat_late, send, keep_late = attend(
        info, slots, q, grad_o, kv_parts, dense_w, mlp_part, 1, (o_early,)
    )
    got_late = swap(send, "ml")
    stats = jnp.concatenate([stat_early, stat_late], axis=1)
    mixed_early = finish(which, tokens, keep_early, got_early, row_of(0), row_of(1), 0, (o_late,))
    after = (mixed_early,)
    mixed_early = lax.all_gather(mixed_early, ("mh", "ml"), axis=0, tiled=True)

    home = rows if seq_size == 2 else 0
    dq, dk, dv, got = [], [], [], []
    for pair in range(q.shape[1] // LANES):
        outs = attend_back(info, slots, q, grad_o, stats, kv_parts, pair, home, after)
        after = (outs[0],)
        dq.append(outs[0])
        if home:
            dk.append(outs[1])
            dv.append(outs[2])
            got.append(swap(outs[3], "seq"))
        else:
            both = jnp.concatenate([outs[1], outs[2]], axis=1).astype(BF16)
            got.append(lax.psum_scatter(both, "seq", scatter_dimension=0, tiled=True))
            dk.append(jnp.zeros((rows, LANES), F32))
            dv.append(jnp.zeros((rows, LANES), F32))
        if pair == 0:
            mixed_late = finish(which, tokens, keep_late, got_late, row_of(0), row_of(1), 1, after)
            after = (outs[0], mixed_late)
            mixed_late = lax.all_gather(mixed_late, ("mh", "ml"), axis=0, tiled=True)
        elif pair > 0:
            after = (outs[0], got[pair - 1])
    feed_weights, mlp_vectors, grad_up_b = feed_grads(
        which, tokens, out_grad, act, mlp_grad, up_w, column_of(4), column_of(5), after + (mixed_early,)
    )
    dq = jnp.concatenate(dq, axis=1)
    dproj, send, keep = back(
        which, dq, dk, dv, got, qkv_w, row_of(2), mlp_dx, tables, (grad_up_b,)
    )
    mixed = lay_gathered(mixed_early, mixed_late, (dproj,))
    got = [swap(send[run * quarter : (run + 1) * quarter], "ml") for run in range(2)]
    attended = jnp.concatenate([o_early, o_late], axis=0)
    grad_qkv, grad_dense, qkv_vectors, grad_qkv_b = weight_grads(
        which, tokens, out_grad, dproj, attended, qkv_w, column_of(2), column_of(3), (mixed_late,)
    )
    ties = ((grad_qkv_b,), ())
    input_grad = [
        round_mp(norm_back(which, tokens, out_grad, keep, got[run], run, ties[run])) for run in range(2)
    ]
    input_grad = lay_round(index, *input_grad)

    def scatter(grads):
        return lax.psum_scatter(grads, ("dp", "seq"), scatter_dimension=0, tiled=True)

    def settle(sums):
        sums = sums.astype(F32)
        mine = lax.dynamic_index_in_dim(sums, side, 1, keepdims=False)
        other = lax.dynamic_index_in_dim(sums, 1 - side, 1, keepdims=False)
        return mine + swap(other.astype(BF16), "mh").astype(F32)

    vector_grads = (mlp_vectors + qkv_vectors)[:, None, :5]
    vector_grads = jnp.broadcast_to(vector_grads, (width, 2, 5))
    bias_qkv = grad_qkv_b.reshape(3, 2, heads, owners, piece).transpose(3, 0, 2, 4, 1)
    bias_qkv = bias_qkv.reshape(owners, 3 * heads * piece, 2)
    bias_qkv = jnp.pad(bias_qkv, ((0, 0), (0, share - 3 * heads * piece), (0, 0))).reshape(width, 2, 1)
    bias_up = grad_up_b.reshape(2, up_rows, owners, up_cols).transpose(2, 1, 3, 0).reshape(width, 2, 1)
    tail = jnp.concatenate([vector_grads, bias_qkv, bias_up], axis=2)
    tail = jnp.pad(tail, ((0, 0), (0, 0), (0, LANES // 2 - 7))).astype(BF16).reshape(width, LANES)
    packed = scatter(jnp.concatenate([grad_qkv, grad_dense, tail, feed_weights], axis=1))
    first, owned_feed = packed[:, : 8 * cols + LANES], packed[:, 8 * cols + LANES :]
    owned_feed = owned_feed.reshape(share, 2, 2, units).transpose(0, 2, 1, 3).reshape(share, 2, 2 * units)
    owned_qkv = first[:, : 6 * cols].reshape(share, 3, 2, cols).transpose(0, 2, 1, 3).reshape(share, 2, 3 * cols)
    owned_dense = first[:, 6 * cols : 8 * cols].reshape(share, 2, cols)
    owned_tail = first[:, 8 * cols :].reshape(share, 2, LANES // 2)
    owned = settle(jnp.concatenate([owned_feed, owned_qkv, owned_dense, owned_tail], axis=2))
    owned_feed, owned = owned[:, : 2 * units], owned[:, 2 * units :]
    vectors = owned[:, 4 * cols :]
    norms = vectors[:, :5]
    norms = norms + swap(norms, "ml")
    bias_grad = norms[:, 0]
    return (
        mixed,
        input_grad,
        owned[:, : 3 * cols].reshape(share, 3, cols).transpose(1, 0, 2),
        vectors[: 3 * heads * piece, 5].reshape(b_qkv.shape),
        owned[:, 3 * cols : 4 * cols].T,
        bias_grad,
        owned_feed[:, :units],
        vectors[:, 6].reshape(b_up.shape),
        owned_feed[:, units:].T,
        bias_grad,
        norms[:, 1],
        norms[:, 2],
        norms[:, 3],
        norms[:, 4],
    )


def solution(mesh):
    dp, seq, mp = (mesh.shape[axis] for axis in ("dp", "seq", "mp"))
    split = Mesh(mesh.devices.reshape(dp, seq, 2, mp // 2), ("dp", "seq", "mh", "ml"))
    mp, owner = ("mh", "ml"), ("dp", "seq")
    row = P("dp", "seq", None)
    vector = P(owner)
    weights = (
        P(None, owner, mp), P(None, mp, owner), P(mp, owner), vector, P(owner, mp), P(mp, owner),
        P(mp, owner), vector, vector, vector, vector, vector,
    )
    return jax.shard_map(
        functools.partial(body, seq_size=seq, owners=dp * seq),
        mesh=split,
        in_specs=(row, P("dp", "seq")) + weights + (row,),
        out_specs=(row, row) + weights,
        check_vma=False,
    )
```

```python
import functools

import jax
import jax.numpy as jnp
from jax import lax
from jax.experimental import pallas as pl
from jax.experimental.pallas import tpu as pltpu
from jax.sharding import Mesh
from jax.sharding import PartitionSpec as P

HD = 64
ROT = 16
LANES = 128
F32 = jnp.float32
BF16 = jnp.bfloat16
LOG2E = 1.4426950408889634
norm_eps = 1e-05
masked_value = -1e30
vmem_bytes = 60 * 2**20
brief = pl.CostEstimate(flops=1, bytes_accessed=1, transcendentals=0)
long = pl.CostEstimate(flops=2**33, bytes_accessed=2**24, transcendentals=0)

NN = (((1,), (0,)), ((), ()))
NT = (((1,), (1,)), ((), ()))
TN = (((0,), (0,)), ((), ()))


def dot(left, right, dims):
    return lax.dot_general(left, right, dims, preferred_element_type=F32)


def normalise(rows):
    centre = jnp.mean(rows, axis=-1, keepdims=True)
    deviate = rows - centre
    spread = jnp.mean(deviate * deviate, axis=-1, keepdims=True)
    scale = lax.rsqrt(spread + norm_eps)
    return deviate * scale, scale


def turn(chunk, cosines, sine_low, sine_high):
    half = ROT // 2
    return (
        chunk * cosines
        + pltpu.roll(chunk, LANES - half, 1) * sine_low
        + pltpu.roll(chunk, half, 1) * sine_high
    )

longest = pl.CostEstimate(flops=2**36, bytes_accessed=2**27, transcendentals=0)


anywhere = pl.BlockSpec(memory_space=pl.ANY)


def whole(shape):
    return pl.BlockSpec(shape, lambda *_: (0,) * len(shape))


def params(**kwargs):
    return pltpu.CompilerParams(vmem_limit_bytes=vmem_bytes, **kwargs)


def place_first_kernel(where, one_ref, two_ref, qkv_ref, dense_ref, small_ref):
    cols = one_ref.shape[-1] // 2
    near = where[0] == 0
    one = [one_ref[0, j] for j in range(2)]
    two = [two_ref[0, j] for j in range(2)]
    one = (jnp.where(near, one[0], one[1]), jnp.where(near, one[1], one[0]))
    two = (jnp.where(near, two[0], two[1]), jnp.where(near, two[1], two[0]))
    pieces = [one[j][:, i * cols : (i + 1) * cols] for i in range(2) for j in range(2)]
    pieces += [two[j][:, :cols] for j in range(2)]
    qkv_ref[...] = jnp.concatenate(pieces, axis=1)
    dense_ref[...] = jnp.concatenate([two[j][:, cols : 2 * cols] for j in range(2)], axis=1)
    small_ref[...] = jnp.concatenate([two[j][:, 2 * cols :] for j in range(2)], axis=1).astype(F32)


def place_second_kernel(pack_ref, up_ref, down_ref):
    units = pack_ref.shape[-1] // 2
    for j in range(2):
        up_ref[:, j * units : (j + 1) * units] = pack_ref[0, j, :, :units]
        down_ref[:, j * units : (j + 1) * units] = pack_ref[0, j, :, units:]


def place_second(pack):
    owners, _, share, width = pack.shape
    return pl.pallas_call(
        place_second_kernel,
        grid=(owners,),
        in_specs=[pl.BlockSpec((1,) + pack.shape[1:], lambda i: (i, 0, 0, 0))],
        out_specs=[pl.BlockSpec((share, width), lambda i: (i, 0))] * 2,
        out_shape=[jax.ShapeDtypeStruct((owners * share, width), BF16)] * 2,
        compiler_params=params(),
        cost_estimate=brief,
        name="place_second",
    )(pack)


def place(kernel, where, one, two, widths, types):
    owners, _, share, _ = one.shape

    def spec(array, low, high):
        def index(i, where):
            bits = i ^ where[1]
            upper, lower, across = bits // 4, (bits // 2) % 2, bits % 2
            near, far = (across, upper) if low == "seq" else (upper, across)
            return (lower * 4 + far * 2 + near, 0, 0, 0)

        return pl.BlockSpec((1,) + array.shape[1:], index)

    return pl.pallas_call(
        kernel,
        grid_spec=pltpu.PrefetchScalarGridSpec(
            num_scalar_prefetch=1,
            grid=(owners,),
            in_specs=[spec(one, "seq", "dp"), spec(two, "dp", "seq")],
            out_specs=[pl.BlockSpec((share, width), lambda i, *_: (i, 0)) for width in widths],
        ),
        out_shape=[jax.ShapeDtypeStruct((owners * share, width), kind) for width, kind in zip(widths, types)],
        compiler_params=params(),
        cost_estimate=brief,
        name="place",
    )(where, one, two)


def front_kernel(
    which, x_ref, dy_ref, w_ref, wb_ref, dense_ref, gain_ref, shift_ref, cos_ref, low_ref, high_ref,
    q_ref, kv_ref, do_ref,
):
    half = q_ref.shape[1]
    xhat, _ = normalise(x_ref[0].astype(F32))
    normed = (xhat * gain_ref[...] + shift_ref[...]).astype(BF16)
    proj = dot(normed, w_ref[...], NN) + wb_ref[...]
    cosines, low, high = cos_ref[...], low_ref[...], high_ref[...]
    for j in range(half // LANES):
        at = slice(j * LANES, (j + 1) * LANES)
        query = turn(proj[:, at], cosines, low, high).astype(BF16)
        q_ref[:, at] = query * BF16(HD**-0.5)
        key = proj[:, half + j * LANES : half + (j + 1) * LANES]
        kv_ref[:, at] = turn(key, cosines, low, high).astype(BF16)
    kv_ref[:, half:] = proj[:, 2 * half :].astype(BF16)
    do_ref[...] = dot(dy_ref[0], dense_ref[...], NN).astype(BF16)


def front(which, x, dy, w, wb, dense, gain, shift, tables):
    _, rows, width = x.shape
    half = dense.shape[1]
    step = min(512, rows)
    chosen = pl.BlockSpec((1, step, width), lambda i, which: (which[0], i, 0))
    by_row = lambda cols: pl.BlockSpec((step, cols), lambda i, *_: (i, 0))
    return pl.pallas_call(
        front_kernel,
        grid_spec=pltpu.PrefetchScalarGridSpec(
            num_scalar_prefetch=1,
            grid=(rows // step,),
            in_specs=[chosen, chosen, whole(w.shape), whole(wb.shape), whole(dense.shape),
                      whole(gain.shape), whole(shift.shape)] + [by_row(LANES)] * 3,
            out_specs=[by_row(half), by_row(2 * half), by_row(half)],
        ),
        out_shape=[
            jax.ShapeDtypeStruct((rows, half), BF16),
            jax.ShapeDtypeStruct((rows, 2 * half), BF16),
            jax.ShapeDtypeStruct((rows, half), BF16),
        ],
        compiler_params=params(),
        cost_estimate=brief,
        name="front",
    )(which, x, dy, w, wb, dense, gain, shift, *tables)


def feed_kernel(
    which, x_ref, dy_ref, up_ref, upb_ref, down_ref, gain_ref, shift_ref, part_ref, dx_ref, act_ref, grad_ref
):
    xhat, _ = normalise(x_ref[0].astype(F32))
    normed = (xhat * gain_ref[...] + shift_ref[...]).astype(BF16)
    hidden = dot(normed, up_ref[...], NN) + upb_ref[...]
    share = 0.5 * (1.0 + lax.erf(hidden * F32(0.5**0.5)))
    act = (hidden * share).astype(BF16)
    act_ref[...] = act
    slope = share + hidden * (jnp.exp(hidden * hidden * -0.5) * F32(0.3989422804014327))
    part_ref[...] = dot(act, down_ref[...], NT).astype(part_ref.dtype)
    grad_low = (dot(dy_ref[0], down_ref[...], NN) * slope).astype(BF16)
    grad_ref[...] = grad_low
    dx_ref[...] = (dot(grad_low, up_ref[...], NT) * gain_ref[...]).astype(dx_ref.dtype)


def feed(which, x, dy, up, upb, down, gain, shift):
    _, rows, width = x.shape
    units = up.shape[1]
    step = min(256, rows)
    chosen = pl.BlockSpec((1, step, width), lambda i, which: (which[0], i, 0))
    by_row = lambda cols: pl.BlockSpec((step, cols), lambda i, *_: (i, 0))
    return pl.pallas_call(
        feed_kernel,
        grid_spec=pltpu.PrefetchScalarGridSpec(
            num_scalar_prefetch=1,
            grid=(rows // step,),
            in_specs=[chosen, chosen, whole(up.shape), whole(upb.shape), whole(down.shape),
                      whole(gain.shape), whole(shift.shape)],
            out_specs=[by_row(width), by_row(width), by_row(units), by_row(units)],
        ),
        out_shape=[
            jax.ShapeDtypeStruct((rows, width), BF16),
            jax.ShapeDtypeStruct((rows, width), BF16),
            jax.ShapeDtypeStruct((rows, units), BF16),
            jax.ShapeDtypeStruct((rows, units), BF16),
        ],
        compiler_params=params(),
        cost_estimate=brief,
        name="feed",
    )(which, x, dy, up, upb, down, gain, shift)


def feed_grads_kernel(
    which, x_ref, dy_ref, act_ref, grad_ref, up_ref, gain_col, shift_col, *refs
):
    both_ref, vec_ref, gupb_ref, up_acc, down_acc, sum_acc, dy_acc = refs[-7:]
    step = pl.program_id(0)

    @pl.when(step == 0)
    def _():
        up_acc[...] = jnp.zeros_like(up_acc)
        down_acc[...] = jnp.zeros_like(down_acc)
        sum_acc[...] = jnp.zeros_like(sum_acc)
        dy_acc[...] = jnp.zeros_like(dy_acc)

    xhat, _ = normalise(x_ref[0].astype(F32))
    dy, grad = dy_ref[0], grad_ref[...]
    up_acc[...] += dot(xhat.astype(BF16), grad, TN)
    down_acc[...] += dot(dy, act_ref[...], TN)
    sum_acc[...] += jnp.sum(grad.astype(F32), axis=0, keepdims=True)
    dy_acc[...] += jnp.sum(dy.astype(F32), axis=0, keepdims=True)

    @pl.when(step == pl.num_programs(0) - 1)
    def _():
        sums, raw = sum_acc[...], up_acc[...]
        up = up_ref[...].astype(F32)
        units = up.shape[1]
        both_ref[:, :units] = (raw * gain_col[...] + shift_col[...] * sums).astype(both_ref.dtype)
        both_ref[:, units:] = down_acc[...].astype(both_ref.dtype)
        gupb_ref[...] = sums
        lane = lax.broadcasted_iota(jnp.int32, vec_ref.shape, 1)
        gain_grad = jnp.sum(raw * up, axis=1, keepdims=True)
        shift_grad = jnp.sum(up * sums, axis=1, keepdims=True)
        dy_col = jnp.transpose(jnp.broadcast_to(dy_acc[...], (LANES, dy_acc.shape[1])))
        vec_ref[...] = jnp.where(
            lane == 0, dy_col * 0.5,
            jnp.where(lane == 3, gain_grad, jnp.where(lane == 4, shift_grad, 0.0)),
        )


def feed_grads(which, x, dy, act, grad, up, gain_col, shift_col, after=()):
    _, rows, width = x.shape
    units = up.shape[1]
    step = min(512, rows)
    chosen = pl.BlockSpec((1, step, width), lambda i, which: (which[0], i, 0))
    by_row = pl.BlockSpec((step, units), lambda i, *_: (i, 0))
    return pl.pallas_call(
        feed_grads_kernel,
        grid_spec=pltpu.PrefetchScalarGridSpec(
            num_scalar_prefetch=1,
            grid=(rows // step,),
            in_specs=[chosen, chosen, by_row, by_row, whole(up.shape),
                      whole(gain_col.shape), whole(shift_col.shape)] + [anywhere] * len(after),
            out_specs=[whole((width, 2 * units)), whole((width, LANES)), whole((1, units))],
            scratch_shapes=[pltpu.VMEM((width, units), F32), pltpu.VMEM((width, units), F32),
                            pltpu.VMEM((1, units), F32), pltpu.VMEM((1, width), F32)],
        ),
        out_shape=[
            jax.ShapeDtypeStruct((width, 2 * units), BF16),
            jax.ShapeDtypeStruct((width, LANES), F32),
            jax.ShapeDtypeStruct((1, units), F32),
        ],
        compiler_params=params(),
        cost_estimate=long,
        name="feed_grads",
    )(which, x, dy, act, grad, up, gain_col, shift_col, *after)


def lane_fold(values, combine):
    total = values[:, :LANES]
    for j in range(1, values.shape[1] // LANES):
        total = combine(total, values[:, j * LANES : (j + 1) * LANES])
    return total


def pick_heads(both, heads):
    return [jnp.where(mine, both, jnp.zeros_like(both)) for mine in heads]


def attend_kernel(info, slots, q_ref, g_ref, dense_ref, prior_ref, *refs, block, run_rows, parts, run, ties):
    k_parts, v_parts, refs = refs[:parts], refs[parts : 2 * parts], refs[2 * parts + ties :]
    o_ref, stat_ref, send_ref, keep_ref, k_ref, v_ref, score_ref, acc_ref, branch_ref = refs
    per_run = run_rows // block
    pair, place_in_run = pl.program_id(0), pl.program_id(1)
    full = info[run]

    @pl.when((pair == 0) & (place_in_run == 0))
    def _():
        branch_ref[...] = prior_ref[...].astype(F32)

    @pl.when(place_in_run == 0)
    def _():
        at = 0
        for j in range(parts):
            there = pl.ds(at, k_parts[j].shape[0])
            k_ref[there, :] = k_parts[j][...]
            v_ref[there, :] = v_parts[j][...]
            at += k_parts[j].shape[0]

    lane = lax.broadcasted_iota(jnp.int32, (block, LANES), 1)
    heads = (lane < HD, lane >= HD)

    def rows_of(at, count):
        return pl.ds(pl.multiple_of(slots[at] * run_rows, run_rows), count)

    def one_block(within):
        queries = pick_heads(q_ref[...], heads)
        seen = (within + 1) * block

        def score(at, tops, last):
            count = seen if last else run_rows
            keys = k_ref[rows_of(at, count), :]
            out = []
            for h in range(2):
                scores = dot(queries[h], keys, NT)
                if last:
                    row = lax.broadcasted_iota(jnp.int32, (block, count), 0)
                    col = lax.broadcasted_iota(jnp.int32, (block, count), 1)
                    scores = jnp.where(col <= row + within * block, scores, masked_value)
                score_ref[h, at, :, :count] = scores
                out.append(jnp.maximum(tops[h], lane_fold(scores, jnp.maximum)))
            return tuple(out)

        least = jnp.full((block, LANES), masked_value, F32)
        tops = lax.fori_loop(0, full, lambda at, carry: score(at, carry, False), (least, least))
        tops = score(full, tops, True)
        tops = [jnp.max(top, axis=1, keepdims=True) * F32(LOG2E) for top in tops]

        acc_ref[...] = jnp.zeros_like(acc_ref)

        def weigh(at, totals, last):
            count = seen if last else run_rows
            values = v_ref[rows_of(at, count), :]
            out = []
            for h in range(2):
                soft = jnp.exp2(score_ref[h, at, :, :count] * F32(LOG2E) - tops[h])
                out.append(totals[h] + lane_fold(soft, jnp.add))
                acc_ref[h] += dot(soft.astype(BF16), values, NN)
            return tuple(out)

        nought = jnp.zeros((block, LANES), F32)
        totals = lax.fori_loop(0, full, lambda at, carry: weigh(at, carry, False), (nought, nought))
        totals = weigh(full, totals, True)
        totals = [jnp.sum(total, axis=1, keepdims=True) for total in totals]
        attended = jnp.where(heads[0], acc_ref[0] / totals[0], acc_ref[1] / totals[1])
        o_ref[...] = attended.astype(o_ref.dtype)
        mine = pl.ds(within * block, block)
        branch_ref[mine, :] += dot(attended.astype(BF16), dense_ref[...], NT)
        product = attended * g_ref[...].astype(F32)
        row_terms = [jnp.sum(jnp.where(mine, product, 0.0), axis=1, keepdims=True) for mine in heads]
        logs = [tops[h] + jnp.log2(totals[h]) for h in range(2)]
        stats = jnp.where(lane == 0, logs[0], jnp.where(lane == 1, logs[1], 0.0))
        stats = jnp.where(lane == 2, row_terms[0], jnp.where(lane == 3, row_terms[1], stats))
        stat_ref[...] = jnp.transpose(stats)[:8]

    for within in range(per_run):
        pl.when(place_in_run == within)(functools.partial(one_block, within))

    @pl.when((pair == pl.num_programs(0) - 1) & (place_in_run == per_run - 1))
    def _():
        half = run_rows // 2
        send_ref[...] = branch_ref[pl.ds(pl.multiple_of((1 - info[2]) * half, half), half), :].astype(BF16)
        keep_ref[...] = branch_ref[pl.ds(pl.multiple_of(info[2] * half, half), half), :]


def attend(info, slots, q, g, kv_parts, dense, prior, run, after=()):
    rows, width = q.shape
    model = dense.shape[0]
    keys = sum(kv.shape[0] for kv in kv_parts)
    run_rows = rows // 2
    block = min(512, run_rows)
    per_run = run_rows // block
    pairs = width // LANES
    by_query = pl.BlockSpec((block, LANES), lambda p, i, *_: (run * per_run + i, p))
    by_key = [pl.BlockSpec((kv.shape[0], LANES), lambda p, i, *_: (0, p)) for kv in kv_parts]
    by_value = [pl.BlockSpec((kv.shape[0], LANES), lambda p, i, *_: (0, pairs + p)) for kv in kv_parts]
    kernel = functools.partial(
        attend_kernel, block=block, run_rows=run_rows, parts=len(kv_parts), run=run, ties=len(after)
    )
    return pl.pallas_call(
        kernel,
        grid_spec=pltpu.PrefetchScalarGridSpec(
            num_scalar_prefetch=2,
            grid=(pairs, per_run),
            in_specs=[
                by_query, by_query,
                pl.BlockSpec((model, LANES), lambda p, i, *_: (0, p)),
                pl.BlockSpec((run_rows, model), lambda p, i, *_: (run, 0)),
                *by_key, *by_value,
            ] + [anywhere] * len(after),
            out_specs=[
                pl.BlockSpec((block, LANES), lambda p, i, *_: (i, p)),
                pl.BlockSpec((8, block), lambda p, i, *_: (p, i)),
                whole((run_rows // 2, model)),
                whole((run_rows // 2, model)),
            ],
            scratch_shapes=[
                pltpu.VMEM((keys, LANES), BF16),
                pltpu.VMEM((keys, LANES), BF16),
                pltpu.VMEM((2, keys // run_rows, block, run_rows), F32),
                pltpu.VMEM((2, block, LANES), F32),
                pltpu.VMEM((run_rows, model), F32),
            ],
        ),
        out_shape=[
            jax.ShapeDtypeStruct((run_rows, width), BF16),
            jax.ShapeDtypeStruct((8 * pairs, run_rows), F32),
            jax.ShapeDtypeStruct((run_rows // 2, model), BF16),
            jax.ShapeDtypeStruct((run_rows // 2, model), F32),
        ],
        compiler_params=params(),
        cost_estimate=brief,
        name="attend",
    )(info, slots, q, g, dense, prior, *kv_parts, *kv_parts, *after)


def attend_back_kernel(info, slots, q_ref, g_ref, stat_ref, *refs, block, run_rows, parts, home, ties):
    k_parts, v_parts, refs = refs[:parts], refs[parts : 2 * parts], refs[2 * parts + ties :]
    dq_ref, dk_out, dv_out, refs = refs[0], refs[1], refs[2], refs[3:]
    if home:
        back_ref, refs = refs[0], refs[1:]
    k_ref, v_ref, dk_ref, dv_ref, acc_ref = refs
    per_run = run_rows // block
    step = pl.program_id(0)
    full = info[step // per_run]

    @pl.when(step == 0)
    def _():
        at = 0
        for j in range(parts):
            there = pl.ds(at, k_parts[j].shape[0])
            k_ref[there, :] = k_parts[j][...]
            v_ref[there, :] = v_parts[j][...]
            at += k_parts[j].shape[0]
        dk_ref[...] = jnp.zeros_like(dk_ref)
        dv_ref[...] = jnp.zeros_like(dv_ref)

    lane = lax.broadcasted_iota(jnp.int32, (block, LANES), 1)
    heads = (lane < HD, lane >= HD)

    def rows_of(at, count):
        return pl.ds(pl.multiple_of(slots[at] * run_rows, run_rows), count)

    def one_block(within):
        queries, grads = pick_heads(q_ref[...], heads), pick_heads(g_ref[...], heads)
        stats = jnp.transpose(stat_ref[...])
        logs, row_terms = [stats[:, h : h + 1] for h in range(2)], [stats[:, 2 + h : 3 + h] for h in range(2)]
        seen = (within + 1) * block
        acc_ref[...] = jnp.zeros_like(acc_ref)

        def back(at, last):
            count = seen if last else run_rows
            there = rows_of(at, count)
            keys, values = k_ref[there, :], v_ref[there, :]
            key_terms, value_terms = [], []
            for h in range(2):
                soft = jnp.exp2(dot(queries[h], keys, NT) * F32(LOG2E) - logs[h])
                if last:
                    row = lax.broadcasted_iota(jnp.int32, (block, count), 0)
                    col = lax.broadcasted_iota(jnp.int32, (block, count), 1)
                    soft = jnp.where(col <= row + within * block, soft, 0.0)
                grad_soft = dot(grads[h], values, NT)
                grad_score = (soft * (grad_soft - row_terms[h])).astype(BF16)
                acc_ref[h] += dot(grad_score, keys, NN)
                key_terms.append(dot(grad_score, queries[h], TN))
                value_terms.append(dot(soft.astype(BF16), grads[h], TN))
            dk_ref[there, :] += key_terms[0] + key_terms[1]
            dv_ref[there, :] += value_terms[0] + value_terms[1]

        def back_whole(at, carry):
            back(at, False)
            return carry

        lax.fori_loop(0, full, back_whole, 0)
        back(full, True)
        dq_ref[...] = (jnp.where(heads[0], acc_ref[0], acc_ref[1]) * F32(HD**-0.5)).astype(dq_ref.dtype)

    for within in range(per_run):
        pl.when(step % per_run == within)(functools.partial(one_block, within))

    @pl.when(step == pl.num_programs(0) - 1)
    def _():
        own = dk_out.shape[0]
        dk_out[...] = dk_ref[:own, :]
        dv_out[...] = dv_ref[:own, :]
        if home:
            back_ref[:, :LANES] = dk_ref[home:, :].astype(BF16)
            back_ref[:, LANES:] = dv_ref[home:, :].astype(BF16)


def attend_back(info, slots, q, g, stats, kv_parts, pair, home, after=()):
    rows, width = q.shape
    keys = sum(kv.shape[0] for kv in kv_parts)
    run_rows = rows // 2
    block = min(512, run_rows)
    pairs = width // LANES
    own = home or keys
    by_query = pl.BlockSpec((block, LANES), lambda i, *_: (i, pair))
    by_key = [pl.BlockSpec((kv.shape[0], LANES), lambda i, *_: (0, pair)) for kv in kv_parts]
    by_value = [pl.BlockSpec((kv.shape[0], LANES), lambda i, *_: (0, pairs + pair)) for kv in kv_parts]
    kernel = functools.partial(
        attend_back_kernel, block=block, run_rows=run_rows, parts=len(kv_parts), home=home, ties=len(after)
    )
    out_specs = [pl.BlockSpec((block, LANES), lambda i, *_: (i, 0)), whole((own, LANES)), whole((own, LANES))]
    out_shape = [
        jax.ShapeDtypeStruct((rows, LANES), BF16),
        jax.ShapeDtypeStruct((own, LANES), F32),
        jax.ShapeDtypeStruct((own, LANES), F32),
    ]
    if home:
        out_specs.append(whole((keys - home, 2 * LANES)))
        out_shape.append(jax.ShapeDtypeStruct((keys - home, 2 * LANES), BF16))
    return pl.pallas_call(
        kernel,
        grid_spec=pltpu.PrefetchScalarGridSpec(
            num_scalar_prefetch=2,
            grid=(rows // block,),
            in_specs=[by_query, by_query, pl.BlockSpec((8, block), lambda i, *_: (pair, i)), *by_key, *by_value]
            + [anywhere] * len(after),
            out_specs=out_specs,
            scratch_shapes=[
                pltpu.VMEM((keys, LANES), BF16),
                pltpu.VMEM((keys, LANES), BF16),
                pltpu.VMEM((keys, LANES), F32),
                pltpu.VMEM((keys, LANES), F32),
                pltpu.VMEM((2, block, LANES), F32),
            ],
        ),
        out_shape=out_shape,
        compiler_params=params(),
        cost_estimate=long,
        name="attend_back",
    )(info, slots, q, g, stats, *kv_parts, *kv_parts, *after)


def back_kernel(which, dq_ref, *refs, pairs):
    own_k, refs = refs[:pairs], refs[pairs:]
    own_v, refs = refs[:pairs], refs[pairs:]
    got, refs = refs[:pairs], refs[pairs:]
    w_ref, gain_ref, dx_in, cos_ref, low_ref, high_ref = refs[:6]
    dproj_ref, send_ref, keep_ref = refs[-3:]
    half = dq_ref.shape[1]
    cosines, low, high = cos_ref[...], low_ref[...], high_ref[...]
    for j in range(pairs):
        at = slice(j * LANES, (j + 1) * LANES)
        query = dq_ref[:, at].astype(F32)
        dproj_ref[:, at] = turn(query, cosines, -low, -high).astype(BF16)
        key = own_k[j][...] + got[j][:, :LANES].astype(F32)
        dproj_ref[:, half + j * LANES : half + (j + 1) * LANES] = turn(key, cosines, -low, -high).astype(BF16)
        value = own_v[j][...] + got[j][:, LANES:].astype(F32)
        dproj_ref[:, 2 * half + j * LANES : 2 * half + (j + 1) * LANES] = value.astype(BF16)
    summed = dot(dproj_ref[...], w_ref[...], NT) * gain_ref[...] + dx_in[...].astype(F32)
    mine = pl.program_id(0) % 2 == which[1]

    @pl.when(mine)
    def _():
        keep_ref[...] = summed

    @pl.when(jnp.logical_not(mine))
    def _():
        send_ref[...] = summed.astype(send_ref.dtype)


def back(which, dq, dk, dv, got, w, gain, dx_part, tables, after=()):
    rows, half = dq.shape
    width = w.shape[0]
    step = rows // 4
    pairs = len(dk)
    by_row = lambda cols: pl.BlockSpec((step, cols), lambda i, *_: (i, 0))
    by_run = pl.BlockSpec((step, width), lambda i, *_: (i // 2, 0))
    return pl.pallas_call(
        functools.partial(back_kernel, pairs=pairs),
        grid_spec=pltpu.PrefetchScalarGridSpec(
            num_scalar_prefetch=1,
            grid=(4,),
            in_specs=[by_row(half)] + [by_row(LANES)] * (2 * pairs) + [by_row(2 * LANES)] * pairs
            + [whole(w.shape), whole(gain.shape), by_row(width)] + [by_row(LANES)] * 3
            + [anywhere] * len(after),
            out_specs=[by_row(3 * half), by_run, by_run],
        ),
        out_shape=[
            jax.ShapeDtypeStruct((rows, 3 * half), BF16),
            jax.ShapeDtypeStruct((rows // 2, width), BF16),
            jax.ShapeDtypeStruct((rows // 2, width), F32),
        ],
        compiler_params=params(),
        cost_estimate=brief,
        name="back",
    )(which, dq, *dk, *dv, *got, w, gain, dx_part, *tables, *after)


def weight_kernel(
    which, x_ref, dy_ref, dproj_ref, o_ref, w_ref, gain_col, shift_col, *refs
):
    gqkv_ref, gdense_ref, vec_ref, gb_ref, acc, dense_acc, sum_acc = refs[-7:]
    step = pl.program_id(0)

    @pl.when(step == 0)
    def _():
        acc[...] = jnp.zeros_like(acc)
        dense_acc[...] = jnp.zeros_like(dense_acc)
        sum_acc[...] = jnp.zeros_like(sum_acc)

    xhat, _ = normalise(x_ref[0].astype(F32))
    dproj = dproj_ref[...]
    acc[...] += dot(xhat.astype(BF16), dproj, TN)
    dense_acc[...] += dot(dy_ref[0], o_ref[...], TN)
    sum_acc[...] += jnp.sum(dproj.astype(F32), axis=0, keepdims=True)

    @pl.when(step == pl.num_programs(0) - 1)
    def _():
        sums, raw, w = sum_acc[...], acc[...], w_ref[...].astype(F32)
        gqkv_ref[...] = (raw * gain_col[...] + shift_col[...] * sums).astype(gqkv_ref.dtype)
        gdense_ref[...] = dense_acc[...].astype(gdense_ref.dtype)
        gb_ref[...] = sums
        lane = lax.broadcasted_iota(jnp.int32, vec_ref.shape, 1)
        gain_grad = jnp.sum(raw * w, axis=1, keepdims=True)
        shift_grad = jnp.sum(w * sums, axis=1, keepdims=True)
        vec_ref[...] = jnp.where(lane == 1, gain_grad, jnp.where(lane == 2, shift_grad, 0.0))


def weight_grads(which, x, dy, dproj, o, w, gain_col, shift_col, after=()):
    _, rows, width = x.shape
    half = o.shape[1]
    step = min(512, rows)
    chosen = pl.BlockSpec((1, step, width), lambda i, which: (which[0], i, 0))
    by_row = lambda cols: pl.BlockSpec((step, cols), lambda i, *_: (i, 0))
    return pl.pallas_call(
        weight_kernel,
        grid_spec=pltpu.PrefetchScalarGridSpec(
            num_scalar_prefetch=1,
            grid=(rows // step,),
            in_specs=[chosen, chosen, by_row(3 * half), by_row(half), whole(w.shape),
                      whole(gain_col.shape), whole(shift_col.shape)] + [anywhere] * len(after),
            out_specs=[whole((width, 3 * half)), whole((width, half)), whole((width, LANES)), whole((1, 3 * half))],
            scratch_shapes=[pltpu.VMEM((width, 3 * half), F32), pltpu.VMEM((width, half), F32),
                            pltpu.VMEM((1, 3 * half), F32)],
        ),
        out_shape=[
            jax.ShapeDtypeStruct((width, 3 * half), BF16),
            jax.ShapeDtypeStruct((width, half), BF16),
            jax.ShapeDtypeStruct((width, LANES), F32),
            jax.ShapeDtypeStruct((1, 3 * half), F32),
        ],
        compiler_params=params(),
        cost_estimate=long,
        name="weight_grads",
    )(which, x, dy, dproj, o, w, gain_col, shift_col, *after)


def join_kernel(*refs):
    out = refs[-1]
    at = 0
    for ref in refs[:-1]:
        out[:, at : at + ref.shape[1]] = ref[...]
        at += ref.shape[1]


def join(arrays):
    rows = arrays[0].shape[0]
    step = rows // 4
    widths = [array.shape[1] for array in arrays]
    by_row = lambda cols: pl.BlockSpec((step, cols), lambda i: (i, 0))
    return pl.pallas_call(
        join_kernel,
        grid=(4,),
        in_specs=[by_row(width) for width in widths],
        out_specs=by_row(sum(widths)),
        out_shape=jax.ShapeDtypeStruct((rows, sum(widths)), BF16),
        compiler_params=params(),
        cost_estimate=brief,
        name="join",
    )(*arrays)


def norm_back_kernel(which, x_ref, dy_ref, kept_ref, got_ref, *refs):
    out_ref = refs[-1]
    xhat, scale = normalise(x_ref[0].astype(F32))
    grad = kept_ref[...].astype(F32) + got_ref[...].astype(F32)
    centre = jnp.mean(grad, axis=-1, keepdims=True)
    along = jnp.mean(grad * xhat, axis=-1, keepdims=True)
    out_ref[...] = (dy_ref[0].astype(F32) + scale * (grad - centre - xhat * along)).astype(out_ref.dtype)


def norm_back(which, x, dy, kept, got, run, after=()):
    rows, width = got.shape
    step = min(256, rows)
    blocks = rows // step
    chosen = pl.BlockSpec(
        (1, step, width), lambda i, which: (which[0], (2 * run + which[1]) * blocks + i, 0)
    )
    return pl.pallas_call(
        norm_back_kernel,
        grid_spec=pltpu.PrefetchScalarGridSpec(
            num_scalar_prefetch=1,
            grid=(blocks,),
            in_specs=[chosen, chosen,
                      pl.BlockSpec((step, width), lambda i, *_: (run * blocks + i, 0)),
                      pl.BlockSpec((step, width), lambda i, *_: (i, 0))] + [anywhere] * len(after),
            out_specs=pl.BlockSpec((step, width), lambda i, *_: (i, 0)),
        ),
        out_shape=jax.ShapeDtypeStruct((rows, width), BF16),
        compiler_params=params(),
        cost_estimate=longest,
        name="norm_back",
    )(which, x, dy, kept, got, *after)


def finish_kernel(which, x_ref, kept_ref, got_ref, one_ref, two_ref, *refs):
    summed = kept_ref[...] + got_ref[...].astype(F32) + x_ref[0].astype(F32) + one_ref[...] + two_ref[...]
    refs[-1][...] = summed.astype(BF16)


def finish(which, x, kept, got, one, two, run, after=()):
    rows, width = got.shape
    step = min(256, rows)
    blocks = rows // step
    by_row = pl.BlockSpec((step, width), lambda i, *_: (i, 0))
    return pl.pallas_call(
        finish_kernel,
        grid_spec=pltpu.PrefetchScalarGridSpec(
            num_scalar_prefetch=1,
            grid=(blocks,),
            in_specs=[
                pl.BlockSpec((1, step, width), lambda i, which: (which[0], (2 * run + which[1]) * blocks + i, 0)),
                by_row, by_row, whole(one.shape), whole(two.shape),
            ] + [anywhere] * len(after),
            out_specs=by_row,
        ),
        out_shape=jax.ShapeDtypeStruct((rows, width), BF16),
        compiler_params=params(),
        cost_estimate=brief,
        name="finish",
    )(which, x, kept, got, one, two, *after)


def lay_kernel(early_ref, late_ref, *refs):
    out = refs[-1]
    run = pl.program_id(0) % 2

    @pl.when(run == 0)
    def _():
        out[0] = early_ref[...]

    @pl.when(run == 1)
    def _():
        out[0] = late_ref[...]


def lay_gathered(early, late, after=()):
    rows, width = early.shape[0] // 2, early.shape[1]
    half = pl.BlockSpec((rows, width), lambda i: (i // 2, 0))
    return pl.pallas_call(
        lay_kernel,
        grid=(4,),
        in_specs=[half, half] + [anywhere] * len(after),
        out_specs=pl.BlockSpec((1, rows, width), lambda i: (i // 2, i % 2, 0)),
        out_shape=jax.ShapeDtypeStruct((2, 2 * rows, width), BF16),
        compiler_params=params(),
        cost_estimate=brief,
        name="lay_gathered",
    )(early, late, *after)


def lay_round_kernel(index, *refs):
    out = refs[-1]
    run, slot = pl.program_id(0) // 4, pl.program_id(0) % 4
    back = (index[0] + 4 - slot) % 4
    for j in range(8):

        @pl.when((run == j // 4) & (back == j % 4))
        def _(j=j):
            out[0] = refs[j][...]


def lay_round(index, early, late):
    half, width = early[0].shape
    return pl.pallas_call(
        lay_round_kernel,
        grid_spec=pltpu.PrefetchScalarGridSpec(
            num_scalar_prefetch=1,
            grid=(8,),
            in_specs=[whole((half, width))] * 8,
            out_specs=pl.BlockSpec((1, half, width), lambda i, *_: ((i % 4) // 2, 2 * (i // 4) + i % 2, 0)),
        ),
        out_shape=jax.ShapeDtypeStruct((2, 4 * half, width), BF16),
        compiler_params=params(),
        cost_estimate=brief,
        name="lay_round",
    )(index[None], *early, *late)


def swap(values, axis):
    return lax.ppermute(values, axis, [(0, 1), (1, 0)])


def across(values, bit):
    return lax.ppermute(values, "dp", [(i, i ^ bit) for i in range(4)])


def gather_half(values, seq_first):
    values = jnp.concatenate([values[None], swap(values, "mh")[None]], axis=0)
    steps = [lambda v: swap(v, "seq"), lambda v: across(v, 2)]
    for step in steps if seq_first else steps[::-1]:
        values = jnp.concatenate([values, step(values)], axis=0)
    values = jnp.concatenate([values, across(values, 1)], axis=0)
    return values.reshape(8, 2, *values.shape[1:])


def round_mp(mine):
    axes = ("mh", "ml")
    return [mine] + [lax.ppermute(mine, axes, [(i, (i + k) % 4) for i in range(4)]) for k in (1, 2, 3)]


def rotation_tables(positions):
    half = ROT // 2
    frequency = jnp.power(F32(10000.0), -2.0 * jnp.arange(half, dtype=F32) / ROT)
    angles = frequency[:, None] * positions.astype(F32)[None, :]
    cosines, sines = lax.optimization_barrier((jnp.cos(angles), jnp.sin(angles)))
    cosines, sines = cosines.T, sines.T
    rows = positions.shape[0]
    rest = jnp.zeros((rows, HD - ROT), F32)
    blank = jnp.zeros((rows, half), F32)
    per_head = (
        jnp.concatenate([cosines, cosines, rest + 1.0], axis=1),
        jnp.concatenate([-sines, blank, rest], axis=1),
        jnp.concatenate([blank, sines, rest], axis=1),
    )
    return tuple(jnp.tile(table, (1, LANES // HD)) for table in per_head)


def body(
    tokens, places, w_qkv, b_qkv, w_dense, b_dense, w_up, b_up, w_down, b_down,
    norm1_gain, norm1_bias, norm2_gain, norm2_bias, out_grad, *, seq_size, owners,
):
    _, rows, width = tokens.shape
    share = width // owners
    heads = b_qkv.shape[1]
    cols = heads * HD
    units = w_up.shape[1]
    side, part = lax.axis_index("mh"), lax.axis_index("ml")
    index = (2 * side + part).astype(jnp.int32)
    owner = lax.axis_index("dp") * seq_size + lax.axis_index("seq")
    which = jnp.stack([side, part]).astype(jnp.int32)
    where = jnp.stack([side, owner]).astype(jnp.int32)

    run_rows = rows // 2
    held = places[:, ::run_rows] // run_rows

    def column(vector):
        vector = vector.reshape(-1)
        return jnp.pad(vector, (0, share - vector.shape[0]))[:, None]

    small = jnp.concatenate(
        [column(v) for v in (b_dense, b_down, norm1_gain, norm1_bias, norm2_gain, norm2_bias, b_qkv, b_up,
                            held.astype(BF16))],
        axis=1,
    )
    small = jnp.pad(small, ((0, 0), (0, LANES - small.shape[1])))
    one = w_qkv[:2].transpose(1, 0, 2).reshape(share, 2 * cols)
    two = jnp.concatenate([w_qkv[2], w_dense.T, small], axis=1)
    three, four = w_up, w_down.T
    first_widths = (6 * cols, 2 * cols, 2 * LANES)
    if owners == 8 and seq_size == 2:
        one, two = gather_half(one, True), gather_half(two, False)
        qkv_w, dense_w, small = place(place_first_kernel, where, one, two, first_widths, (BF16, BF16, F32))
        pack = lax.all_gather(jnp.concatenate([three, four], axis=1), ("dp", "seq", "mh"), axis=0, tiled=True)
        up_w, down_w = place_second(pack.reshape(owners, 2, share, 2 * units))
    else:

        def gather(values):
            values = lax.all_gather(values, ("dp", "seq", "mh"), axis=0, tiled=True)
            return values.reshape(owners, 2, share, -1).transpose(0, 2, 1, 3).reshape(width, 2, -1)

        one, two, three, four = gather(one), gather(two), gather(three), gather(four)
        qkv_w = jnp.concatenate([one[:, :, :cols], one[:, :, cols:], two[:, :, :cols]], axis=1)
        qkv_w, dense_w = qkv_w.reshape(width, 6 * cols), two[:, :, cols : 2 * cols].reshape(width, 2 * cols)
        small = two[:, :, 2 * cols :].reshape(width, 2 * LANES).astype(F32)
        up_w, down_w = three.reshape(width, 2 * units), four.reshape(width, 2 * units)
    vectors = small[:, :8]
    piece = HD // owners
    biases = small.reshape(owners, share, 2, LANES)
    qkv_b = biases[:, : 3 * heads * piece, :, 6].reshape(owners, 3, heads, piece, 2)
    qkv_b = qkv_b.transpose(1, 4, 2, 0, 3).reshape(1, 6 * cols)
    up_rows, up_cols = b_up.shape
    up_b = biases[..., 7].reshape(owners, up_rows, up_cols, 2).transpose(3, 1, 0, 2).reshape(1, 2 * units)
    by_row = vectors.T
    row_of = lambda at: by_row[at].reshape(1, width)
    column_of = lambda at: vectors[:, at].reshape(width, 1)

    my_places = lax.dynamic_index_in_dim(places, side, 0, keepdims=False)
    runs = lax.dynamic_index_in_dim(held, side, 0, keepdims=False)
    if owners == 8 and seq_size == 2:
        other = lax.dynamic_slice(small, ((owner ^ 1) * share + 2 * side, 8), (2, 1))[:, 0]
        all_runs = jnp.concatenate([runs, (other + 0.5).astype(jnp.int32)])
    elif seq_size == 2:
        all_runs = jnp.concatenate([runs, swap(runs, "seq")])
    else:
        all_runs = lax.all_gather(runs, "seq", axis=0, tiled=True)
    order = jnp.arange(2 * seq_size, dtype=jnp.int32)
    slots = jnp.sum(jnp.where(all_runs[None, :] == order[:, None], order[None, :], 0), axis=1)
    tables = rotation_tables(my_places)

    q, kv, grad_o = front(which, tokens, out_grad, qkv_w, qkv_b, dense_w, row_of(2), row_of(3), tables)
    if seq_size == 2:
        kv_parts = (kv, swap(kv, "seq"))
    else:
        kv_parts = (lax.all_gather(kv, "seq", axis=0, tiled=True),)

    mlp_part, mlp_dx, act, mlp_grad = feed(which, tokens, out_grad, up_w, up_b, down_w, row_of(4), row_of(5))
    info = jnp.concatenate([runs, which[1:]])
    quarter = rows // 4

    o_early, stat_early, send, keep_early = attend(info, slots, q, grad_o, kv_parts, dense_w, mlp_part, 0)
    got_early = swap(send, "ml")
    o_late, stat_late, send, keep_late = attend(
        info, slots, q, grad_o, kv_parts, dense_w, mlp_part, 1, (o_early,)
    )
    got_late = swap(send, "ml")
    stats = jnp.concatenate([stat_early, stat_late], axis=1)
    mixed_early = finish(which, tokens, keep_early, got_early, row_of(0), row_of(1), 0, (o_late,))
    after = (mixed_early,)
    mixed_early = lax.all_gather(mixed_early, ("mh", "ml"), axis=0, tiled=True)

    home = rows if seq_size == 2 else 0
    dq, dk, dv, got = [], [], [], []
    for pair in range(q.shape[1] // LANES):
        outs = attend_back(info, slots, q, grad_o, stats, kv_parts, pair, home, after)
        after = (outs[0],)
        dq.append(outs[0])
        if home:
            dk.append(outs[1])
            dv.append(outs[2])
            got.append(swap(outs[3], "seq"))
        else:
            both = jnp.concatenate([outs[1], outs[2]], axis=1).astype(BF16)
            got.append(lax.psum_scatter(both, "seq", scatter_dimension=0, tiled=True))
            dk.append(jnp.zeros((rows, LANES), F32))
            dv.append(jnp.zeros((rows, LANES), F32))
        if pair == 1:
            mixed_late = finish(which, tokens, keep_late, got_late, row_of(0), row_of(1), 1, after)
            after = (outs[0], mixed_late, got[0])
            mixed_late = lax.all_gather(mixed_late, ("mh", "ml"), axis=0, tiled=True)
        elif pair > 1:
            after = (outs[0], got[pair - 1])
    feed_weights, mlp_vectors, grad_up_b = feed_grads(
        which, tokens, out_grad, act, mlp_grad, up_w, column_of(4), column_of(5), after + (mixed_early,)
    )
    dq = jnp.concatenate(dq, axis=1)
    dproj, send, keep = back(
        which, dq, dk, dv, got, qkv_w, row_of(2), mlp_dx, tables, (grad_up_b,)
    )
    mixed = lay_gathered(mixed_early, mixed_late, (dproj,))
    got = [swap(send[run * quarter : (run + 1) * quarter], "ml") for run in range(2)]
    attended = jnp.concatenate([o_early, o_late], axis=0)
    grad_qkv, grad_dense, qkv_vectors, grad_qkv_b = weight_grads(
        which, tokens, out_grad, dproj, attended, qkv_w, column_of(2), column_of(3), (mixed_late,)
    )
    ties = ((grad_qkv_b,), (grad_qkv_b,))
    input_grad = [norm_back(which, tokens, out_grad, keep, got[run], run, ties[run]) for run in range(2)]
    input_grad = lay_round(index, *[round_mp(rows_done) for rows_done in input_grad])

    def scatter(grads):
        return lax.psum_scatter(grads, ("dp", "seq"), scatter_dimension=0, tiled=True)

    def settle(sums):
        sums = sums.astype(F32)
        mine = lax.dynamic_index_in_dim(sums, side, 1, keepdims=False)
        other = lax.dynamic_index_in_dim(sums, 1 - side, 1, keepdims=False)
        return mine + swap(other.astype(BF16), "mh").astype(F32)

    vector_grads = (mlp_vectors + qkv_vectors)[:, None, :5]
    vector_grads = jnp.broadcast_to(vector_grads, (width, 2, 5))
    bias_qkv = grad_qkv_b.reshape(3, 2, heads, owners, piece).transpose(3, 0, 2, 4, 1)
    bias_qkv = bias_qkv.reshape(owners, 3 * heads * piece, 2)
    bias_qkv = jnp.pad(bias_qkv, ((0, 0), (0, share - 3 * heads * piece), (0, 0))).reshape(width, 2, 1)
    bias_up = grad_up_b.reshape(2, up_rows, owners, up_cols).transpose(2, 1, 3, 0).reshape(width, 2, 1)
    tail = jnp.concatenate([vector_grads, bias_qkv, bias_up], axis=2)
    tail = jnp.pad(tail, ((0, 0), (0, 0), (0, LANES // 2 - 7))).astype(BF16).reshape(width, LANES)
    packed = scatter(join((grad_qkv, grad_dense, tail, feed_weights)))
    first, owned_feed = packed[:, : 8 * cols + LANES], packed[:, 8 * cols + LANES :]
    owned_feed = owned_feed.reshape(share, 2, 2, units).transpose(0, 2, 1, 3).reshape(share, 2, 2 * units)
    owned_qkv = first[:, : 6 * cols].reshape(share, 3, 2, cols).transpose(0, 2, 1, 3).reshape(share, 2, 3 * cols)
    owned_dense = first[:, 6 * cols : 8 * cols].reshape(share, 2, cols)
    owned_tail = first[:, 8 * cols :].reshape(share, 2, LANES // 2)
    owned = settle(jnp.concatenate([owned_feed, owned_qkv, owned_dense, owned_tail], axis=2))
    owned_feed, owned = owned[:, : 2 * units], owned[:, 2 * units :]
    vectors = owned[:, 4 * cols :]
    norms = vectors[:, :5]
    norms = norms + swap(norms, "ml")
    bias_grad = norms[:, 0]
    return (
        mixed,
        input_grad,
        owned[:, : 3 * cols].reshape(share, 3, cols).transpose(1, 0, 2),
        vectors[: 3 * heads * piece, 5].reshape(b_qkv.shape),
        owned[:, 3 * cols : 4 * cols].T,
        bias_grad,
        owned_feed[:, :units],
        vectors[:, 6].reshape(b_up.shape),
        owned_feed[:, units:].T,
        bias_grad,
        norms[:, 1],
        norms[:, 2],
        norms[:, 3],
        norms[:, 4],
    )


def solution(mesh):
    dp, seq, mp = (mesh.shape[axis] for axis in ("dp", "seq", "mp"))
    split = Mesh(mesh.devices.reshape(dp, seq, 2, mp // 2), ("dp", "seq", "mh", "ml"))
    mp, owner = ("mh", "ml"), ("dp", "seq")
    row = P("dp", "seq", None)
    vector = P(owner)
    weights = (
        P(None, owner, mp), P(None, mp, owner), P(mp, owner), vector, P(owner, mp), P(mp, owner),
        P(mp, owner), vector, vector, vector, vector, vector,
    )
    return jax.shard_map(
        functools.partial(body, seq_size=seq, owners=dp * seq),
        mesh=split,
        in_specs=(row, P("dp", "seq")) + weights + (row,),
        out_specs=(row, row) + weights,
        check_vma=False,
    )
```

```python
import functools

import jax
import jax.numpy as jnp
from jax import lax
from jax.experimental import pallas as pl
from jax.experimental.pallas import tpu as pltpu
from jax.sharding import Mesh
from jax.sharding import PartitionSpec as P

HD = 64
ROT = 16
LANES = 128
F32 = jnp.float32
BF16 = jnp.bfloat16
LOG2E = 1.4426950408889634
norm_eps = 1e-05
masked_value = -1e30
vmem_bytes = 60 * 2**20
brief = pl.CostEstimate(flops=1, bytes_accessed=1, transcendentals=0)
long = pl.CostEstimate(flops=2**33, bytes_accessed=2**24, transcendentals=0)

NN = (((1,), (0,)), ((), ()))
NT = (((1,), (1,)), ((), ()))
TN = (((0,), (0,)), ((), ()))


def dot(left, right, dims):
    return lax.dot_general(left, right, dims, preferred_element_type=F32)


def normalise(rows):
    centre = jnp.mean(rows, axis=-1, keepdims=True)
    deviate = rows - centre
    spread = jnp.mean(deviate * deviate, axis=-1, keepdims=True)
    scale = lax.rsqrt(spread + norm_eps)
    return deviate * scale, scale


def turn(chunk, cosines, sine_low, sine_high):
    half = ROT // 2
    return (
        chunk * cosines
        + pltpu.roll(chunk, LANES - half, 1) * sine_low
        + pltpu.roll(chunk, half, 1) * sine_high
    )

longest = pl.CostEstimate(flops=2**36, bytes_accessed=2**27, transcendentals=0)


anywhere = pl.BlockSpec(memory_space=pl.ANY)


def whole(shape):
    return pl.BlockSpec(shape, lambda *_: (0,) * len(shape))


def params(**kwargs):
    return pltpu.CompilerParams(vmem_limit_bytes=vmem_bytes, **kwargs)


def place_first_kernel(where, one_ref, two_ref, qkv_ref, dense_ref, small_ref):
    cols = one_ref.shape[-1] // 2
    near = where[0] == 0
    one = [one_ref[0, j] for j in range(2)]
    two = [two_ref[0, j] for j in range(2)]
    one = (jnp.where(near, one[0], one[1]), jnp.where(near, one[1], one[0]))
    two = (jnp.where(near, two[0], two[1]), jnp.where(near, two[1], two[0]))
    pieces = [one[j][:, i * cols : (i + 1) * cols] for i in range(2) for j in range(2)]
    pieces += [two[j][:, :cols] for j in range(2)]
    qkv_ref[...] = jnp.concatenate(pieces, axis=1)
    dense_ref[...] = jnp.concatenate([two[j][:, cols : 2 * cols] for j in range(2)], axis=1)
    small_ref[...] = jnp.concatenate([two[j][:, 2 * cols :] for j in range(2)], axis=1).astype(F32)


def place_second_kernel(pack_ref, up_ref, down_ref):
    units = pack_ref.shape[-1] // 2
    share = pack_ref.shape[2]
    for i in range(2):
        rows = slice(i * share, (i + 1) * share)
        for j in range(2):
            up_ref[rows, j * units : (j + 1) * units] = pack_ref[i, j, :, :units]
            down_ref[rows, j * units : (j + 1) * units] = pack_ref[i, j, :, units:]


def place_second(pack):
    owners, _, share, width = pack.shape
    return pl.pallas_call(
        place_second_kernel,
        grid=(owners // 2,),
        in_specs=[pl.BlockSpec((2,) + pack.shape[1:], lambda i: (i, 0, 0, 0))],
        out_specs=[pl.BlockSpec((2 * share, width), lambda i: (i, 0))] * 2,
        out_shape=[jax.ShapeDtypeStruct((owners * share, width), BF16)] * 2,
        compiler_params=params(),
        cost_estimate=brief,
        name="place_second",
    )(pack)


def place(kernel, where, one, two, widths, types):
    owners, _, share, _ = one.shape

    def spec(array, low, high):
        def index(i, where):
            bits = i ^ where[1]
            upper, lower, across = bits // 4, (bits // 2) % 2, bits % 2
            near, far = (across, upper) if low == "seq" else (upper, across)
            return (lower * 4 + far * 2 + near, 0, 0, 0)

        return pl.BlockSpec((1,) + array.shape[1:], index)

    return pl.pallas_call(
        kernel,
        grid_spec=pltpu.PrefetchScalarGridSpec(
            num_scalar_prefetch=1,
            grid=(owners,),
            in_specs=[spec(one, "seq", "dp"), spec(two, "dp", "seq")],
            out_specs=[pl.BlockSpec((share, width), lambda i, *_: (i, 0)) for width in widths],
        ),
        out_shape=[jax.ShapeDtypeStruct((owners * share, width), kind) for width, kind in zip(widths, types)],
        compiler_params=params(),
        cost_estimate=brief,
        name="place",
    )(where, one, two)


def front_kernel(
    which, x_ref, dy_ref, w_ref, wb_ref, dense_ref, gain_ref, shift_ref, cos_ref, low_ref, high_ref,
    q_ref, kv_most, kv_last, do_ref,
):
    half = q_ref.shape[1]
    most = kv_most.shape[1] // 2
    xhat, _ = normalise(x_ref[0].astype(F32))
    normed = (xhat * gain_ref[...] + shift_ref[...]).astype(BF16)
    proj = dot(normed, w_ref[...], NN) + wb_ref[...]
    cosines, low, high = cos_ref[...], low_ref[...], high_ref[...]
    for j in range(half // LANES):
        at = slice(j * LANES, (j + 1) * LANES)
        query = turn(proj[:, at], cosines, low, high).astype(BF16)
        q_ref[:, at] = query * BF16(HD**-0.5)
        key = turn(proj[:, half + j * LANES : half + (j + 1) * LANES], cosines, low, high).astype(BF16)
        if j * LANES < most:
            kv_most[:, at] = key
        else:
            kv_last[:, :LANES] = key
    kv_most[:, most:] = proj[:, 2 * half : 2 * half + most].astype(BF16)
    kv_last[:, LANES:] = proj[:, 2 * half + most :].astype(BF16)
    do_ref[...] = dot(dy_ref[0], dense_ref[...], NN).astype(BF16)


def front(which, x, dy, w, wb, dense, gain, shift, tables):
    _, rows, width = x.shape
    half = dense.shape[1]
    step = min(512, rows)
    chosen = pl.BlockSpec((1, step, width), lambda i, which: (which[0], i, 0))
    by_row = lambda cols: pl.BlockSpec((step, cols), lambda i, *_: (i, 0))
    return pl.pallas_call(
        front_kernel,
        grid_spec=pltpu.PrefetchScalarGridSpec(
            num_scalar_prefetch=1,
            grid=(rows // step,),
            in_specs=[chosen, chosen, whole(w.shape), whole(wb.shape), whole(dense.shape),
                      whole(gain.shape), whole(shift.shape)] + [by_row(LANES)] * 3,
            out_specs=[by_row(half), by_row(2 * half - 2 * LANES), by_row(2 * LANES), by_row(half)],
        ),
        out_shape=[
            jax.ShapeDtypeStruct((rows, half), BF16),
            jax.ShapeDtypeStruct((rows, 2 * half - 2 * LANES), BF16),
            jax.ShapeDtypeStruct((rows, 2 * LANES), BF16),
            jax.ShapeDtypeStruct((rows, half), BF16),
        ],
        compiler_params=params(),
        cost_estimate=brief,
        name="front",
    )(which, x, dy, w, wb, dense, gain, shift, *tables)


def feed_kernel(
    which, x_ref, dy_ref, up_ref, upb_ref, down_ref, gain_ref, shift_ref, part_ref, dx_ref, act_ref, grad_ref
):
    xhat, _ = normalise(x_ref[0].astype(F32))
    normed = (xhat * gain_ref[...] + shift_ref[...]).astype(BF16)
    hidden = dot(normed, up_ref[...], NN) + upb_ref[...]
    share = 0.5 * (1.0 + lax.erf(hidden * F32(0.5**0.5)))
    act = (hidden * share).astype(BF16)
    act_ref[...] = act
    slope = share + hidden * (jnp.exp(hidden * hidden * -0.5) * F32(0.3989422804014327))
    part_ref[...] = dot(act, down_ref[...], NT).astype(part_ref.dtype)
    grad_low = (dot(dy_ref[0], down_ref[...], NN) * slope).astype(BF16)
    grad_ref[...] = grad_low
    dx_ref[...] = (dot(grad_low, up_ref[...], NT) * gain_ref[...]).astype(dx_ref.dtype)


def feed(which, x, dy, up, upb, down, gain, shift):
    _, rows, width = x.shape
    units = up.shape[1]
    step = min(256, rows)
    chosen = pl.BlockSpec((1, step, width), lambda i, which: (which[0], i, 0))
    by_row = lambda cols: pl.BlockSpec((step, cols), lambda i, *_: (i, 0))
    return pl.pallas_call(
        feed_kernel,
        grid_spec=pltpu.PrefetchScalarGridSpec(
            num_scalar_prefetch=1,
            grid=(rows // step,),
            in_specs=[chosen, chosen, whole(up.shape), whole(upb.shape), whole(down.shape),
                      whole(gain.shape), whole(shift.shape)],
            out_specs=[by_row(width), by_row(width), by_row(units), by_row(units)],
        ),
        out_shape=[
            jax.ShapeDtypeStruct((rows, width), BF16),
            jax.ShapeDtypeStruct((rows, width), BF16),
            jax.ShapeDtypeStruct((rows, units), BF16),
            jax.ShapeDtypeStruct((rows, units), BF16),
        ],
        compiler_params=params(),
        cost_estimate=brief,
        name="feed",
    )(which, x, dy, up, upb, down, gain, shift)


def feed_grads_kernel(
    which, x_ref, dy_ref, act_ref, grad_ref, up_ref, gain_col, shift_col, *refs
):
    both_ref, vec_ref, gupb_ref, up_acc, down_acc, sum_acc, dy_acc = refs[-7:]
    step = pl.program_id(0)

    @pl.when(step == 0)
    def _():
        up_acc[...] = jnp.zeros_like(up_acc)
        down_acc[...] = jnp.zeros_like(down_acc)
        sum_acc[...] = jnp.zeros_like(sum_acc)
        dy_acc[...] = jnp.zeros_like(dy_acc)

    xhat, _ = normalise(x_ref[0].astype(F32))
    dy, grad = dy_ref[0], grad_ref[...]
    up_acc[...] += dot(xhat.astype(BF16), grad, TN)
    down_acc[...] += dot(dy, act_ref[...], TN)
    sum_acc[...] += jnp.sum(grad.astype(F32), axis=0, keepdims=True)
    dy_acc[...] += jnp.sum(dy.astype(F32), axis=0, keepdims=True)

    @pl.when(step == pl.num_programs(0) - 1)
    def _():
        sums, raw = sum_acc[...], up_acc[...]
        up = up_ref[...].astype(F32)
        units = up.shape[1]
        both_ref[:, :units] = (raw * gain_col[...] + shift_col[...] * sums).astype(both_ref.dtype)
        both_ref[:, units:] = down_acc[...].astype(both_ref.dtype)
        gupb_ref[...] = sums
        lane = lax.broadcasted_iota(jnp.int32, vec_ref.shape, 1)
        gain_grad = jnp.sum(raw * up, axis=1, keepdims=True)
        shift_grad = jnp.sum(up * sums, axis=1, keepdims=True)
        dy_col = jnp.transpose(jnp.broadcast_to(dy_acc[...], (LANES, dy_acc.shape[1])))
        vec_ref[...] = jnp.where(
            lane == 0, dy_col * 0.5,
            jnp.where(lane == 3, gain_grad, jnp.where(lane == 4, shift_grad, 0.0)),
        )


def feed_grads(which, x, dy, act, grad, up, gain_col, shift_col, after=()):
    _, rows, width = x.shape
    units = up.shape[1]
    step = min(512, rows)
    chosen = pl.BlockSpec((1, step, width), lambda i, which: (which[0], i, 0))
    by_row = pl.BlockSpec((step, units), lambda i, *_: (i, 0))
    return pl.pallas_call(
        feed_grads_kernel,
        grid_spec=pltpu.PrefetchScalarGridSpec(
            num_scalar_prefetch=1,
            grid=(rows // step,),
            in_specs=[chosen, chosen, by_row, by_row, whole(up.shape),
                      whole(gain_col.shape), whole(shift_col.shape)] + [anywhere] * len(after),
            out_specs=[whole((width, 2 * units)), whole((width, LANES)), whole((1, units))],
            scratch_shapes=[pltpu.VMEM((width, units), F32), pltpu.VMEM((width, units), F32),
                            pltpu.VMEM((1, units), F32), pltpu.VMEM((1, width), F32)],
        ),
        out_shape=[
            jax.ShapeDtypeStruct((width, 2 * units), BF16),
            jax.ShapeDtypeStruct((width, LANES), F32),
            jax.ShapeDtypeStruct((1, units), F32),
        ],
        compiler_params=params(),
        cost_estimate=long,
        name="feed_grads",
    )(which, x, dy, act, grad, up, gain_col, shift_col, *after)


def lane_fold(values, combine):
    total = values[:, :LANES]
    for j in range(1, values.shape[1] // LANES):
        total = combine(total, values[:, j * LANES : (j + 1) * LANES])
    return total


def pick_heads(both, heads):
    return [jnp.where(mine, both, jnp.zeros_like(both)) for mine in heads]


def attend_kernel(info, slots, q_ref, g_ref, dense_ref, prior_ref, *refs, block, run_rows, parts, run, ties, split):
    k_parts, v_parts, refs = refs[:parts], refs[parts : 2 * parts], refs[2 * parts + ties :]
    o_ref, stat_ref, refs = refs[0], refs[1], refs[2:]
    if split:
        send_ref, keep_ref, refs = refs[0], refs[1], refs[2:]
    else:
        sum_ref, refs = refs[0], refs[1:]
    k_ref, v_ref, score_ref, acc_ref, branch_ref = refs
    per_run = run_rows // block
    pair, place_in_run = pl.program_id(0), pl.program_id(1)
    full = info[run]

    @pl.when((pair == 0) & (place_in_run == 0))
    def _():
        branch_ref[...] = prior_ref[...].astype(F32)

    @pl.when(place_in_run == 0)
    def _():
        at = 0
        for j in range(parts):
            there = pl.ds(at, k_parts[j].shape[0])
            k_ref[there, :] = k_parts[j][...]
            v_ref[there, :] = v_parts[j][...]
            at += k_parts[j].shape[0]

    lane = lax.broadcasted_iota(jnp.int32, (block, LANES), 1)
    heads = (lane < HD, lane >= HD)

    def rows_of(at, count):
        return pl.ds(pl.multiple_of(slots[at] * run_rows, run_rows), count)

    def one_block(within):
        queries = pick_heads(q_ref[...], heads)
        seen = (within + 1) * block

        def score(at, tops, last):
            count = seen if last else run_rows
            keys = k_ref[rows_of(at, count), :]
            out = []
            for h in range(2):
                scores = dot(queries[h], keys, NT)
                if last:
                    row = lax.broadcasted_iota(jnp.int32, (block, count), 0)
                    col = lax.broadcasted_iota(jnp.int32, (block, count), 1)
                    scores = jnp.where(col <= row + within * block, scores, masked_value)
                score_ref[h, at, :, :count] = scores
                out.append(jnp.maximum(tops[h], lane_fold(scores, jnp.maximum)))
            return tuple(out)

        least = jnp.full((block, LANES), masked_value, F32)
        tops = lax.fori_loop(0, full, lambda at, carry: score(at, carry, False), (least, least))
        tops = score(full, tops, True)
        tops = [jnp.max(top, axis=1, keepdims=True) * F32(LOG2E) for top in tops]

        acc_ref[...] = jnp.zeros_like(acc_ref)

        def weigh(at, totals, last):
            count = seen if last else run_rows
            values = v_ref[rows_of(at, count), :]
            out = []
            for h in range(2):
                soft = jnp.exp2(score_ref[h, at, :, :count] * F32(LOG2E) - tops[h])
                out.append(totals[h] + lane_fold(soft, jnp.add))
                acc_ref[h] += dot(soft.astype(BF16), values, NN)
            return tuple(out)

        nought = jnp.zeros((block, LANES), F32)
        totals = lax.fori_loop(0, full, lambda at, carry: weigh(at, carry, False), (nought, nought))
        totals = weigh(full, totals, True)
        totals = [jnp.sum(total, axis=1, keepdims=True) for total in totals]
        attended = jnp.where(heads[0], acc_ref[0] / totals[0], acc_ref[1] / totals[1])
        o_ref[...] = attended.astype(o_ref.dtype)
        mine = pl.ds(within * block, block)
        branch_ref[mine, :] += dot(attended.astype(BF16), dense_ref[...], NT)
        product = attended * g_ref[...].astype(F32)
        row_terms = [jnp.sum(jnp.where(mine, product, 0.0), axis=1, keepdims=True) for mine in heads]
        logs = [tops[h] + jnp.log2(totals[h]) for h in range(2)]
        stats = jnp.where(lane == 0, logs[0], jnp.where(lane == 1, logs[1], 0.0))
        stats = jnp.where(lane == 2, row_terms[0], jnp.where(lane == 3, row_terms[1], stats))
        stat_ref[...] = jnp.transpose(stats)[:8]

    for within in range(per_run):
        pl.when(place_in_run == within)(functools.partial(one_block, within))

    @pl.when((pair == pl.num_programs(0) - 1) & (place_in_run == per_run - 1))
    def _():
        if split:
            half = run_rows // 2
            send_ref[...] = branch_ref[pl.ds(pl.multiple_of((1 - info[2]) * half, half), half), :].astype(BF16)
            keep_ref[...] = branch_ref[pl.ds(pl.multiple_of(info[2] * half, half), half), :]
        else:
            sum_ref[...] = branch_ref[...]


def attend(info, slots, q, g, kv_parts, dense, prior, run, base, after=()):
    rows, width = q.shape
    model = dense.shape[0]
    keys = sum(kv.shape[0] for kv in kv_parts)
    run_rows = rows // 2
    block = min(512, run_rows)
    per_run = run_rows // block
    pairs = kv_parts[0].shape[1] // (2 * LANES)
    split = (base + pairs) * LANES == width
    prior_row = run if prior.shape[0] == rows else 0
    by_query = pl.BlockSpec((block, LANES), lambda p, i, *_: (run * per_run + i, base + p))
    by_key = [pl.BlockSpec((kv.shape[0], LANES), lambda p, i, *_: (0, p)) for kv in kv_parts]
    by_value = [pl.BlockSpec((kv.shape[0], LANES), lambda p, i, *_: (0, pairs + p)) for kv in kv_parts]
    kernel = functools.partial(
        attend_kernel, block=block, run_rows=run_rows, parts=len(kv_parts), run=run,
        ties=len(after), split=split,
    )
    return pl.pallas_call(
        kernel,
        grid_spec=pltpu.PrefetchScalarGridSpec(
            num_scalar_prefetch=2,
            grid=(pairs, per_run),
            in_specs=[
                by_query, by_query,
                pl.BlockSpec((model, LANES), lambda p, i, *_: (0, base + p)),
                pl.BlockSpec((run_rows, model), lambda p, i, *_: (prior_row, 0)),
                *by_key, *by_value,
            ] + [anywhere] * len(after),
            out_specs=[
                pl.BlockSpec((block, LANES), lambda p, i, *_: (i, p)),
                pl.BlockSpec((8, block), lambda p, i, *_: (p, i)),
            ] + ([whole((run_rows // 2, model))] * 2 if split else [whole((run_rows, model))]),
            scratch_shapes=[
                pltpu.VMEM((keys, LANES), BF16),
                pltpu.VMEM((keys, LANES), BF16),
                pltpu.VMEM((2, keys // run_rows, block, run_rows), F32),
                pltpu.VMEM((2, block, LANES), F32),
                pltpu.VMEM((run_rows, model), F32),
            ],
        ),
        out_shape=[
            jax.ShapeDtypeStruct((run_rows, pairs * LANES), BF16),
            jax.ShapeDtypeStruct((8 * pairs, run_rows), F32),
        ] + ([
            jax.ShapeDtypeStruct((run_rows // 2, model), BF16),
            jax.ShapeDtypeStruct((run_rows // 2, model), F32),
        ] if split else [jax.ShapeDtypeStruct((run_rows, model), F32)]),
        compiler_params=params(),
        cost_estimate=brief,
        name="attend",
    )(info, slots, q, g, dense, prior, *kv_parts, *kv_parts, *after)


def attend_back_kernel(info, slots, q_ref, g_ref, stat_ref, *refs, block, run_rows, parts, home, ties):
    k_parts, v_parts, refs = refs[:parts], refs[parts : 2 * parts], refs[2 * parts + ties :]
    dq_ref, dk_out, dv_out, refs = refs[0], refs[1], refs[2], refs[3:]
    if home:
        back_ref, refs = refs[0], refs[1:]
    k_ref, v_ref, dk_ref, dv_ref, acc_ref = refs
    per_run = run_rows // block
    step = pl.program_id(0)
    full = info[step // per_run]

    @pl.when(step == 0)
    def _():
        at = 0
        for j in range(parts):
            there = pl.ds(at, k_parts[j].shape[0])
            k_ref[there, :] = k_parts[j][...]
            v_ref[there, :] = v_parts[j][...]
            at += k_parts[j].shape[0]
        dk_ref[...] = jnp.zeros_like(dk_ref)
        dv_ref[...] = jnp.zeros_like(dv_ref)

    lane = lax.broadcasted_iota(jnp.int32, (block, LANES), 1)
    heads = (lane < HD, lane >= HD)

    def rows_of(at, count):
        return pl.ds(pl.multiple_of(slots[at] * run_rows, run_rows), count)

    def one_block(within):
        queries, grads = pick_heads(q_ref[...], heads), pick_heads(g_ref[...], heads)
        stats = jnp.transpose(stat_ref[...])
        logs, row_terms = [stats[:, h : h + 1] for h in range(2)], [stats[:, 2 + h : 3 + h] for h in range(2)]
        seen = (within + 1) * block
        acc_ref[...] = jnp.zeros_like(acc_ref)

        def back(at, last):
            count = seen if last else run_rows
            there = rows_of(at, count)
            keys, values = k_ref[there, :], v_ref[there, :]
            key_terms, value_terms = [], []
            for h in range(2):
                soft = jnp.exp2(dot(queries[h], keys, NT) * F32(LOG2E) - logs[h])
                if last:
                    row = lax.broadcasted_iota(jnp.int32, (block, count), 0)
                    col = lax.broadcasted_iota(jnp.int32, (block, count), 1)
                    soft = jnp.where(col <= row + within * block, soft, 0.0)
                grad_soft = dot(grads[h], values, NT)
                grad_score = (soft * (grad_soft - row_terms[h])).astype(BF16)
                acc_ref[h] += dot(grad_score, keys, NN)
                key_terms.append(dot(grad_score, queries[h], TN))
                value_terms.append(dot(soft.astype(BF16), grads[h], TN))
            dk_ref[there, :] += key_terms[0] + key_terms[1]
            dv_ref[there, :] += value_terms[0] + value_terms[1]

        def back_whole(at, carry):
            back(at, False)
            return carry

        lax.fori_loop(0, full, back_whole, 0)
        back(full, True)
        dq_ref[...] = (jnp.where(heads[0], acc_ref[0], acc_ref[1]) * F32(HD**-0.5)).astype(dq_ref.dtype)

    for within in range(per_run):
        pl.when(step % per_run == within)(functools.partial(one_block, within))

    @pl.when(step == pl.num_programs(0) - 1)
    def _():
        own = dk_out.shape[0]
        dk_out[...] = dk_ref[:own, :]
        dv_out[...] = dv_ref[:own, :]
        if home:
            back_ref[:, :LANES] = dk_ref[home:, :].astype(BF16)
            back_ref[:, LANES:] = dv_ref[home:, :].astype(BF16)


def attend_back(info, slots, q, g, stats, kv_parts, pair, at, home, after=()):
    rows, width = q.shape
    keys = sum(kv.shape[0] for kv in kv_parts)
    run_rows = rows // 2
    block = min(512, run_rows)
    pairs = kv_parts[0].shape[1] // (2 * LANES)
    own = home or keys
    by_query = pl.BlockSpec((block, LANES), lambda i, *_: (i, pair))
    by_key = [pl.BlockSpec((kv.shape[0], LANES), lambda i, *_: (0, at)) for kv in kv_parts]
    by_value = [pl.BlockSpec((kv.shape[0], LANES), lambda i, *_: (0, pairs + at)) for kv in kv_parts]
    kernel = functools.partial(
        attend_back_kernel, block=block, run_rows=run_rows, parts=len(kv_parts), home=home, ties=len(after)
    )
    out_specs = [pl.BlockSpec((block, LANES), lambda i, *_: (i, 0)), whole((own, LANES)), whole((own, LANES))]
    out_shape = [
        jax.ShapeDtypeStruct((rows, LANES), BF16),
        jax.ShapeDtypeStruct((own, LANES), F32),
        jax.ShapeDtypeStruct((own, LANES), F32),
    ]
    if home:
        out_specs.append(whole((keys - home, 2 * LANES)))
        out_shape.append(jax.ShapeDtypeStruct((keys - home, 2 * LANES), BF16))
    return pl.pallas_call(
        kernel,
        grid_spec=pltpu.PrefetchScalarGridSpec(
            num_scalar_prefetch=2,
            grid=(rows // block,),
            in_specs=[by_query, by_query, pl.BlockSpec((8, block), lambda i, *_: (pair, i)), *by_key, *by_value]
            + [anywhere] * len(after),
            out_specs=out_specs,
            scratch_shapes=[
                pltpu.VMEM((keys, LANES), BF16),
                pltpu.VMEM((keys, LANES), BF16),
                pltpu.VMEM((keys, LANES), F32),
                pltpu.VMEM((keys, LANES), F32),
                pltpu.VMEM((2, block, LANES), F32),
            ],
        ),
        out_shape=out_shape,
        compiler_params=params(),
        cost_estimate=long,
        name="attend_back",
    )(info, slots, q, g, stats, *kv_parts, *kv_parts, *after)


def back_kernel(which, dq_ref, *refs, pairs):
    own_k, refs = refs[:pairs], refs[pairs:]
    own_v, refs = refs[:pairs], refs[pairs:]
    got, refs = refs[:pairs], refs[pairs:]
    w_ref, gain_ref, dx_in, cos_ref, low_ref, high_ref = refs[:6]
    dproj_ref, send_ref, keep_ref = refs[-3:]
    half = dq_ref.shape[1]
    cosines, low, high = cos_ref[...], low_ref[...], high_ref[...]
    for j in range(pairs):
        at = slice(j * LANES, (j + 1) * LANES)
        query = dq_ref[:, at].astype(F32)
        dproj_ref[:, at] = turn(query, cosines, -low, -high).astype(BF16)
        key = own_k[j][...] + got[j][:, :LANES].astype(F32)
        dproj_ref[:, half + j * LANES : half + (j + 1) * LANES] = turn(key, cosines, -low, -high).astype(BF16)
        value = own_v[j][...] + got[j][:, LANES:].astype(F32)
        dproj_ref[:, 2 * half + j * LANES : 2 * half + (j + 1) * LANES] = value.astype(BF16)
    summed = dot(dproj_ref[...], w_ref[...], NT) * gain_ref[...] + dx_in[...].astype(F32)
    mine = pl.program_id(0) % 2 == which[1]

    @pl.when(mine)
    def _():
        keep_ref[...] = summed

    @pl.when(jnp.logical_not(mine))
    def _():
        send_ref[...] = summed.astype(send_ref.dtype)


def back(which, dq, dk, dv, got, w, gain, dx_part, tables, after=()):
    rows, half = dq.shape
    width = w.shape[0]
    step = rows // 4
    pairs = len(dk)
    by_row = lambda cols: pl.BlockSpec((step, cols), lambda i, *_: (i, 0))
    by_run = pl.BlockSpec((step, width), lambda i, *_: (i // 2, 0))
    return pl.pallas_call(
        functools.partial(back_kernel, pairs=pairs),
        grid_spec=pltpu.PrefetchScalarGridSpec(
            num_scalar_prefetch=1,
            grid=(4,),
            in_specs=[by_row(half)] + [by_row(LANES)] * (2 * pairs) + [by_row(2 * LANES)] * pairs
            + [whole(w.shape), whole(gain.shape), by_row(width)] + [by_row(LANES)] * 3
            + [anywhere] * len(after),
            out_specs=[by_row(3 * half), by_run, by_run],
        ),
        out_shape=[
            jax.ShapeDtypeStruct((rows, 3 * half), BF16),
            jax.ShapeDtypeStruct((rows // 2, width), BF16),
            jax.ShapeDtypeStruct((rows // 2, width), F32),
        ],
        compiler_params=params(),
        cost_estimate=brief,
        name="back",
    )(which, dq, *dk, *dv, *got, w, gain, dx_part, *tables, *after)


def weight_kernel(
    which, x_ref, dy_ref, dproj_ref, o_ref, w_ref, gain_col, shift_col, *refs
):
    gqkv_ref, gdense_ref, vec_ref, gb_ref, acc, dense_acc, sum_acc = refs[-7:]
    step = pl.program_id(0)

    @pl.when(step == 0)
    def _():
        acc[...] = jnp.zeros_like(acc)
        dense_acc[...] = jnp.zeros_like(dense_acc)
        sum_acc[...] = jnp.zeros_like(sum_acc)

    xhat, _ = normalise(x_ref[0].astype(F32))
    dproj = dproj_ref[...]
    acc[...] += dot(xhat.astype(BF16), dproj, TN)
    dense_acc[...] += dot(dy_ref[0], o_ref[...], TN)
    sum_acc[...] += jnp.sum(dproj.astype(F32), axis=0, keepdims=True)

    @pl.when(step == pl.num_programs(0) - 1)
    def _():
        sums, raw, w = sum_acc[...], acc[...], w_ref[...].astype(F32)
        gqkv_ref[...] = (raw * gain_col[...] + shift_col[...] * sums).astype(gqkv_ref.dtype)
        gdense_ref[...] = dense_acc[...].astype(gdense_ref.dtype)
        gb_ref[...] = sums
        lane = lax.broadcasted_iota(jnp.int32, vec_ref.shape, 1)
        gain_grad = jnp.sum(raw * w, axis=1, keepdims=True)
        shift_grad = jnp.sum(w * sums, axis=1, keepdims=True)
        vec_ref[...] = jnp.where(lane == 1, gain_grad, jnp.where(lane == 2, shift_grad, 0.0))


def weight_grads(which, x, dy, dproj, o, w, gain_col, shift_col, after=()):
    _, rows, width = x.shape
    half = o.shape[1]
    step = min(512, rows)
    chosen = pl.BlockSpec((1, step, width), lambda i, which: (which[0], i, 0))
    by_row = lambda cols: pl.BlockSpec((step, cols), lambda i, *_: (i, 0))
    return pl.pallas_call(
        weight_kernel,
        grid_spec=pltpu.PrefetchScalarGridSpec(
            num_scalar_prefetch=1,
            grid=(rows // step,),
            in_specs=[chosen, chosen, by_row(3 * half), by_row(half), whole(w.shape),
                      whole(gain_col.shape), whole(shift_col.shape)] + [anywhere] * len(after),
            out_specs=[whole((width, 3 * half)), whole((width, half)), whole((width, LANES)), whole((1, 3 * half))],
            scratch_shapes=[pltpu.VMEM((width, 3 * half), F32), pltpu.VMEM((width, half), F32),
                            pltpu.VMEM((1, 3 * half), F32)],
        ),
        out_shape=[
            jax.ShapeDtypeStruct((width, 3 * half), BF16),
            jax.ShapeDtypeStruct((width, half), BF16),
            jax.ShapeDtypeStruct((width, LANES), F32),
            jax.ShapeDtypeStruct((1, 3 * half), F32),
        ],
        compiler_params=params(),
        cost_estimate=long,
        name="weight_grads",
    )(which, x, dy, dproj, o, w, gain_col, shift_col, *after)


def join_kernel(*refs):
    out = refs[-1]
    at = 0
    for ref in refs[:-1]:
        out[:, at : at + ref.shape[1]] = ref[...]
        at += ref.shape[1]


def join(arrays):
    rows = arrays[0].shape[0]
    step = rows // 4
    widths = [array.shape[1] for array in arrays]
    by_row = lambda cols: pl.BlockSpec((step, cols), lambda i: (i, 0))
    return pl.pallas_call(
        join_kernel,
        grid=(4,),
        in_specs=[by_row(width) for width in widths],
        out_specs=by_row(sum(widths)),
        out_shape=jax.ShapeDtypeStruct((rows, sum(widths)), BF16),
        compiler_params=params(),
        cost_estimate=brief,
        name="join",
    )(*arrays)


def norm_back_kernel(which, x_ref, dy_ref, kept_ref, got_ref, *refs):
    out_ref = refs[-1]
    xhat, scale = normalise(x_ref[0].astype(F32))
    grad = kept_ref[...].astype(F32) + got_ref[...].astype(F32)
    centre = jnp.mean(grad, axis=-1, keepdims=True)
    along = jnp.mean(grad * xhat, axis=-1, keepdims=True)
    out_ref[...] = (dy_ref[0].astype(F32) + scale * (grad - centre - xhat * along)).astype(out_ref.dtype)


def norm_back(which, x, dy, kept, got, run, after=()):
    rows, width = got.shape
    step = min(256, rows)
    blocks = rows // step
    chosen = pl.BlockSpec(
        (1, step, width), lambda i, which: (which[0], (2 * run + which[1]) * blocks + i, 0)
    )
    return pl.pallas_call(
        norm_back_kernel,
        grid_spec=pltpu.PrefetchScalarGridSpec(
            num_scalar_prefetch=1,
            grid=(blocks,),
            in_specs=[chosen, chosen,
                      pl.BlockSpec((step, width), lambda i, *_: (run * blocks + i, 0)),
                      pl.BlockSpec((step, width), lambda i, *_: (i, 0))] + [anywhere] * len(after),
            out_specs=pl.BlockSpec((step, width), lambda i, *_: (i, 0)),
        ),
        out_shape=jax.ShapeDtypeStruct((rows, width), BF16),
        compiler_params=params(),
        cost_estimate=longest,
        name="norm_back",
    )(which, x, dy, kept, got, *after)


def finish_kernel(which, x_ref, kept_ref, got_ref, one_ref, two_ref, *refs):
    summed = kept_ref[...] + got_ref[...].astype(F32) + x_ref[0].astype(F32) + one_ref[...] + two_ref[...]
    refs[-1][...] = summed.astype(BF16)


def finish(which, x, kept, got, one, two, run, after=()):
    rows, width = got.shape
    step = min(256, rows)
    blocks = rows // step
    by_row = pl.BlockSpec((step, width), lambda i, *_: (i, 0))
    return pl.pallas_call(
        finish_kernel,
        grid_spec=pltpu.PrefetchScalarGridSpec(
            num_scalar_prefetch=1,
            grid=(blocks,),
            in_specs=[
                pl.BlockSpec((1, step, width), lambda i, which: (which[0], (2 * run + which[1]) * blocks + i, 0)),
                by_row, by_row, whole(one.shape), whole(two.shape),
            ] + [anywhere] * len(after),
            out_specs=by_row,
        ),
        out_shape=jax.ShapeDtypeStruct((rows, width), BF16),
        compiler_params=params(),
        cost_estimate=brief,
        name="finish",
    )(which, x, kept, got, one, two, *after)


def lay_kernel(early_ref, late_ref, *refs):
    out = refs[-1]
    run = pl.program_id(0) % 2

    @pl.when(run == 0)
    def _():
        out[0] = early_ref[...]

    @pl.when(run == 1)
    def _():
        out[0] = late_ref[...]


def lay_gathered(early, late, after=()):
    rows, width = early.shape[0] // 2, early.shape[1]
    half = pl.BlockSpec((rows, width), lambda i: (i // 2, 0))
    return pl.pallas_call(
        lay_kernel,
        grid=(4,),
        in_specs=[half, half] + [anywhere] * len(after),
        out_specs=pl.BlockSpec((1, rows, width), lambda i: (i // 2, i % 2, 0)),
        out_shape=jax.ShapeDtypeStruct((2, 2 * rows, width), BF16),
        compiler_params=params(),
        cost_estimate=brief,
        name="lay_gathered",
    )(early, late, *after)


def lay_round_kernel(index, *refs):
    out = refs[-1]
    run, slot = pl.program_id(0) // 4, pl.program_id(0) % 4
    back = (index[0] + 4 - slot) % 4
    for j in range(8):

        @pl.when((run == j // 4) & (back == j % 4))
        def _(j=j):
            out[0] = refs[j][...]


def lay_round(index, early, late):
    half, width = early[0].shape
    return pl.pallas_call(
        lay_round_kernel,
        grid_spec=pltpu.PrefetchScalarGridSpec(
            num_scalar_prefetch=1,
            grid=(8,),
            in_specs=[whole((half, width))] * 8,
            out_specs=pl.BlockSpec((1, half, width), lambda i, *_: ((i % 4) // 2, 2 * (i // 4) + i % 2, 0)),
        ),
        out_shape=jax.ShapeDtypeStruct((2, 4 * half, width), BF16),
        compiler_params=params(),
        cost_estimate=brief,
        name="lay_round",
    )(index[None], *early, *late)


def swap(values, axis):
    return lax.ppermute(values, axis, [(0, 1), (1, 0)])


def across(values, bit):
    return lax.ppermute(values, "dp", [(i, i ^ bit) for i in range(4)])


def gather_half(values, seq_first):
    values = jnp.concatenate([values[None], swap(values, "mh")[None]], axis=0)
    steps = [lambda v: swap(v, "seq"), lambda v: across(v, 2)]
    for step in steps if seq_first else steps[::-1]:
        values = jnp.concatenate([values, step(values)], axis=0)
    values = jnp.concatenate([values, across(values, 1)], axis=0)
    return values.reshape(8, 2, *values.shape[1:])


def round_mp(mine):
    axes = ("mh", "ml")
    return [mine] + [lax.ppermute(mine, axes, [(i, (i + k) % 4) for i in range(4)]) for k in (1, 2, 3)]


def rotation_tables(positions):
    half = ROT // 2
    frequency = jnp.power(F32(10000.0), -2.0 * jnp.arange(half, dtype=F32) / ROT)
    angles = frequency[:, None] * positions.astype(F32)[None, :]
    cosines, sines = lax.optimization_barrier((jnp.cos(angles), jnp.sin(angles)))
    cosines, sines = cosines.T, sines.T
    rows = positions.shape[0]
    rest = jnp.zeros((rows, HD - ROT), F32)
    blank = jnp.zeros((rows, half), F32)
    per_head = (
        jnp.concatenate([cosines, cosines, rest + 1.0], axis=1),
        jnp.concatenate([-sines, blank, rest], axis=1),
        jnp.concatenate([blank, sines, rest], axis=1),
    )
    return tuple(jnp.tile(table, (1, LANES // HD)) for table in per_head)


def body(
    tokens, places, w_qkv, b_qkv, w_dense, b_dense, w_up, b_up, w_down, b_down,
    norm1_gain, norm1_bias, norm2_gain, norm2_bias, out_grad, *, seq_size, owners,
):
    _, rows, width = tokens.shape
    share = width // owners
    heads = b_qkv.shape[1]
    cols = heads * HD
    units = w_up.shape[1]
    side, part = lax.axis_index("mh"), lax.axis_index("ml")
    index = (2 * side + part).astype(jnp.int32)
    owner = lax.axis_index("dp") * seq_size + lax.axis_index("seq")
    which = jnp.stack([side, part]).astype(jnp.int32)
    where = jnp.stack([side, owner]).astype(jnp.int32)

    run_rows = rows // 2
    held = places[:, ::run_rows] // run_rows

    def column(vector):
        vector = vector.reshape(-1)
        return jnp.pad(vector, (0, share - vector.shape[0]))[:, None]

    small = jnp.concatenate(
        [column(v) for v in (b_dense, b_down, norm1_gain, norm1_bias, norm2_gain, norm2_bias, b_qkv, b_up,
                            held.astype(BF16))],
        axis=1,
    )
    small = jnp.pad(small, ((0, 0), (0, LANES - small.shape[1])))
    one = w_qkv[:2].transpose(1, 0, 2).reshape(share, 2 * cols)
    two = jnp.concatenate([w_qkv[2], w_dense.T, small], axis=1)
    three, four = w_up, w_down.T
    first_widths = (6 * cols, 2 * cols, 2 * LANES)
    if owners == 8 and seq_size == 2:
        one, two = gather_half(one, True), gather_half(two, False)
        qkv_w, dense_w, small = place(place_first_kernel, where, one, two, first_widths, (BF16, BF16, F32))
        pack = lax.all_gather(jnp.concatenate([three, four], axis=1), ("dp", "seq", "mh"), axis=0, tiled=True)
        up_w, down_w = place_second(pack.reshape(owners, 2, share, 2 * units))
    else:

        def gather(values):
            values = lax.all_gather(values, ("dp", "seq", "mh"), axis=0, tiled=True)
            return values.reshape(owners, 2, share, -1).transpose(0, 2, 1, 3).reshape(width, 2, -1)

        one, two, three, four = gather(one), gather(two), gather(three), gather(four)
        qkv_w = jnp.concatenate([one[:, :, :cols], one[:, :, cols:], two[:, :, :cols]], axis=1)
        qkv_w, dense_w = qkv_w.reshape(width, 6 * cols), two[:, :, cols : 2 * cols].reshape(width, 2 * cols)
        small = two[:, :, 2 * cols :].reshape(width, 2 * LANES).astype(F32)
        up_w, down_w = three.reshape(width, 2 * units), four.reshape(width, 2 * units)
    vectors = small[:, :8]
    piece = HD // owners
    biases = small.reshape(owners, share, 2, LANES)
    qkv_b = biases[:, : 3 * heads * piece, :, 6].reshape(owners, 3, heads, piece, 2)
    qkv_b = qkv_b.transpose(1, 4, 2, 0, 3).reshape(1, 6 * cols)
    up_rows, up_cols = b_up.shape
    up_b = biases[..., 7].reshape(owners, up_rows, up_cols, 2).transpose(3, 1, 0, 2).reshape(1, 2 * units)
    by_row = vectors.T
    row_of = lambda at: by_row[at].reshape(1, width)
    column_of = lambda at: vectors[:, at].reshape(width, 1)

    my_places = lax.dynamic_index_in_dim(places, side, 0, keepdims=False)
    runs = lax.dynamic_index_in_dim(held, side, 0, keepdims=False)
    if owners == 8 and seq_size == 2:
        other = lax.dynamic_slice(small, ((owner ^ 1) * share + 2 * side, 8), (2, 1))[:, 0]
        all_runs = jnp.concatenate([runs, (other + 0.5).astype(jnp.int32)])
    elif seq_size == 2:
        all_runs = jnp.concatenate([runs, swap(runs, "seq")])
    else:
        all_runs = lax.all_gather(runs, "seq", axis=0, tiled=True)
    order = jnp.arange(2 * seq_size, dtype=jnp.int32)
    slots = jnp.sum(jnp.where(all_runs[None, :] == order[:, None], order[None, :], 0), axis=1)
    tables = rotation_tables(my_places)

    q, kv_most, kv_last, grad_o = front(
        which, tokens, out_grad, qkv_w, qkv_b, dense_w, row_of(2), row_of(3), tables
    )
    if seq_size == 2:
        kv_most, kv_last = (kv_most, swap(kv_most, "seq")), (kv_last, swap(kv_last, "seq"))
    else:
        kv_most = (lax.all_gather(kv_most, "seq", axis=0, tiled=True),)
        kv_last = (lax.all_gather(kv_last, "seq", axis=0, tiled=True),)
    pairs = q.shape[1] // LANES
    mlp_part, mlp_dx, act, mlp_grad = feed(which, tokens, out_grad, up_w, up_b, down_w, row_of(4), row_of(5))
    info = jnp.concatenate([runs, which[1:]])
    quarter = rows // 4

    def forward(kv_parts, prior, run, base, after):
        return attend(info, slots, q, grad_o, kv_parts, dense_w, prior, run, base, after)

    o_most_early, stat_most_early, summed_early = forward(kv_most, mlp_part, 0, 0, ())
    o_most_late, stat_most_late, summed_late = forward(kv_most, mlp_part, 1, 0, (o_most_early,))
    o_last_early, stat_last_early, send, keep_early = forward(kv_last, summed_early, 0, pairs - 1, (o_most_late,))
    got_early = swap(send, "ml")
    o_last_late, stat_last_late, send, keep_late = forward(kv_last, summed_late, 1, pairs - 1, (o_last_early,))
    got_late = swap(send, "ml")
    stats = jnp.concatenate(
        [
            jnp.concatenate([stat_most_early, stat_last_early], axis=0),
            jnp.concatenate([stat_most_late, stat_last_late], axis=0),
        ],
        axis=1,
    )
    attended = jnp.concatenate(
        [
            jnp.concatenate([o_most_early, o_last_early], axis=1),
            jnp.concatenate([o_most_late, o_last_late], axis=1),
        ],
        axis=0,
    )
    mixed_early = finish(which, tokens, keep_early, got_early, row_of(0), row_of(1), 0, (o_last_late,))
    after = (mixed_early,)
    mixed_early = lax.all_gather(mixed_early, ("mh", "ml"), axis=0, tiled=True)

    home = rows if seq_size == 2 else 0
    dq, dk, dv, got = [], [], [], []
    for pair in range(pairs):
        kv_parts, at = (kv_last, 0) if pair == pairs - 1 else (kv_most, pair)
        outs = attend_back(info, slots, q, grad_o, stats, kv_parts, pair, at, home, after)
        after = (outs[0],)
        dq.append(outs[0])
        if home:
            dk.append(outs[1])
            dv.append(outs[2])
            got.append(swap(outs[3], "seq"))
        else:
            both = jnp.concatenate([outs[1], outs[2]], axis=1).astype(BF16)
            got.append(lax.psum_scatter(both, "seq", scatter_dimension=0, tiled=True))
            dk.append(jnp.zeros((rows, LANES), F32))
            dv.append(jnp.zeros((rows, LANES), F32))
        if pair == 1:
            mixed_late = finish(which, tokens, keep_late, got_late, row_of(0), row_of(1), 1, (outs[0], got[0]))
            after = (outs[0], mixed_late)
            mixed_late = lax.all_gather(mixed_late, ("mh", "ml"), axis=0, tiled=True)
        elif pair > 1:
            after = (outs[0], got[pair - 1])
    feed_weights, mlp_vectors, grad_up_b = feed_grads(
        which, tokens, out_grad, act, mlp_grad, up_w, column_of(4), column_of(5), after + (mixed_early,)
    )
    dq = jnp.concatenate(dq, axis=1)
    dproj, send, keep = back(
        which, dq, dk, dv, got, qkv_w, row_of(2), mlp_dx, tables, (grad_up_b,)
    )
    mixed = lay_gathered(mixed_early, mixed_late, (dproj,))
    got = [swap(send[run * quarter : (run + 1) * quarter], "ml") for run in range(2)]
    grad_qkv, grad_dense, qkv_vectors, grad_qkv_b = weight_grads(
        which, tokens, out_grad, dproj, attended, qkv_w, column_of(2), column_of(3), (mixed_late,)
    )
    ties = ((grad_qkv_b,), (grad_qkv_b,))
    input_grad = [norm_back(which, tokens, out_grad, keep, got[run], run, ties[run]) for run in range(2)]
    input_grad = lay_round(index, *[round_mp(rows_done) for rows_done in input_grad])

    def scatter(grads):
        return lax.psum_scatter(grads, ("dp", "seq"), scatter_dimension=0, tiled=True)

    def settle(sums):
        sums = sums.astype(F32)
        mine = lax.dynamic_index_in_dim(sums, side, 1, keepdims=False)
        other = lax.dynamic_index_in_dim(sums, 1 - side, 1, keepdims=False)
        return mine + swap(other.astype(BF16), "mh").astype(F32)

    vector_grads = (mlp_vectors + qkv_vectors)[:, None, :5]
    vector_grads = jnp.broadcast_to(vector_grads, (width, 2, 5))
    bias_qkv = grad_qkv_b.reshape(3, 2, heads, owners, piece).transpose(3, 0, 2, 4, 1)
    bias_qkv = bias_qkv.reshape(owners, 3 * heads * piece, 2)
    bias_qkv = jnp.pad(bias_qkv, ((0, 0), (0, share - 3 * heads * piece), (0, 0))).reshape(width, 2, 1)
    bias_up = grad_up_b.reshape(2, up_rows, owners, up_cols).transpose(2, 1, 3, 0).reshape(width, 2, 1)
    tail = jnp.concatenate([vector_grads, bias_qkv, bias_up], axis=2)
    tail = jnp.pad(tail, ((0, 0), (0, 0), (0, LANES // 2 - 7))).astype(BF16).reshape(width, LANES)
    packed = scatter(join((grad_qkv, grad_dense, tail, feed_weights)))
    first, owned_feed = packed[:, : 8 * cols + LANES], packed[:, 8 * cols + LANES :]
    owned_feed = owned_feed.reshape(share, 2, 2, units).transpose(0, 2, 1, 3).reshape(share, 2, 2 * units)
    owned_qkv = first[:, : 6 * cols].reshape(share, 3, 2, cols).transpose(0, 2, 1, 3).reshape(share, 2, 3 * cols)
    owned_dense = first[:, 6 * cols : 8 * cols].reshape(share, 2, cols)
    owned_tail = first[:, 8 * cols :].reshape(share, 2, LANES // 2)
    owned = settle(jnp.concatenate([owned_feed, owned_qkv, owned_dense, owned_tail], axis=2))
    owned_feed, owned = owned[:, : 2 * units], owned[:, 2 * units :]
    vectors = owned[:, 4 * cols :]
    norms = vectors[:, :5]
    norms = norms + swap(norms, "ml")
    bias_grad = norms[:, 0]
    return (
        mixed,
        input_grad,
        owned[:, : 3 * cols].reshape(share, 3, cols).transpose(1, 0, 2),
        vectors[: 3 * heads * piece, 5].reshape(b_qkv.shape),
        owned[:, 3 * cols : 4 * cols].T,
        bias_grad,
        owned_feed[:, :units],
        vectors[:, 6].reshape(b_up.shape),
        owned_feed[:, units:].T,
        bias_grad,
        norms[:, 1],
        norms[:, 2],
        norms[:, 3],
        norms[:, 4],
    )


def solution(mesh):
    dp, seq, mp = (mesh.shape[axis] for axis in ("dp", "seq", "mp"))
    split = Mesh(mesh.devices.reshape(dp, seq, 2, mp // 2), ("dp", "seq", "mh", "ml"))
    mp, owner = ("mh", "ml"), ("dp", "seq")
    row = P("dp", "seq", None)
    vector = P(owner)
    weights = (
        P(None, owner, mp), P(None, mp, owner), P(mp, owner), vector, P(owner, mp), P(mp, owner),
        P(mp, owner), vector, vector, vector, vector, vector,
    )
    return jax.shard_map(
        functools.partial(body, seq_size=seq, owners=dp * seq),
        mesh=split,
        in_specs=(row, P("dp", "seq")) + weights + (row,),
        out_specs=(row, row) + weights,
        check_vma=False,
    )
```

```python
import functools

import jax
import jax.numpy as jnp
from jax import lax
from jax.experimental import pallas as pl
from jax.experimental.pallas import tpu as pltpu
from jax.sharding import Mesh
from jax.sharding import PartitionSpec as P

HD = 64
ROT = 16
LANES = 128
F32 = jnp.float32
BF16 = jnp.bfloat16
LOG2E = 1.4426950408889634
norm_eps = 1e-05
masked_value = -1e30
vmem_bytes = 60 * 2**20
brief = pl.CostEstimate(flops=1, bytes_accessed=1, transcendentals=0)
long = pl.CostEstimate(flops=2**33, bytes_accessed=2**24, transcendentals=0)

NN = (((1,), (0,)), ((), ()))
NT = (((1,), (1,)), ((), ()))
TN = (((0,), (0,)), ((), ()))


def dot(left, right, dims):
    return lax.dot_general(left, right, dims, preferred_element_type=F32)


def normalise(rows):
    centre = jnp.mean(rows, axis=-1, keepdims=True)
    deviate = rows - centre
    spread = jnp.mean(deviate * deviate, axis=-1, keepdims=True)
    scale = lax.rsqrt(spread + norm_eps)
    return deviate * scale, scale


def turn(chunk, cosines, sine_low, sine_high):
    half = ROT // 2
    return (
        chunk * cosines
        + pltpu.roll(chunk, LANES - half, 1) * sine_low
        + pltpu.roll(chunk, half, 1) * sine_high
    )

longest = pl.CostEstimate(flops=2**36, bytes_accessed=2**27, transcendentals=0)


anywhere = pl.BlockSpec(memory_space=pl.ANY)


def whole(shape):
    return pl.BlockSpec(shape, lambda *_: (0,) * len(shape))


def params(**kwargs):
    return pltpu.CompilerParams(vmem_limit_bytes=vmem_bytes, **kwargs)


def place_first_kernel(where, one_ref, two_ref, qkv_ref, dense_ref, small_ref):
    cols = one_ref.shape[-1] // 2
    share = one_ref.shape[2]
    near = where[0] == 0
    for i in range(4):
        bits = (pl.program_id(0) * 4 + i) ^ where[1]
        upper, lower, across = bits // 4, (bits // 2) % 2, bits % 2
        one = [one_ref[lower * 4 + upper * 2 + across, j] for j in range(2)]
        two = [two_ref[lower * 4 + across * 2 + upper, j] for j in range(2)]
        one = (jnp.where(near, one[0], one[1]), jnp.where(near, one[1], one[0]))
        two = (jnp.where(near, two[0], two[1]), jnp.where(near, two[1], two[0]))
        pieces = [one[j][:, at * cols : (at + 1) * cols] for at in range(2) for j in range(2)]
        pieces += [two[j][:, :cols] for j in range(2)]
        rows = slice(i * share, (i + 1) * share)
        qkv_ref[rows, :] = jnp.concatenate(pieces, axis=1)
        dense_ref[rows, :] = jnp.concatenate([two[j][:, cols : 2 * cols] for j in range(2)], axis=1)
        small_ref[rows, :] = jnp.concatenate([two[j][:, 2 * cols :] for j in range(2)], axis=1).astype(F32)


def place_second_kernel(pack_ref, up_ref, down_ref):
    units = pack_ref.shape[-1] // 2
    share = pack_ref.shape[2]
    for i in range(2):
        rows = slice(i * share, (i + 1) * share)
        for j in range(2):
            up_ref[rows, j * units : (j + 1) * units] = pack_ref[i, j, :, :units]
            down_ref[rows, j * units : (j + 1) * units] = pack_ref[i, j, :, units:]


def place_second(pack):
    owners, _, share, width = pack.shape
    return pl.pallas_call(
        place_second_kernel,
        grid=(owners // 2,),
        in_specs=[pl.BlockSpec((2,) + pack.shape[1:], lambda i: (i, 0, 0, 0))],
        out_specs=[pl.BlockSpec((2 * share, width), lambda i: (i, 0))] * 2,
        out_shape=[jax.ShapeDtypeStruct((owners * share, width), BF16)] * 2,
        compiler_params=params(),
        cost_estimate=brief,
        name="place_second",
    )(pack)


def place_first(where, one, two, widths, types):
    owners, _, share, _ = one.shape
    return pl.pallas_call(
        place_first_kernel,
        grid_spec=pltpu.PrefetchScalarGridSpec(
            num_scalar_prefetch=1,
            grid=(owners // 4,),
            in_specs=[whole(one.shape), whole(two.shape)],
            out_specs=[pl.BlockSpec((4 * share, width), lambda i, *_: (i, 0)) for width in widths],
        ),
        out_shape=[jax.ShapeDtypeStruct((owners * share, width), kind) for width, kind in zip(widths, types)],
        compiler_params=params(),
        cost_estimate=brief,
        name="place_first",
    )(where, one, two)


def front_kernel(
    which, x_ref, dy_ref, w_ref, wb_ref, dense_ref, gain_ref, shift_ref, cos_ref, low_ref, high_ref,
    q_ref, kv_most, kv_last, do_ref,
):
    half = q_ref.shape[1]
    most = kv_most.shape[1] // 2
    xhat, _ = normalise(x_ref[0].astype(F32))
    normed = (xhat * gain_ref[...] + shift_ref[...]).astype(BF16)
    proj = dot(normed, w_ref[...], NN) + wb_ref[...]
    cosines, low, high = cos_ref[...], low_ref[...], high_ref[...]
    for j in range(half // LANES):
        at = slice(j * LANES, (j + 1) * LANES)
        query = turn(proj[:, at], cosines, low, high).astype(BF16)
        q_ref[:, at] = query * BF16(HD**-0.5)
        key = turn(proj[:, half + j * LANES : half + (j + 1) * LANES], cosines, low, high).astype(BF16)
        if j * LANES < most:
            kv_most[:, at] = key
        else:
            kv_last[:, :LANES] = key
    kv_most[:, most:] = proj[:, 2 * half : 2 * half + most].astype(BF16)
    kv_last[:, LANES:] = proj[:, 2 * half + most :].astype(BF16)
    do_ref[...] = dot(dy_ref[0], dense_ref[...], NN).astype(BF16)


def front(which, x, dy, w, wb, dense, gain, shift, tables):
    _, rows, width = x.shape
    half = dense.shape[1]
    step = min(512, rows)
    chosen = pl.BlockSpec((1, step, width), lambda i, which: (which[0], i, 0))
    by_row = lambda cols: pl.BlockSpec((step, cols), lambda i, *_: (i, 0))
    return pl.pallas_call(
        front_kernel,
        grid_spec=pltpu.PrefetchScalarGridSpec(
            num_scalar_prefetch=1,
            grid=(rows // step,),
            in_specs=[chosen, chosen, whole(w.shape), whole(wb.shape), whole(dense.shape),
                      whole(gain.shape), whole(shift.shape)] + [by_row(LANES)] * 3,
            out_specs=[by_row(half), by_row(2 * half - 2 * LANES), by_row(2 * LANES), by_row(half)],
        ),
        out_shape=[
            jax.ShapeDtypeStruct((rows, half), BF16),
            jax.ShapeDtypeStruct((rows, 2 * half - 2 * LANES), BF16),
            jax.ShapeDtypeStruct((rows, 2 * LANES), BF16),
            jax.ShapeDtypeStruct((rows, half), BF16),
        ],
        compiler_params=params(),
        cost_estimate=brief,
        name="front",
    )(which, x, dy, w, wb, dense, gain, shift, *tables)


def feed_kernel(
    which, x_ref, dy_ref, up_ref, upb_ref, down_ref, gain_ref, shift_ref, part_ref, dx_ref, act_ref, grad_ref
):
    xhat, _ = normalise(x_ref[0].astype(F32))
    normed = (xhat * gain_ref[...] + shift_ref[...]).astype(BF16)
    hidden = dot(normed, up_ref[...], NN) + upb_ref[...]
    share = 0.5 * (1.0 + lax.erf(hidden * F32(0.5**0.5)))
    act = (hidden * share).astype(BF16)
    act_ref[...] = act
    slope = share + hidden * (jnp.exp(hidden * hidden * -0.5) * F32(0.3989422804014327))
    part_ref[...] = dot(act, down_ref[...], NT).astype(part_ref.dtype)
    grad_low = (dot(dy_ref[0], down_ref[...], NN) * slope).astype(BF16)
    grad_ref[...] = grad_low
    dx_ref[...] = (dot(grad_low, up_ref[...], NT) * gain_ref[...]).astype(dx_ref.dtype)


def feed(which, x, dy, up, upb, down, gain, shift):
    _, rows, width = x.shape
    units = up.shape[1]
    step = min(256, rows)
    chosen = pl.BlockSpec((1, step, width), lambda i, which: (which[0], i, 0))
    by_row = lambda cols: pl.BlockSpec((step, cols), lambda i, *_: (i, 0))
    return pl.pallas_call(
        feed_kernel,
        grid_spec=pltpu.PrefetchScalarGridSpec(
            num_scalar_prefetch=1,
            grid=(rows // step,),
            in_specs=[chosen, chosen, whole(up.shape), whole(upb.shape), whole(down.shape),
                      whole(gain.shape), whole(shift.shape)],
            out_specs=[by_row(width), by_row(width), by_row(units), by_row(units)],
        ),
        out_shape=[
            jax.ShapeDtypeStruct((rows, width), BF16),
            jax.ShapeDtypeStruct((rows, width), BF16),
            jax.ShapeDtypeStruct((rows, units), BF16),
            jax.ShapeDtypeStruct((rows, units), BF16),
        ],
        compiler_params=params(),
        cost_estimate=brief,
        name="feed",
    )(which, x, dy, up, upb, down, gain, shift)


def feed_grads_kernel(
    which, x_ref, dy_ref, act_ref, grad_ref, up_ref, gain_col, shift_col, *refs
):
    both_ref, vec_ref, gupb_ref, up_acc, down_acc, sum_acc, dy_acc = refs[-7:]
    step = pl.program_id(0)

    @pl.when(step == 0)
    def _():
        up_acc[...] = jnp.zeros_like(up_acc)
        down_acc[...] = jnp.zeros_like(down_acc)
        sum_acc[...] = jnp.zeros_like(sum_acc)
        dy_acc[...] = jnp.zeros_like(dy_acc)

    xhat, _ = normalise(x_ref[0].astype(F32))
    dy, grad = dy_ref[0], grad_ref[...]
    up_acc[...] += dot(xhat.astype(BF16), grad, TN)
    down_acc[...] += dot(dy, act_ref[...], TN)
    sum_acc[...] += jnp.sum(grad.astype(F32), axis=0, keepdims=True)
    dy_acc[...] += jnp.sum(dy.astype(F32), axis=0, keepdims=True)

    @pl.when(step == pl.num_programs(0) - 1)
    def _():
        sums, raw = sum_acc[...], up_acc[...]
        up = up_ref[...].astype(F32)
        units = up.shape[1]
        both_ref[:, :units] = (raw * gain_col[...] + shift_col[...] * sums).astype(both_ref.dtype)
        both_ref[:, units:] = down_acc[...].astype(both_ref.dtype)
        gupb_ref[...] = sums
        lane = lax.broadcasted_iota(jnp.int32, vec_ref.shape, 1)
        gain_grad = jnp.sum(raw * up, axis=1, keepdims=True)
        shift_grad = jnp.sum(up * sums, axis=1, keepdims=True)
        dy_col = jnp.transpose(jnp.broadcast_to(dy_acc[...], (LANES, dy_acc.shape[1])))
        vec_ref[...] = jnp.where(
            lane == 0, dy_col * 0.5,
            jnp.where(lane == 3, gain_grad, jnp.where(lane == 4, shift_grad, 0.0)),
        )


def feed_grads(which, x, dy, act, grad, up, gain_col, shift_col, after=()):
    _, rows, width = x.shape
    units = up.shape[1]
    step = min(512, rows)
    chosen = pl.BlockSpec((1, step, width), lambda i, which: (which[0], i, 0))
    by_row = pl.BlockSpec((step, units), lambda i, *_: (i, 0))
    return pl.pallas_call(
        feed_grads_kernel,
        grid_spec=pltpu.PrefetchScalarGridSpec(
            num_scalar_prefetch=1,
            grid=(rows // step,),
            in_specs=[chosen, chosen, by_row, by_row, whole(up.shape),
                      whole(gain_col.shape), whole(shift_col.shape)] + [anywhere] * len(after),
            out_specs=[whole((width, 2 * units)), whole((width, LANES)), whole((1, units))],
            scratch_shapes=[pltpu.VMEM((width, units), F32), pltpu.VMEM((width, units), F32),
                            pltpu.VMEM((1, units), F32), pltpu.VMEM((1, width), F32)],
        ),
        out_shape=[
            jax.ShapeDtypeStruct((width, 2 * units), BF16),
            jax.ShapeDtypeStruct((width, LANES), F32),
            jax.ShapeDtypeStruct((1, units), F32),
        ],
        compiler_params=params(),
        cost_estimate=long,
        name="feed_grads",
    )(which, x, dy, act, grad, up, gain_col, shift_col, *after)


def lane_fold(values, combine):
    total = values[:, :LANES]
    for j in range(1, values.shape[1] // LANES):
        total = combine(total, values[:, j * LANES : (j + 1) * LANES])
    return total


def pick_heads(both, heads):
    return [jnp.where(mine, both, jnp.zeros_like(both)) for mine in heads]


def head_lanes(rows):
    lane = lax.broadcasted_iota(jnp.int32, (rows, LANES), 1)
    return lane < HD, lane >= HD


def tiles(block, last):
    half = block // 2
    if last and block >= 512:
        return (0, 0, half), (half, half, half)
    return ((0, 0, block),)


def visible(shape):
    return lax.broadcasted_iota(jnp.int32, shape, 1) <= lax.broadcasted_iota(jnp.int32, shape, 0)


def merge(whole_rows, row, part, combine):
    if row == 0:
        return combine(whole_rows, part)
    return jnp.concatenate([whole_rows[:row], combine(whole_rows[row:], part)], axis=0)


def attend_kernel(info, slots, q_ref, g_ref, dense_ref, prior_ref, *refs, block, parts, run, ties, split):
    k_parts, v_parts, refs = refs[:parts], refs[parts : 2 * parts], refs[2 * parts + ties :]
    o_ref, stat_ref, refs = refs[0], refs[1], refs[2:]
    if split:
        send_ref, keep_ref, refs = refs[0], refs[1], refs[2:]
    else:
        sum_ref, refs = refs[0], refs[1:]
    k_ref, v_ref, score_ref, acc_ref, branch_ref = refs
    pair = pl.program_id(0)
    full = info[run]

    @pl.when(pair == 0)
    def _():
        branch_ref[...] = prior_ref[...].astype(F32)

    at = 0
    for j in range(parts):
        there = pl.ds(at, k_parts[j].shape[0])
        k_ref[there, :] = k_parts[j][...]
        v_ref[there, :] = v_parts[j][...]
        at += k_parts[j].shape[0]

    heads = head_lanes(block)
    queries = pick_heads(q_ref[...], heads)

    def rows_of(at, col, count):
        return pl.ds(pl.multiple_of(slots[at] * block + col, count), count)

    def score(at, tops, last):
        out = []
        for h in range(2):
            top = tops[h]
            for row, col, count in tiles(block, last):
                scores = dot(queries[h][row:], k_ref[rows_of(at, col, count), :], NT)
                if last:
                    scores = jnp.where(visible(scores.shape), scores, masked_value)
                score_ref[h, at, row:, col : col + count] = scores
                top = merge(top, row, lane_fold(scores, jnp.maximum), jnp.maximum)
            out.append(top)
        return tuple(out)

    least = jnp.full((block, LANES), masked_value, F32)
    tops = lax.fori_loop(0, full, lambda at, carry: score(at, carry, False), (least, least))
    tops = score(full, tops, True)
    tops = [jnp.max(top, axis=1, keepdims=True) * F32(LOG2E) for top in tops]

    acc_ref[...] = jnp.zeros_like(acc_ref)

    def weigh(at, totals, last):
        out = []
        for h in range(2):
            total = totals[h]
            for row, col, count in tiles(block, last):
                values = v_ref[rows_of(at, col, count), :]
                soft = jnp.exp2(score_ref[h, at, row:, col : col + count] * F32(LOG2E) - tops[h][row:])
                total = merge(total, row, lane_fold(soft, jnp.add), jnp.add)
                acc_ref[h, row:, :] += dot(soft.astype(BF16), values, NN)
            out.append(total)
        return tuple(out)

    nought = jnp.zeros((block, LANES), F32)
    totals = lax.fori_loop(0, full, lambda at, carry: weigh(at, carry, False), (nought, nought))
    totals = weigh(full, totals, True)
    totals = [jnp.sum(total, axis=1, keepdims=True) for total in totals]
    attended = jnp.where(heads[0], acc_ref[0] / totals[0], acc_ref[1] / totals[1])
    o_ref[...] = attended.astype(o_ref.dtype)
    branch_ref[...] += dot(attended.astype(BF16), dense_ref[...], NT)
    product = attended * g_ref[...].astype(F32)
    row_terms = [jnp.sum(jnp.where(mine, product, 0.0), axis=1, keepdims=True) for mine in heads]
    logs = [tops[h] + jnp.log2(totals[h]) for h in range(2)]
    lane = lax.broadcasted_iota(jnp.int32, (block, LANES), 1)
    stats = jnp.where(lane == 0, logs[0], jnp.where(lane == 1, logs[1], 0.0))
    stats = jnp.where(lane == 2, row_terms[0], jnp.where(lane == 3, row_terms[1], stats))
    stat_ref[...] = jnp.transpose(stats)[:8]

    @pl.when(pair == pl.num_programs(0) - 1)
    def _():
        if split:
            half = block // 2
            send_ref[...] = branch_ref[pl.ds(pl.multiple_of((1 - info[2]) * half, half), half), :].astype(BF16)
            keep_ref[...] = branch_ref[pl.ds(pl.multiple_of(info[2] * half, half), half), :]
        else:
            sum_ref[...] = branch_ref[...]


def attend(info, slots, q, g, kv_parts, dense, prior, run, base, after=()):
    rows, width = q.shape
    model = dense.shape[0]
    keys = sum(kv.shape[0] for kv in kv_parts)
    run_rows = rows // 2
    block = run_rows
    pairs = kv_parts[0].shape[1] // (2 * LANES)
    split = (base + pairs) * LANES == width
    prior_row = run if prior.shape[0] == rows else 0
    by_query = pl.BlockSpec((block, LANES), lambda p, *_: (run, base + p))
    by_key = [pl.BlockSpec((kv.shape[0], LANES), lambda p, *_: (0, p)) for kv in kv_parts]
    by_value = [pl.BlockSpec((kv.shape[0], LANES), lambda p, *_: (0, pairs + p)) for kv in kv_parts]
    kernel = functools.partial(
        attend_kernel, block=block, parts=len(kv_parts), run=run,
        ties=len(after), split=split,
    )
    return pl.pallas_call(
        kernel,
        grid_spec=pltpu.PrefetchScalarGridSpec(
            num_scalar_prefetch=2,
            grid=(pairs,),
            in_specs=[
                by_query, by_query,
                pl.BlockSpec((model, LANES), lambda p, *_: (0, base + p)),
                pl.BlockSpec((run_rows, model), lambda p, *_: (prior_row, 0)),
                *by_key, *by_value,
            ] + [anywhere] * len(after),
            out_specs=[
                pl.BlockSpec((block, LANES), lambda p, *_: (0, p)),
                pl.BlockSpec((8, block), lambda p, *_: (p, 0)),
            ] + ([whole((run_rows // 2, model))] * 2 if split else [whole((run_rows, model))]),
            scratch_shapes=[
                pltpu.VMEM((keys, LANES), BF16),
                pltpu.VMEM((keys, LANES), BF16),
                pltpu.VMEM((2, keys // run_rows, block, run_rows), F32),
                pltpu.VMEM((2, block, LANES), F32),
                pltpu.VMEM((run_rows, model), F32),
            ],
        ),
        out_shape=[
            jax.ShapeDtypeStruct((run_rows, pairs * LANES), BF16),
            jax.ShapeDtypeStruct((8 * pairs, run_rows), F32),
        ] + ([
            jax.ShapeDtypeStruct((run_rows // 2, model), BF16),
            jax.ShapeDtypeStruct((run_rows // 2, model), F32),
        ] if split else [jax.ShapeDtypeStruct((run_rows, model), F32)]),
        compiler_params=params(),
        cost_estimate=brief,
        name="attend",
    )(info, slots, q, g, dense, prior, *kv_parts, *kv_parts, *after)


def attend_back_kernel(info, slots, q_ref, g_ref, stat_ref, *refs, block, parts, home, ties):
    k_parts, v_parts, refs = refs[:parts], refs[parts : 2 * parts], refs[2 * parts + ties :]
    dq_ref, dk_out, dv_out, refs = refs[0], refs[1], refs[2], refs[3:]
    if home:
        back_ref, refs = refs[0], refs[1:]
    k_ref, v_ref, dk_ref, dv_ref, acc_ref = refs
    step = pl.program_id(0)
    full = info[step]

    @pl.when(step == 0)
    def _():
        at = 0
        for j in range(parts):
            there = pl.ds(at, k_parts[j].shape[0])
            k_ref[there, :] = k_parts[j][...]
            v_ref[there, :] = v_parts[j][...]
            at += k_parts[j].shape[0]
        dk_ref[...] = jnp.zeros_like(dk_ref)
        dv_ref[...] = jnp.zeros_like(dv_ref)

    heads = head_lanes(block)
    queries, grads = pick_heads(q_ref[...], heads), pick_heads(g_ref[...], heads)
    stats = jnp.transpose(stat_ref[...])
    logs, row_terms = [stats[:, h : h + 1] for h in range(2)], [stats[:, 2 + h : 3 + h] for h in range(2)]
    acc_ref[...] = jnp.zeros_like(acc_ref)

    def back(at, last):
        for row, col, count in tiles(block, last):
            there = pl.ds(pl.multiple_of(slots[at] * block + col, count), count)
            keys, values = k_ref[there, :], v_ref[there, :]
            key_terms, value_terms = [], []
            for h in range(2):
                query, grad = queries[h][row:], grads[h][row:]
                soft = jnp.exp2(dot(query, keys, NT) * F32(LOG2E) - logs[h][row:])
                if last:
                    soft = jnp.where(visible(soft.shape), soft, 0.0)
                grad_soft = dot(grad, values, NT)
                grad_score = (soft * (grad_soft - row_terms[h][row:])).astype(BF16)
                acc_ref[h, row:, :] += dot(grad_score, keys, NN)
                key_terms.append(dot(grad_score, query, TN))
                value_terms.append(dot(soft.astype(BF16), grad, TN))
            dk_ref[there, :] += key_terms[0] + key_terms[1]
            dv_ref[there, :] += value_terms[0] + value_terms[1]

    def back_whole(at, carry):
        back(at, False)
        return carry

    lax.fori_loop(0, full, back_whole, 0)
    back(full, True)
    dq_ref[...] = (jnp.where(heads[0], acc_ref[0], acc_ref[1]) * F32(HD**-0.5)).astype(dq_ref.dtype)

    @pl.when(step == pl.num_programs(0) - 1)
    def _():
        own = dk_out.shape[0]
        dk_out[...] = dk_ref[:own, :]
        dv_out[...] = dv_ref[:own, :]
        if home:
            back_ref[:, :LANES] = dk_ref[home:, :].astype(BF16)
            back_ref[:, LANES:] = dv_ref[home:, :].astype(BF16)


def attend_back(info, slots, q, g, stats, kv_parts, pair, at, home, after=()):
    rows, width = q.shape
    keys = sum(kv.shape[0] for kv in kv_parts)
    run_rows = rows // 2
    block = run_rows
    pairs = kv_parts[0].shape[1] // (2 * LANES)
    own = home or keys
    by_query = pl.BlockSpec((block, LANES), lambda i, *_: (i, pair))
    by_key = [pl.BlockSpec((kv.shape[0], LANES), lambda i, *_: (0, at)) for kv in kv_parts]
    by_value = [pl.BlockSpec((kv.shape[0], LANES), lambda i, *_: (0, pairs + at)) for kv in kv_parts]
    kernel = functools.partial(
        attend_back_kernel, block=block, parts=len(kv_parts), home=home, ties=len(after)
    )
    out_specs = [pl.BlockSpec((block, LANES), lambda i, *_: (i, 0)), whole((own, LANES)), whole((own, LANES))]
    out_shape = [
        jax.ShapeDtypeStruct((rows, LANES), BF16),
        jax.ShapeDtypeStruct((own, LANES), F32),
        jax.ShapeDtypeStruct((own, LANES), F32),
    ]
    if home:
        out_specs.append(whole((keys - home, 2 * LANES)))
        out_shape.append(jax.ShapeDtypeStruct((keys - home, 2 * LANES), BF16))
    return pl.pallas_call(
        kernel,
        grid_spec=pltpu.PrefetchScalarGridSpec(
            num_scalar_prefetch=2,
            grid=(rows // block,),
            in_specs=[by_query, by_query, pl.BlockSpec((8, block), lambda i, *_: (pair, i)), *by_key, *by_value]
            + [anywhere] * len(after),
            out_specs=out_specs,
            scratch_shapes=[
                pltpu.VMEM((keys, LANES), BF16),
                pltpu.VMEM((keys, LANES), BF16),
                pltpu.VMEM((keys, LANES), F32),
                pltpu.VMEM((keys, LANES), F32),
                pltpu.VMEM((2, block, LANES), F32),
            ],
        ),
        out_shape=out_shape,
        compiler_params=params(),
        cost_estimate=long,
        name="attend_back",
    )(info, slots, q, g, stats, *kv_parts, *kv_parts, *after)


def back_kernel(which, dq_ref, *refs, pairs):
    own_k, refs = refs[:pairs], refs[pairs:]
    own_v, refs = refs[:pairs], refs[pairs:]
    got, refs = refs[:pairs], refs[pairs:]
    w_ref, gain_ref, dx_in, cos_ref, low_ref, high_ref = refs[:6]
    dproj_ref, send_ref, keep_ref = refs[-3:]
    half = dq_ref.shape[1]
    cosines, low, high = cos_ref[...], low_ref[...], high_ref[...]
    for j in range(pairs):
        at = slice(j * LANES, (j + 1) * LANES)
        query = dq_ref[:, at].astype(F32)
        dproj_ref[:, at] = turn(query, cosines, -low, -high).astype(BF16)
        key = own_k[j][...] + got[j][:, :LANES].astype(F32)
        dproj_ref[:, half + j * LANES : half + (j + 1) * LANES] = turn(key, cosines, -low, -high).astype(BF16)
        value = own_v[j][...] + got[j][:, LANES:].astype(F32)
        dproj_ref[:, 2 * half + j * LANES : 2 * half + (j + 1) * LANES] = value.astype(BF16)
    summed = dot(dproj_ref[...], w_ref[...], NT) * gain_ref[...] + dx_in[...].astype(F32)
    mine = pl.program_id(0) % 2 == which[1]

    @pl.when(mine)
    def _():
        keep_ref[...] = summed

    @pl.when(jnp.logical_not(mine))
    def _():
        send_ref[...] = summed.astype(send_ref.dtype)


def back(which, dq, dk, dv, got, w, gain, dx_part, tables, after=()):
    rows, half = dq.shape
    width = w.shape[0]
    step = rows // 4
    pairs = len(dk)
    by_row = lambda cols: pl.BlockSpec((step, cols), lambda i, *_: (i, 0))
    by_run = pl.BlockSpec((step, width), lambda i, *_: (i // 2, 0))
    return pl.pallas_call(
        functools.partial(back_kernel, pairs=pairs),
        grid_spec=pltpu.PrefetchScalarGridSpec(
            num_scalar_prefetch=1,
            grid=(4,),
            in_specs=[by_row(half)] + [by_row(LANES)] * (2 * pairs) + [by_row(2 * LANES)] * pairs
            + [whole(w.shape), whole(gain.shape), by_row(width)] + [by_row(LANES)] * 3
            + [anywhere] * len(after),
            out_specs=[by_row(3 * half), by_run, by_run],
        ),
        out_shape=[
            jax.ShapeDtypeStruct((rows, 3 * half), BF16),
            jax.ShapeDtypeStruct((rows // 2, width), BF16),
            jax.ShapeDtypeStruct((rows // 2, width), F32),
        ],
        compiler_params=params(),
        cost_estimate=brief,
        name="back",
    )(which, dq, *dk, *dv, *got, w, gain, dx_part, *tables, *after)


def weight_kernel(
    which, x_ref, dy_ref, dproj_ref, o_ref, w_ref, gain_col, shift_col, *refs
):
    gqkv_ref, gdense_ref, vec_ref, gb_ref, acc, dense_acc, sum_acc = refs[-7:]
    step = pl.program_id(0)

    @pl.when(step == 0)
    def _():
        acc[...] = jnp.zeros_like(acc)
        dense_acc[...] = jnp.zeros_like(dense_acc)
        sum_acc[...] = jnp.zeros_like(sum_acc)

    xhat, _ = normalise(x_ref[0].astype(F32))
    dproj = dproj_ref[...]
    acc[...] += dot(xhat.astype(BF16), dproj, TN)
    dense_acc[...] += dot(dy_ref[0], o_ref[...], TN)
    sum_acc[...] += jnp.sum(dproj.astype(F32), axis=0, keepdims=True)

    @pl.when(step == pl.num_programs(0) - 1)
    def _():
        sums, raw, w = sum_acc[...], acc[...], w_ref[...].astype(F32)
        gqkv_ref[...] = (raw * gain_col[...] + shift_col[...] * sums).astype(gqkv_ref.dtype)
        gdense_ref[...] = dense_acc[...].astype(gdense_ref.dtype)
        gb_ref[...] = sums
        lane = lax.broadcasted_iota(jnp.int32, vec_ref.shape, 1)
        gain_grad = jnp.sum(raw * w, axis=1, keepdims=True)
        shift_grad = jnp.sum(w * sums, axis=1, keepdims=True)
        vec_ref[...] = jnp.where(lane == 1, gain_grad, jnp.where(lane == 2, shift_grad, 0.0))


def weight_grads(which, x, dy, dproj, o, w, gain_col, shift_col, after=()):
    _, rows, width = x.shape
    half = o.shape[1]
    step = min(512, rows)
    chosen = pl.BlockSpec((1, step, width), lambda i, which: (which[0], i, 0))
    by_row = lambda cols: pl.BlockSpec((step, cols), lambda i, *_: (i, 0))
    return pl.pallas_call(
        weight_kernel,
        grid_spec=pltpu.PrefetchScalarGridSpec(
            num_scalar_prefetch=1,
            grid=(rows // step,),
            in_specs=[chosen, chosen, by_row(3 * half), by_row(half), whole(w.shape),
                      whole(gain_col.shape), whole(shift_col.shape)] + [anywhere] * len(after),
            out_specs=[whole((width, 3 * half)), whole((width, half)), whole((width, LANES)), whole((1, 3 * half))],
            scratch_shapes=[pltpu.VMEM((width, 3 * half), F32), pltpu.VMEM((width, half), F32),
                            pltpu.VMEM((1, 3 * half), F32)],
        ),
        out_shape=[
            jax.ShapeDtypeStruct((width, 3 * half), BF16),
            jax.ShapeDtypeStruct((width, half), BF16),
            jax.ShapeDtypeStruct((width, LANES), F32),
            jax.ShapeDtypeStruct((1, 3 * half), F32),
        ],
        compiler_params=params(),
        cost_estimate=long,
        name="weight_grads",
    )(which, x, dy, dproj, o, w, gain_col, shift_col, *after)


def join_kernel(*refs):
    out = refs[-1]
    at = 0
    for ref in refs[:-1]:
        out[:, at : at + ref.shape[1]] = ref[...]
        at += ref.shape[1]


def join(arrays):
    rows = arrays[0].shape[0]
    step = rows // 4
    widths = [array.shape[1] for array in arrays]
    by_row = lambda cols: pl.BlockSpec((step, cols), lambda i: (i, 0))
    return pl.pallas_call(
        join_kernel,
        grid=(4,),
        in_specs=[by_row(width) for width in widths],
        out_specs=by_row(sum(widths)),
        out_shape=jax.ShapeDtypeStruct((rows, sum(widths)), BF16),
        compiler_params=params(),
        cost_estimate=brief,
        name="join",
    )(*arrays)


def norm_back_kernel(which, x_ref, dy_ref, kept_ref, got_ref, *refs):
    out_ref = refs[-1]
    xhat, scale = normalise(x_ref[0].astype(F32))
    grad = kept_ref[...].astype(F32) + got_ref[...].astype(F32)
    centre = jnp.mean(grad, axis=-1, keepdims=True)
    along = jnp.mean(grad * xhat, axis=-1, keepdims=True)
    out_ref[...] = (dy_ref[0].astype(F32) + scale * (grad - centre - xhat * along)).astype(out_ref.dtype)


def norm_back(which, x, dy, kept, got, run, after=()):
    rows, width = got.shape
    step = min(256, rows)
    blocks = rows // step
    chosen = pl.BlockSpec(
        (1, step, width), lambda i, which: (which[0], (2 * run + which[1]) * blocks + i, 0)
    )
    return pl.pallas_call(
        norm_back_kernel,
        grid_spec=pltpu.PrefetchScalarGridSpec(
            num_scalar_prefetch=1,
            grid=(blocks,),
            in_specs=[chosen, chosen,
                      pl.BlockSpec((step, width), lambda i, *_: (run * blocks + i, 0)),
                      pl.BlockSpec((step, width), lambda i, *_: (i, 0))] + [anywhere] * len(after),
            out_specs=pl.BlockSpec((step, width), lambda i, *_: (i, 0)),
        ),
        out_shape=jax.ShapeDtypeStruct((rows, width), BF16),
        compiler_params=params(),
        cost_estimate=longest,
        name="norm_back",
    )(which, x, dy, kept, got, *after)


def finish_kernel(which, x_ref, kept_ref, got_ref, one_ref, two_ref, *refs):
    summed = kept_ref[...] + got_ref[...].astype(F32) + x_ref[0].astype(F32) + one_ref[...] + two_ref[...]
    refs[-1][...] = summed.astype(BF16)


def finish(which, x, kept, got, one, two, run, after=()):
    rows, width = got.shape
    step = min(256, rows)
    blocks = rows // step
    by_row = pl.BlockSpec((step, width), lambda i, *_: (i, 0))
    return pl.pallas_call(
        finish_kernel,
        grid_spec=pltpu.PrefetchScalarGridSpec(
            num_scalar_prefetch=1,
            grid=(blocks,),
            in_specs=[
                pl.BlockSpec((1, step, width), lambda i, which: (which[0], (2 * run + which[1]) * blocks + i, 0)),
                by_row, by_row, whole(one.shape), whole(two.shape),
            ] + [anywhere] * len(after),
            out_specs=by_row,
        ),
        out_shape=jax.ShapeDtypeStruct((rows, width), BF16),
        compiler_params=params(),
        cost_estimate=brief,
        name="finish",
    )(which, x, kept, got, one, two, *after)


def lay_kernel(early_ref, late_ref, *refs):
    out = refs[-1]
    run = pl.program_id(0) % 2

    @pl.when(run == 0)
    def _():
        out[0] = early_ref[...]

    @pl.when(run == 1)
    def _():
        out[0] = late_ref[...]


def lay_gathered(early, late, after=()):
    rows, width = early.shape[0] // 2, early.shape[1]
    half = pl.BlockSpec((rows, width), lambda i: (i // 2, 0))
    return pl.pallas_call(
        lay_kernel,
        grid=(4,),
        in_specs=[half, half] + [anywhere] * len(after),
        out_specs=pl.BlockSpec((1, rows, width), lambda i: (i // 2, i % 2, 0)),
        out_shape=jax.ShapeDtypeStruct((2, 2 * rows, width), BF16),
        compiler_params=params(),
        cost_estimate=brief,
        name="lay_gathered",
    )(early, late, *after)


STEPS = (0, 1, 2, 3, -1, -2, -3)


def lay_line_kernel(index, *refs):
    out = refs[-1]
    run, slot = pl.program_id(0) // 4, pl.program_id(0) % 4
    for j in range(2 * len(STEPS)):

        @pl.when((run == j // len(STEPS)) & (index[0] - slot == STEPS[j % len(STEPS)]))
        def _(j=j):
            out[0] = refs[j][...]


def lay_line(index, early, late):
    half, width = early[0].shape
    return pl.pallas_call(
        lay_line_kernel,
        grid_spec=pltpu.PrefetchScalarGridSpec(
            num_scalar_prefetch=1,
            grid=(8,),
            in_specs=[whole((half, width))] * 14,
            out_specs=pl.BlockSpec((1, half, width), lambda i, *_: ((i % 4) // 2, 2 * (i // 4) + i % 2, 0)),
        ),
        out_shape=jax.ShapeDtypeStruct((2, 4 * half, width), BF16),
        compiler_params=params(),
        cost_estimate=brief,
        name="lay_line",
    )(index[None], *early, *late)


def sides_kernel(which, sums_ref, *refs, segments):
    keep_ref, send_ref = refs[-2:]
    near = which[0] == 0
    at = out = 0
    for cols in segments:
        one, two = sums_ref[:, at : at + cols], sums_ref[:, at + cols : at + 2 * cols]
        keep_ref[:, out : out + cols] = jnp.where(near, one, two)
        send_ref[:, out : out + cols] = jnp.where(near, two, one)
        at, out = at + 2 * cols, out + cols


def sides(which, sums, segments, after):
    rows = sums.shape[0]
    half = sum(segments)
    return pl.pallas_call(
        functools.partial(sides_kernel, segments=segments),
        grid_spec=pltpu.PrefetchScalarGridSpec(
            num_scalar_prefetch=1,
            grid=(1,),
            in_specs=[whole(sums.shape)] + [anywhere] * len(after),
            out_specs=[whole((rows, half))] * 2,
        ),
        out_shape=[jax.ShapeDtypeStruct((rows, half), BF16)] * 2,
        compiler_params=params(),
        cost_estimate=brief,
        name="sides",
    )(which, sums, *after)


def swap(values, axis):
    return lax.ppermute(values, axis, [(0, 1), (1, 0)])


def across(values, bit):
    return lax.ppermute(values, "dp", [(i, i ^ bit) for i in range(4)])


def gather_half(values, seq_first):
    values = jnp.concatenate([values[None], swap(values, "mh")[None]], axis=0)
    steps = [lambda v: swap(v, "seq"), lambda v: across(v, 2)]
    for step in steps if seq_first else steps[::-1]:
        values = jnp.concatenate([values, step(values)], axis=0)
    values = jnp.concatenate([values, across(values, 1)], axis=0)
    return values.reshape(8, 2, *values.shape[1:])


def line_mp(mine):
    axes = ("mh", "ml")
    before, behind = [mine], [mine]
    for _ in range(3):
        before.append(lax.ppermute(before[-1], axes, [(i, i + 1) for i in range(3)]))
        behind.append(lax.ppermute(behind[-1], axes, [(i + 1, i) for i in range(3)]))
    return before + behind[1:]


def rotation_tables(positions):
    half = ROT // 2
    frequency = jnp.power(F32(10000.0), -2.0 * jnp.arange(half, dtype=F32) / ROT)
    angles = frequency[:, None] * positions.astype(F32)[None, :]
    cosines, sines = lax.optimization_barrier((jnp.cos(angles), jnp.sin(angles)))
    cosines, sines = cosines.T, sines.T
    rows = positions.shape[0]
    rest = jnp.zeros((rows, HD - ROT), F32)
    blank = jnp.zeros((rows, half), F32)
    per_head = (
        jnp.concatenate([cosines, cosines, rest + 1.0], axis=1),
        jnp.concatenate([-sines, blank, rest], axis=1),
        jnp.concatenate([blank, sines, rest], axis=1),
    )
    return tuple(jnp.tile(table, (1, LANES // HD)) for table in per_head)


def body(
    tokens, places, w_qkv, b_qkv, w_dense, b_dense, w_up, b_up, w_down, b_down,
    norm1_gain, norm1_bias, norm2_gain, norm2_bias, out_grad, *, seq_size, owners,
):
    _, rows, width = tokens.shape
    share = width // owners
    heads = b_qkv.shape[1]
    cols = heads * HD
    units = w_up.shape[1]
    side, part = lax.axis_index("mh"), lax.axis_index("ml")
    index = (2 * side + part).astype(jnp.int32)
    owner = lax.axis_index("dp") * seq_size + lax.axis_index("seq")
    which = jnp.stack([side, part]).astype(jnp.int32)
    where = jnp.stack([side, owner]).astype(jnp.int32)

    run_rows = rows // 2
    held = places[:, ::run_rows] // run_rows

    def column(vector):
        vector = vector.reshape(-1)
        return jnp.pad(vector, (0, share - vector.shape[0]))[:, None]

    small = jnp.concatenate(
        [column(v) for v in (b_dense, b_down, norm1_gain, norm1_bias, norm2_gain, norm2_bias, b_qkv, b_up,
                            held.astype(BF16))],
        axis=1,
    )
    small = jnp.pad(small, ((0, 0), (0, LANES - small.shape[1])))
    one = w_qkv[:2].transpose(1, 0, 2).reshape(share, 2 * cols)
    two = jnp.concatenate([w_qkv[2], w_dense.T, small], axis=1)
    three, four = w_up, w_down.T
    first_widths = (6 * cols, 2 * cols, 2 * LANES)
    if owners == 8 and seq_size == 2:
        one, two = gather_half(one, True), gather_half(two, False)
        qkv_w, dense_w, small = place_first(where, one, two, first_widths, (BF16, BF16, F32))
        pack = lax.all_gather(jnp.concatenate([three, four], axis=1), ("dp", "seq", "mh"), axis=0, tiled=True)
        up_w, down_w = place_second(pack.reshape(owners, 2, share, 2 * units))
    else:

        def gather(values):
            values = lax.all_gather(values, ("dp", "seq", "mh"), axis=0, tiled=True)
            return values.reshape(owners, 2, share, -1).transpose(0, 2, 1, 3).reshape(width, 2, -1)

        one, two, three, four = gather(one), gather(two), gather(three), gather(four)
        qkv_w = jnp.concatenate([one[:, :, :cols], one[:, :, cols:], two[:, :, :cols]], axis=1)
        qkv_w, dense_w = qkv_w.reshape(width, 6 * cols), two[:, :, cols : 2 * cols].reshape(width, 2 * cols)
        small = two[:, :, 2 * cols :].reshape(width, 2 * LANES).astype(F32)
        up_w, down_w = three.reshape(width, 2 * units), four.reshape(width, 2 * units)
    vectors = small[:, :8]
    piece = HD // owners
    biases = small.reshape(owners, share, 2, LANES)
    qkv_b = biases[:, : 3 * heads * piece, :, 6].reshape(owners, 3, heads, piece, 2)
    qkv_b = qkv_b.transpose(1, 4, 2, 0, 3).reshape(1, 6 * cols)
    up_rows, up_cols = b_up.shape
    up_b = biases[..., 7].reshape(owners, up_rows, up_cols, 2).transpose(3, 1, 0, 2).reshape(1, 2 * units)
    by_row = vectors.T
    row_of = lambda at: by_row[at].reshape(1, width)
    column_of = lambda at: vectors[:, at].reshape(width, 1)

    my_places = lax.dynamic_index_in_dim(places, side, 0, keepdims=False)
    runs = lax.dynamic_index_in_dim(held, side, 0, keepdims=False)
    if owners == 8 and seq_size == 2:
        other = lax.dynamic_slice(small, ((owner ^ 1) * share + 2 * side, 8), (2, 1))[:, 0]
        all_runs = jnp.concatenate([runs, (other + 0.5).astype(jnp.int32)])
    elif seq_size == 2:
        all_runs = jnp.concatenate([runs, swap(runs, "seq")])
    else:
        all_runs = lax.all_gather(runs, "seq", axis=0, tiled=True)
    order = jnp.arange(2 * seq_size, dtype=jnp.int32)
    slots = jnp.sum(jnp.where(all_runs[None, :] == order[:, None], order[None, :], 0), axis=1)
    tables = rotation_tables(my_places)

    q, kv_most, kv_last, grad_o = front(
        which, tokens, out_grad, qkv_w, qkv_b, dense_w, row_of(2), row_of(3), tables
    )
    if seq_size == 2:
        kv_most, kv_last = (kv_most, swap(kv_most, "seq")), (kv_last, swap(kv_last, "seq"))
    else:
        kv_most = (lax.all_gather(kv_most, "seq", axis=0, tiled=True),)
        kv_last = (lax.all_gather(kv_last, "seq", axis=0, tiled=True),)
    pairs = q.shape[1] // LANES
    mlp_part, mlp_dx, act, mlp_grad = feed(which, tokens, out_grad, up_w, up_b, down_w, row_of(4), row_of(5))
    info = jnp.concatenate([runs, which[1:]])
    quarter = rows // 4

    def forward(kv_parts, prior, run, base, after):
        return attend(info, slots, q, grad_o, kv_parts, dense_w, prior, run, base, after)

    o_most_early, stat_most_early, summed_early = forward(kv_most, mlp_part, 0, 0, ())
    o_most_late, stat_most_late, summed_late = forward(kv_most, mlp_part, 1, 0, (o_most_early,))
    o_last_early, stat_last_early, send, keep_early = forward(kv_last, summed_early, 0, pairs - 1, (o_most_late,))
    got_early = swap(send, "ml")
    o_last_late, stat_last_late, send, keep_late = forward(kv_last, summed_late, 1, pairs - 1, (o_last_early,))
    got_late = swap(send, "ml")
    stats = jnp.concatenate(
        [
            jnp.concatenate([stat_most_early, stat_last_early], axis=0),
            jnp.concatenate([stat_most_late, stat_last_late], axis=0),
        ],
        axis=1,
    )
    attended = jnp.concatenate(
        [
            jnp.concatenate([o_most_early, o_last_early], axis=1),
            jnp.concatenate([o_most_late, o_last_late], axis=1),
        ],
        axis=0,
    )
    mixed_early = finish(which, tokens, keep_early, got_early, row_of(0), row_of(1), 0, (o_last_late,))
    after = (mixed_early,)
    mixed_early = lax.all_gather(mixed_early, ("mh", "ml"), axis=0, tiled=True)

    home = rows if seq_size == 2 else 0
    dq, dk, dv, got = [], [], [], []
    for pair in range(pairs):
        kv_parts, at = (kv_last, 0) if pair == pairs - 1 else (kv_most, pair)
        outs = attend_back(info, slots, q, grad_o, stats, kv_parts, pair, at, home, after)
        after = (outs[0],)
        dq.append(outs[0])
        if home:
            dk.append(outs[1])
            dv.append(outs[2])
            got.append(swap(outs[3], "seq"))
        else:
            both = jnp.concatenate([outs[1], outs[2]], axis=1).astype(BF16)
            got.append(lax.psum_scatter(both, "seq", scatter_dimension=0, tiled=True))
            dk.append(jnp.zeros((rows, LANES), F32))
            dv.append(jnp.zeros((rows, LANES), F32))
        if pair == 1:
            mixed_late = finish(which, tokens, keep_late, got_late, row_of(0), row_of(1), 1, (outs[0], got[0]))
            after = (outs[0], mixed_late)
            mixed_late = lax.all_gather(mixed_late, ("mh", "ml"), axis=0, tiled=True)
        elif pair > 1:
            after = (outs[0], got[pair - 1])
    feed_weights, mlp_vectors, grad_up_b = feed_grads(
        which, tokens, out_grad, act, mlp_grad, up_w, column_of(4), column_of(5), after + (mixed_early,)
    )
    dq = jnp.concatenate(dq, axis=1)
    dproj, send, keep = back(
        which, dq, dk, dv, got, qkv_w, row_of(2), mlp_dx, tables, (grad_up_b,)
    )
    mixed = lay_gathered(mixed_early, mixed_late, (dproj,))
    got = [swap(send[run * quarter : (run + 1) * quarter], "ml") for run in range(2)]
    grad_qkv, grad_dense, qkv_vectors, grad_qkv_b = weight_grads(
        which, tokens, out_grad, dproj, attended, qkv_w, column_of(2), column_of(3), (mixed_late,)
    )
    ties = ((grad_qkv_b,), (grad_qkv_b,))
    input_grad = [norm_back(which, tokens, out_grad, keep, got[run], run, ties[run]) for run in range(2)]
    travelled = [line_mp(rows_done) for rows_done in input_grad]
    input_grad = lay_line(index, *travelled)

    def scatter(grads):
        return lax.psum_scatter(grads, ("dp", "seq"), scatter_dimension=0, tiled=True)

    vector_grads = (mlp_vectors + qkv_vectors)[:, None, :5]
    vector_grads = jnp.broadcast_to(vector_grads, (width, 2, 5))
    bias_qkv = grad_qkv_b.reshape(3, 2, heads, owners, piece).transpose(3, 0, 2, 4, 1)
    bias_qkv = bias_qkv.reshape(owners, 3 * heads * piece, 2)
    bias_qkv = jnp.pad(bias_qkv, ((0, 0), (0, share - 3 * heads * piece), (0, 0))).reshape(width, 2, 1)
    bias_up = grad_up_b.reshape(2, up_rows, owners, up_cols).transpose(2, 1, 3, 0).reshape(width, 2, 1)
    tail = jnp.concatenate([vector_grads, bias_qkv, bias_up], axis=2)
    tail = jnp.pad(tail, ((0, 0), (0, 0), (0, LANES // 2 - 7))).astype(BF16).reshape(width, LANES)
    packed = scatter(join((grad_qkv, grad_dense, tail, feed_weights)))
    segments = (cols,) * 4 + (LANES // 2, units, units)
    kept, sent = sides(which, packed, segments, [steps[at] for steps in travelled for at in (2, 5)])
    owned = kept.astype(F32) + swap(sent, "mh").astype(F32)
    owned, owned_feed = owned[:, : 4 * cols + LANES // 2], owned[:, 4 * cols + LANES // 2 :]
    vectors = owned[:, 4 * cols :]
    norms = vectors[:, :5]
    norms = norms + swap(norms, "ml")
    bias_grad = norms[:, 0]
    return (
        mixed,
        input_grad,
        owned[:, : 3 * cols].reshape(share, 3, cols).transpose(1, 0, 2),
        vectors[: 3 * heads * piece, 5].reshape(b_qkv.shape),
        owned[:, 3 * cols : 4 * cols].T,
        bias_grad,
        owned_feed[:, :units],
        vectors[:, 6].reshape(b_up.shape),
        owned_feed[:, units:].T,
        bias_grad,
        norms[:, 1],
        norms[:, 2],
        norms[:, 3],
        norms[:, 4],
    )


def solution(mesh):
    dp, seq, mp = (mesh.shape[axis] for axis in ("dp", "seq", "mp"))
    split = Mesh(mesh.devices.reshape(dp, seq, 2, mp // 2), ("dp", "seq", "mh", "ml"))
    mp, owner = ("mh", "ml"), ("dp", "seq")
    row = P("dp", "seq", None)
    vector = P(owner)
    weights = (
        P(None, owner, mp), P(None, mp, owner), P(mp, owner), vector, P(owner, mp), P(mp, owner),
        P(mp, owner), vector, vector, vector, vector, vector,
    )
    return jax.shard_map(
        functools.partial(body, seq_size=seq, owners=dp * seq),
        mesh=split,
        in_specs=(row, P("dp", "seq")) + weights + (row,),
        out_specs=(row, row) + weights,
        check_vma=False,
    )
```

```python
import functools

import jax
import jax.numpy as jnp
from jax import lax
from jax.experimental import pallas as pl
from jax.experimental.pallas import tpu as pltpu
from jax.sharding import Mesh
from jax.sharding import PartitionSpec as P

HD = 64
ROT = 16
LANES = 128
F32 = jnp.float32
BF16 = jnp.bfloat16
LOG2E = 1.4426950408889634
norm_eps = 1e-05
masked_value = -1e30
vmem_bytes = 60 * 2**20
brief = pl.CostEstimate(flops=1, bytes_accessed=1, transcendentals=0)
long = pl.CostEstimate(flops=2**33, bytes_accessed=2**24, transcendentals=0)

NN = (((1,), (0,)), ((), ()))
NT = (((1,), (1,)), ((), ()))
TN = (((0,), (0,)), ((), ()))


def dot(left, right, dims):
    return lax.dot_general(left, right, dims, preferred_element_type=F32)


def normalise(rows):
    centre = jnp.mean(rows, axis=-1, keepdims=True)
    deviate = rows - centre
    spread = jnp.mean(deviate * deviate, axis=-1, keepdims=True)
    scale = lax.rsqrt(spread + norm_eps)
    return deviate * scale, scale


def turn(chunk, cosines, sine_low, sine_high):
    half = ROT // 2
    return (
        chunk * cosines
        + pltpu.roll(chunk, LANES - half, 1) * sine_low
        + pltpu.roll(chunk, half, 1) * sine_high
    )

longest = pl.CostEstimate(flops=2**36, bytes_accessed=2**27, transcendentals=0)


anywhere = pl.BlockSpec(memory_space=pl.ANY)


def whole(shape):
    return pl.BlockSpec(shape, lambda *_: (0,) * len(shape))


def params(**kwargs):
    return pltpu.CompilerParams(vmem_limit_bytes=vmem_bytes, **kwargs)


def place_first_kernel(where, one_ref, two_ref, qkv_ref, dense_ref, small_ref):
    cols = one_ref.shape[-1] // 2
    share = one_ref.shape[2]
    near = where[0] == 0
    for i in range(4):
        bits = (pl.program_id(0) * 4 + i) ^ where[1]
        upper, lower, across = bits // 4, (bits // 2) % 2, bits % 2
        one = [one_ref[lower * 4 + upper * 2 + across, j] for j in range(2)]
        two = [two_ref[lower * 4 + across * 2 + upper, j] for j in range(2)]
        one = (jnp.where(near, one[0], one[1]), jnp.where(near, one[1], one[0]))
        two = (jnp.where(near, two[0], two[1]), jnp.where(near, two[1], two[0]))
        pieces = [one[j][:, at * cols : (at + 1) * cols] for at in range(2) for j in range(2)]
        pieces += [two[j][:, :cols] for j in range(2)]
        rows = slice(i * share, (i + 1) * share)
        qkv_ref[rows, :] = jnp.concatenate(pieces, axis=1)
        dense_ref[rows, :] = jnp.concatenate([two[j][:, cols : 2 * cols] for j in range(2)], axis=1)
        small_ref[rows, :] = jnp.concatenate([two[j][:, 2 * cols :] for j in range(2)], axis=1).astype(F32)


def place_second_kernel(pack_ref, up_ref, down_ref):
    units = pack_ref.shape[-1] // 2
    share = pack_ref.shape[2]
    for i in range(2):
        rows = slice(i * share, (i + 1) * share)
        for j in range(2):
            up_ref[rows, j * units : (j + 1) * units] = pack_ref[i, j, :, :units]
            down_ref[rows, j * units : (j + 1) * units] = pack_ref[i, j, :, units:]


def place_second(pack):
    owners, _, share, width = pack.shape
    return pl.pallas_call(
        place_second_kernel,
        grid=(owners // 2,),
        in_specs=[pl.BlockSpec((2,) + pack.shape[1:], lambda i: (i, 0, 0, 0))],
        out_specs=[pl.BlockSpec((2 * share, width), lambda i: (i, 0))] * 2,
        out_shape=[jax.ShapeDtypeStruct((owners * share, width), BF16)] * 2,
        compiler_params=params(),
        cost_estimate=brief,
        name="place_second",
    )(pack)


def place_first(where, one, two, widths, types):
    owners, _, share, _ = one.shape
    return pl.pallas_call(
        place_first_kernel,
        grid_spec=pltpu.PrefetchScalarGridSpec(
            num_scalar_prefetch=1,
            grid=(owners // 4,),
            in_specs=[whole(one.shape), whole(two.shape)],
            out_specs=[pl.BlockSpec((4 * share, width), lambda i, *_: (i, 0)) for width in widths],
        ),
        out_shape=[jax.ShapeDtypeStruct((owners * share, width), kind) for width, kind in zip(widths, types)],
        compiler_params=params(),
        cost_estimate=brief,
        name="place_first",
    )(where, one, two)


def front_kernel(
    which, x_ref, dy_ref, w_ref, wb_ref, dense_ref, gain_ref, shift_ref, cos_ref, low_ref, high_ref,
    q_ref, kv_most, kv_last, do_ref,
):
    half = q_ref.shape[1]
    most = kv_most.shape[1] // 2
    xhat, _ = normalise(x_ref[0].astype(F32))
    normed = (xhat * gain_ref[...] + shift_ref[...]).astype(BF16)
    proj = dot(normed, w_ref[...], NN) + wb_ref[...]
    cosines, low, high = cos_ref[...], low_ref[...], high_ref[...]
    for j in range(half // LANES):
        at = slice(j * LANES, (j + 1) * LANES)
        query = turn(proj[:, at], cosines, low, high).astype(BF16)
        q_ref[:, at] = query * BF16(HD**-0.5)
        key = turn(proj[:, half + j * LANES : half + (j + 1) * LANES], cosines, low, high).astype(BF16)
        if j * LANES < most:
            kv_most[:, at] = key
        else:
            kv_last[:, :LANES] = key
    kv_most[:, most:] = proj[:, 2 * half : 2 * half + most].astype(BF16)
    kv_last[:, LANES:] = proj[:, 2 * half + most :].astype(BF16)
    do_ref[...] = dot(dy_ref[0], dense_ref[...], NN).astype(BF16)


def front(which, x, dy, w, wb, dense, gain, shift, tables):
    _, rows, width = x.shape
    half = dense.shape[1]
    step = min(512, rows)
    chosen = pl.BlockSpec((1, step, width), lambda i, which: (which[0], i, 0))
    by_row = lambda cols: pl.BlockSpec((step, cols), lambda i, *_: (i, 0))
    return pl.pallas_call(
        front_kernel,
        grid_spec=pltpu.PrefetchScalarGridSpec(
            num_scalar_prefetch=1,
            grid=(rows // step,),
            in_specs=[chosen, chosen, whole(w.shape), whole(wb.shape), whole(dense.shape),
                      whole(gain.shape), whole(shift.shape)] + [by_row(LANES)] * 3,
            out_specs=[by_row(half), by_row(2 * half - 2 * LANES), by_row(2 * LANES), by_row(half)],
        ),
        out_shape=[
            jax.ShapeDtypeStruct((rows, half), BF16),
            jax.ShapeDtypeStruct((rows, 2 * half - 2 * LANES), BF16),
            jax.ShapeDtypeStruct((rows, 2 * LANES), BF16),
            jax.ShapeDtypeStruct((rows, half), BF16),
        ],
        compiler_params=params(),
        cost_estimate=brief,
        name="front",
    )(which, x, dy, w, wb, dense, gain, shift, *tables)


def feed_kernel(
    which, x_ref, dy_ref, up_ref, upb_ref, down_ref, gain_ref, shift_ref, part_ref, dx_ref, act_ref, grad_ref
):
    xhat, _ = normalise(x_ref[0].astype(F32))
    normed = (xhat * gain_ref[...] + shift_ref[...]).astype(BF16)
    hidden = dot(normed, up_ref[...], NN) + upb_ref[...]
    share = 0.5 * (1.0 + lax.erf(hidden * F32(0.5**0.5)))
    act = (hidden * share).astype(BF16)
    act_ref[...] = act
    slope = share + hidden * (jnp.exp(hidden * hidden * -0.5) * F32(0.3989422804014327))
    part_ref[...] = dot(act, down_ref[...], NT).astype(part_ref.dtype)
    grad_low = (dot(dy_ref[0], down_ref[...], NN) * slope).astype(BF16)
    grad_ref[...] = grad_low
    dx_ref[...] = (dot(grad_low, up_ref[...], NT) * gain_ref[...]).astype(dx_ref.dtype)


def feed(which, x, dy, up, upb, down, gain, shift):
    _, rows, width = x.shape
    units = up.shape[1]
    step = min(256, rows)
    chosen = pl.BlockSpec((1, step, width), lambda i, which: (which[0], i, 0))
    by_row = lambda cols: pl.BlockSpec((step, cols), lambda i, *_: (i, 0))
    return pl.pallas_call(
        feed_kernel,
        grid_spec=pltpu.PrefetchScalarGridSpec(
            num_scalar_prefetch=1,
            grid=(rows // step,),
            in_specs=[chosen, chosen, whole(up.shape), whole(upb.shape), whole(down.shape),
                      whole(gain.shape), whole(shift.shape)],
            out_specs=[by_row(width), by_row(width), by_row(units), by_row(units)],
        ),
        out_shape=[
            jax.ShapeDtypeStruct((rows, width), BF16),
            jax.ShapeDtypeStruct((rows, width), BF16),
            jax.ShapeDtypeStruct((rows, units), BF16),
            jax.ShapeDtypeStruct((rows, units), BF16),
        ],
        compiler_params=params(),
        cost_estimate=brief,
        name="feed",
    )(which, x, dy, up, upb, down, gain, shift)


def feed_grads_kernel(
    which, x_ref, dy_ref, act_ref, grad_ref, up_ref, gain_col, shift_col, *refs
):
    both_ref, vec_ref, gupb_ref, up_acc, down_acc, sum_acc, dy_acc = refs[-7:]
    step = pl.program_id(0)

    @pl.when(step == 0)
    def _():
        up_acc[...] = jnp.zeros_like(up_acc)
        down_acc[...] = jnp.zeros_like(down_acc)
        sum_acc[...] = jnp.zeros_like(sum_acc)
        dy_acc[...] = jnp.zeros_like(dy_acc)

    xhat, _ = normalise(x_ref[0].astype(F32))
    dy, grad = dy_ref[0], grad_ref[...]
    up_acc[...] += dot(xhat.astype(BF16), grad, TN)
    down_acc[...] += dot(dy, act_ref[...], TN)
    sum_acc[...] += jnp.sum(grad.astype(F32), axis=0, keepdims=True)
    dy_acc[...] += jnp.sum(dy.astype(F32), axis=0, keepdims=True)

    @pl.when(step == pl.num_programs(0) - 1)
    def _():
        sums, raw = sum_acc[...], up_acc[...]
        up = up_ref[...].astype(F32)
        units = up.shape[1]
        both_ref[:, :units] = (raw * gain_col[...] + shift_col[...] * sums).astype(both_ref.dtype)
        both_ref[:, units:] = down_acc[...].astype(both_ref.dtype)
        gupb_ref[...] = sums
        lane = lax.broadcasted_iota(jnp.int32, vec_ref.shape, 1)
        gain_grad = jnp.sum(raw * up, axis=1, keepdims=True)
        shift_grad = jnp.sum(up * sums, axis=1, keepdims=True)
        dy_col = jnp.transpose(jnp.broadcast_to(dy_acc[...], (LANES, dy_acc.shape[1])))
        vec_ref[...] = jnp.where(
            lane == 0, dy_col * 0.5,
            jnp.where(lane == 3, gain_grad, jnp.where(lane == 4, shift_grad, 0.0)),
        )


def feed_grads(which, x, dy, act, grad, up, gain_col, shift_col, after=()):
    _, rows, width = x.shape
    units = up.shape[1]
    step = min(512, rows)
    chosen = pl.BlockSpec((1, step, width), lambda i, which: (which[0], i, 0))
    by_row = pl.BlockSpec((step, units), lambda i, *_: (i, 0))
    return pl.pallas_call(
        feed_grads_kernel,
        grid_spec=pltpu.PrefetchScalarGridSpec(
            num_scalar_prefetch=1,
            grid=(rows // step,),
            in_specs=[chosen, chosen, by_row, by_row, whole(up.shape),
                      whole(gain_col.shape), whole(shift_col.shape)] + [anywhere] * len(after),
            out_specs=[whole((width, 2 * units)), whole((width, LANES)), whole((1, units))],
            scratch_shapes=[pltpu.VMEM((width, units), F32), pltpu.VMEM((width, units), F32),
                            pltpu.VMEM((1, units), F32), pltpu.VMEM((1, width), F32)],
        ),
        out_shape=[
            jax.ShapeDtypeStruct((width, 2 * units), BF16),
            jax.ShapeDtypeStruct((width, LANES), F32),
            jax.ShapeDtypeStruct((1, units), F32),
        ],
        compiler_params=params(),
        cost_estimate=long,
        name="feed_grads",
    )(which, x, dy, act, grad, up, gain_col, shift_col, *after)


def lane_fold(values, combine):
    total = values[:, :LANES]
    for j in range(1, values.shape[1] // LANES):
        total = combine(total, values[:, j * LANES : (j + 1) * LANES])
    return total


def pick_heads(both, heads):
    return [jnp.where(mine, both, jnp.zeros_like(both)) for mine in heads]


def head_lanes(rows):
    lane = lax.broadcasted_iota(jnp.int32, (rows, LANES), 1)
    return lane < HD, lane >= HD


def tiles(block, last):
    half = block // 2
    if last and block >= 512:
        return (0, 0, half), (half, half, half)
    return ((0, 0, block),)


def visible(shape):
    return lax.broadcasted_iota(jnp.int32, shape, 1) <= lax.broadcasted_iota(jnp.int32, shape, 0)


def merge(whole_rows, row, part, combine):
    if row == 0:
        return combine(whole_rows, part)
    return jnp.concatenate([whole_rows[:row], combine(whole_rows[row:], part)], axis=0)


def attend_kernel(info, slots, q_ref, g_ref, dense_ref, prior_ref, *refs, block, parts, run, ties, split):
    k_parts, v_parts, refs = refs[:parts], refs[parts : 2 * parts], refs[2 * parts + ties :]
    o_ref, stat_ref, refs = refs[0], refs[1], refs[2:]
    if split:
        send_ref, keep_ref, refs = refs[0], refs[1], refs[2:]
    else:
        sum_ref, refs = refs[0], refs[1:]
    k_ref, v_ref, score_ref, acc_ref, branch_ref = refs
    pair = pl.program_id(0)
    full = info[run]

    @pl.when(pair == 0)
    def _():
        branch_ref[...] = prior_ref[...].astype(F32)

    at = 0
    for j in range(parts):
        there = pl.ds(at, k_parts[j].shape[0])
        k_ref[there, :] = k_parts[j][...]
        v_ref[there, :] = v_parts[j][...]
        at += k_parts[j].shape[0]

    heads = head_lanes(block)
    queries = pick_heads(q_ref[...], heads)

    def rows_of(at, col, count):
        return pl.ds(pl.multiple_of(slots[at] * block + col, count), count)

    def score(at, tops, last):
        out = []
        for h in range(2):
            top = tops[h]
            for row, col, count in tiles(block, last):
                scores = dot(queries[h][row:], k_ref[rows_of(at, col, count), :], NT)
                if last:
                    scores = jnp.where(visible(scores.shape), scores, masked_value)
                score_ref[h, at, row:, col : col + count] = scores
                top = merge(top, row, lane_fold(scores, jnp.maximum), jnp.maximum)
            out.append(top)
        return tuple(out)

    least = jnp.full((block, LANES), masked_value, F32)
    tops = lax.fori_loop(0, full, lambda at, carry: score(at, carry, False), (least, least))
    tops = score(full, tops, True)
    tops = [jnp.max(top, axis=1, keepdims=True) * F32(LOG2E) for top in tops]

    acc_ref[...] = jnp.zeros_like(acc_ref)

    def weigh(at, totals, last):
        out = []
        for h in range(2):
            total = totals[h]
            for row, col, count in tiles(block, last):
                values = v_ref[rows_of(at, col, count), :]
                soft = jnp.exp2(score_ref[h, at, row:, col : col + count] * F32(LOG2E) - tops[h][row:])
                total = merge(total, row, lane_fold(soft, jnp.add), jnp.add)
                acc_ref[h, row:, :] += dot(soft.astype(BF16), values, NN)
            out.append(total)
        return tuple(out)

    nought = jnp.zeros((block, LANES), F32)
    totals = lax.fori_loop(0, full, lambda at, carry: weigh(at, carry, False), (nought, nought))
    totals = weigh(full, totals, True)
    totals = [jnp.sum(total, axis=1, keepdims=True) for total in totals]
    attended = jnp.where(heads[0], acc_ref[0] / totals[0], acc_ref[1] / totals[1])
    o_ref[...] = attended.astype(o_ref.dtype)
    branch_ref[...] += dot(attended.astype(BF16), dense_ref[...], NT)
    product = attended * g_ref[...].astype(F32)
    row_terms = [jnp.sum(jnp.where(mine, product, 0.0), axis=1, keepdims=True) for mine in heads]
    logs = [tops[h] + jnp.log2(totals[h]) for h in range(2)]
    lane = lax.broadcasted_iota(jnp.int32, (block, LANES), 1)
    stats = jnp.where(lane == 0, logs[0], jnp.where(lane == 1, logs[1], 0.0))
    stats = jnp.where(lane == 2, row_terms[0], jnp.where(lane == 3, row_terms[1], stats))
    stat_ref[...] = jnp.transpose(stats)[:8]

    @pl.when(pair == pl.num_programs(0) - 1)
    def _():
        if split:
            half = block // 2
            send_ref[...] = branch_ref[pl.ds(pl.multiple_of((1 - info[2]) * half, half), half), :].astype(BF16)
            keep_ref[...] = branch_ref[pl.ds(pl.multiple_of(info[2] * half, half), half), :]
        else:
            sum_ref[...] = branch_ref[...]


def attend(info, slots, q, g, kv_parts, dense, prior, run, base, after=()):
    rows, width = q.shape
    model = dense.shape[0]
    keys = sum(kv.shape[0] for kv in kv_parts)
    run_rows = rows // 2
    block = run_rows
    pairs = kv_parts[0].shape[1] // (2 * LANES)
    split = (base + pairs) * LANES == width
    prior_row = run if prior.shape[0] == rows else 0
    by_query = pl.BlockSpec((block, LANES), lambda p, *_: (run, base + p))
    by_key = [pl.BlockSpec((kv.shape[0], LANES), lambda p, *_: (0, p)) for kv in kv_parts]
    by_value = [pl.BlockSpec((kv.shape[0], LANES), lambda p, *_: (0, pairs + p)) for kv in kv_parts]
    kernel = functools.partial(
        attend_kernel, block=block, parts=len(kv_parts), run=run,
        ties=len(after), split=split,
    )
    return pl.pallas_call(
        kernel,
        grid_spec=pltpu.PrefetchScalarGridSpec(
            num_scalar_prefetch=2,
            grid=(pairs,),
            in_specs=[
                by_query, by_query,
                pl.BlockSpec((model, LANES), lambda p, *_: (0, base + p)),
                pl.BlockSpec((run_rows, model), lambda p, *_: (prior_row, 0)),
                *by_key, *by_value,
            ] + [anywhere] * len(after),
            out_specs=[
                pl.BlockSpec((block, LANES), lambda p, *_: (0, p)),
                pl.BlockSpec((8, block), lambda p, *_: (p, 0)),
            ] + ([whole((run_rows // 2, model))] * 2 if split else [whole((run_rows, model))]),
            scratch_shapes=[
                pltpu.VMEM((keys, LANES), BF16),
                pltpu.VMEM((keys, LANES), BF16),
                pltpu.VMEM((2, keys // run_rows, block, run_rows), F32),
                pltpu.VMEM((2, block, LANES), F32),
                pltpu.VMEM((run_rows, model), F32),
            ],
        ),
        out_shape=[
            jax.ShapeDtypeStruct((run_rows, pairs * LANES), BF16),
            jax.ShapeDtypeStruct((8 * pairs, run_rows), F32),
        ] + ([
            jax.ShapeDtypeStruct((run_rows // 2, model), BF16),
            jax.ShapeDtypeStruct((run_rows // 2, model), F32),
        ] if split else [jax.ShapeDtypeStruct((run_rows, model), F32)]),
        compiler_params=params(),
        cost_estimate=brief,
        name="attend",
    )(info, slots, q, g, dense, prior, *kv_parts, *kv_parts, *after)


def attend_back_kernel(info, slots, q_ref, g_ref, stat_ref, *refs, block, parts, home, ties):
    k_parts, v_parts, refs = refs[:parts], refs[parts : 2 * parts], refs[2 * parts + ties :]
    dq_ref, dk_out, dv_out, refs = refs[0], refs[1], refs[2], refs[3:]
    if home:
        back_ref, refs = refs[0], refs[1:]
    k_ref, v_ref, dk_ref, dv_ref, acc_ref = refs
    step = pl.program_id(0)
    full = info[step]

    @pl.when(step == 0)
    def _():
        at = 0
        for j in range(parts):
            there = pl.ds(at, k_parts[j].shape[0])
            k_ref[there, :] = k_parts[j][...]
            v_ref[there, :] = v_parts[j][...]
            at += k_parts[j].shape[0]
        dk_ref[...] = jnp.zeros_like(dk_ref)
        dv_ref[...] = jnp.zeros_like(dv_ref)

    heads = head_lanes(block)
    queries, grads = pick_heads(q_ref[...], heads), pick_heads(g_ref[...], heads)
    stats = jnp.transpose(stat_ref[...])
    logs, row_terms = [stats[:, h : h + 1] for h in range(2)], [stats[:, 2 + h : 3 + h] for h in range(2)]
    acc_ref[...] = jnp.zeros_like(acc_ref)

    def back(at, last):
        for row, col, count in tiles(block, last):
            there = pl.ds(pl.multiple_of(slots[at] * block + col, count), count)
            keys, values = k_ref[there, :], v_ref[there, :]
            key_terms, value_terms = [], []
            for h in range(2):
                query, grad = queries[h][row:], grads[h][row:]
                soft = jnp.exp2(dot(query, keys, NT) * F32(LOG2E) - logs[h][row:])
                if last:
                    soft = jnp.where(visible(soft.shape), soft, 0.0)
                grad_soft = dot(grad, values, NT)
                grad_score = (soft * (grad_soft - row_terms[h][row:])).astype(BF16)
                acc_ref[h, row:, :] += dot(grad_score, keys, NN)
                key_terms.append(dot(grad_score, query, TN))
                value_terms.append(dot(soft.astype(BF16), grad, TN))
            dk_ref[there, :] += key_terms[0] + key_terms[1]
            dv_ref[there, :] += value_terms[0] + value_terms[1]

    def back_whole(at, carry):
        back(at, False)
        return carry

    lax.fori_loop(0, full, back_whole, 0)
    back(full, True)
    dq_ref[...] = (jnp.where(heads[0], acc_ref[0], acc_ref[1]) * F32(HD**-0.5)).astype(dq_ref.dtype)

    @pl.when(step == pl.num_programs(0) - 1)
    def _():
        own = dk_out.shape[0]
        dk_out[...] = dk_ref[:own, :]
        dv_out[...] = dv_ref[:own, :]
        if home:
            back_ref[:, :LANES] = dk_ref[home:, :].astype(BF16)
            back_ref[:, LANES:] = dv_ref[home:, :].astype(BF16)


def attend_back(info, slots, q, g, stats, kv_parts, pair, at, home, after=()):
    rows, width = q.shape
    keys = sum(kv.shape[0] for kv in kv_parts)
    run_rows = rows // 2
    block = run_rows
    pairs = kv_parts[0].shape[1] // (2 * LANES)
    own = home or keys
    by_query = pl.BlockSpec((block, LANES), lambda i, *_: (i, pair))
    by_key = [pl.BlockSpec((kv.shape[0], LANES), lambda i, *_: (0, at)) for kv in kv_parts]
    by_value = [pl.BlockSpec((kv.shape[0], LANES), lambda i, *_: (0, pairs + at)) for kv in kv_parts]
    kernel = functools.partial(
        attend_back_kernel, block=block, parts=len(kv_parts), home=home, ties=len(after)
    )
    out_specs = [pl.BlockSpec((block, LANES), lambda i, *_: (i, 0)), whole((own, LANES)), whole((own, LANES))]
    out_shape = [
        jax.ShapeDtypeStruct((rows, LANES), BF16),
        jax.ShapeDtypeStruct((own, LANES), F32),
        jax.ShapeDtypeStruct((own, LANES), F32),
    ]
    if home:
        out_specs.append(whole((keys - home, 2 * LANES)))
        out_shape.append(jax.ShapeDtypeStruct((keys - home, 2 * LANES), BF16))
    return pl.pallas_call(
        kernel,
        grid_spec=pltpu.PrefetchScalarGridSpec(
            num_scalar_prefetch=2,
            grid=(rows // block,),
            in_specs=[by_query, by_query, pl.BlockSpec((8, block), lambda i, *_: (pair, i)), *by_key, *by_value]
            + [anywhere] * len(after),
            out_specs=out_specs,
            scratch_shapes=[
                pltpu.VMEM((keys, LANES), BF16),
                pltpu.VMEM((keys, LANES), BF16),
                pltpu.VMEM((keys, LANES), F32),
                pltpu.VMEM((keys, LANES), F32),
                pltpu.VMEM((2, block, LANES), F32),
            ],
        ),
        out_shape=out_shape,
        compiler_params=params(),
        cost_estimate=long,
        name="attend_back",
    )(info, slots, q, g, stats, *kv_parts, *kv_parts, *after)


def back_kernel(which, dq_ref, *refs, pairs):
    own_k, refs = refs[:pairs], refs[pairs:]
    own_v, refs = refs[:pairs], refs[pairs:]
    got, refs = refs[:pairs], refs[pairs:]
    w_ref, gain_ref, dx_in, cos_ref, low_ref, high_ref = refs[:6]
    dproj_ref, send_ref, keep_ref = refs[-3:]
    half = dq_ref.shape[1]
    cosines, low, high = cos_ref[...], low_ref[...], high_ref[...]
    for j in range(pairs):
        at = slice(j * LANES, (j + 1) * LANES)
        query = dq_ref[:, at].astype(F32)
        dproj_ref[:, at] = turn(query, cosines, -low, -high).astype(BF16)
        key = own_k[j][...] + got[j][:, :LANES].astype(F32)
        dproj_ref[:, half + j * LANES : half + (j + 1) * LANES] = turn(key, cosines, -low, -high).astype(BF16)
        value = own_v[j][...] + got[j][:, LANES:].astype(F32)
        dproj_ref[:, 2 * half + j * LANES : 2 * half + (j + 1) * LANES] = value.astype(BF16)
    summed = dot(dproj_ref[...], w_ref[...], NT) * gain_ref[...] + dx_in[...].astype(F32)
    mine = pl.program_id(0) % 2 == which[1]

    @pl.when(mine)
    def _():
        keep_ref[...] = summed

    @pl.when(jnp.logical_not(mine))
    def _():
        send_ref[...] = summed.astype(send_ref.dtype)


def back(which, dq, dk, dv, got, w, gain, dx_part, tables, after=()):
    rows, half = dq.shape
    width = w.shape[0]
    step = rows // 4
    pairs = len(dk)
    by_row = lambda cols: pl.BlockSpec((step, cols), lambda i, *_: (i, 0))
    by_run = pl.BlockSpec((step, width), lambda i, *_: (i // 2, 0))
    return pl.pallas_call(
        functools.partial(back_kernel, pairs=pairs),
        grid_spec=pltpu.PrefetchScalarGridSpec(
            num_scalar_prefetch=1,
            grid=(4,),
            in_specs=[by_row(half)] + [by_row(LANES)] * (2 * pairs) + [by_row(2 * LANES)] * pairs
            + [whole(w.shape), whole(gain.shape), by_row(width)] + [by_row(LANES)] * 3
            + [anywhere] * len(after),
            out_specs=[by_row(3 * half), by_run, by_run],
        ),
        out_shape=[
            jax.ShapeDtypeStruct((rows, 3 * half), BF16),
            jax.ShapeDtypeStruct((rows // 2, width), BF16),
            jax.ShapeDtypeStruct((rows // 2, width), F32),
        ],
        compiler_params=params(),
        cost_estimate=brief,
        name="back",
    )(which, dq, *dk, *dv, *got, w, gain, dx_part, *tables, *after)


def weight_kernel(
    which, x_ref, dy_ref, dproj_ref, o_ref, w_ref, gain_col, shift_col, *refs
):
    gqkv_ref, gdense_ref, vec_ref, gb_ref, acc, dense_acc, sum_acc = refs[-7:]
    step = pl.program_id(0)

    @pl.when(step == 0)
    def _():
        acc[...] = jnp.zeros_like(acc)
        dense_acc[...] = jnp.zeros_like(dense_acc)
        sum_acc[...] = jnp.zeros_like(sum_acc)

    xhat, _ = normalise(x_ref[0].astype(F32))
    dproj = dproj_ref[...]
    acc[...] += dot(xhat.astype(BF16), dproj, TN)
    dense_acc[...] += dot(dy_ref[0], o_ref[...], TN)
    sum_acc[...] += jnp.sum(dproj.astype(F32), axis=0, keepdims=True)

    @pl.when(step == pl.num_programs(0) - 1)
    def _():
        sums, raw, w = sum_acc[...], acc[...], w_ref[...].astype(F32)
        gqkv_ref[...] = (raw * gain_col[...] + shift_col[...] * sums).astype(gqkv_ref.dtype)
        gdense_ref[...] = dense_acc[...].astype(gdense_ref.dtype)
        gb_ref[...] = sums
        lane = lax.broadcasted_iota(jnp.int32, vec_ref.shape, 1)
        gain_grad = jnp.sum(raw * w, axis=1, keepdims=True)
        shift_grad = jnp.sum(w * sums, axis=1, keepdims=True)
        vec_ref[...] = jnp.where(lane == 1, gain_grad, jnp.where(lane == 2, shift_grad, 0.0))


def weight_grads(which, x, dy, dproj, o, w, gain_col, shift_col, after=()):
    _, rows, width = x.shape
    half = o.shape[1]
    step = min(512, rows)
    chosen = pl.BlockSpec((1, step, width), lambda i, which: (which[0], i, 0))
    by_row = lambda cols: pl.BlockSpec((step, cols), lambda i, *_: (i, 0))
    return pl.pallas_call(
        weight_kernel,
        grid_spec=pltpu.PrefetchScalarGridSpec(
            num_scalar_prefetch=1,
            grid=(rows // step,),
            in_specs=[chosen, chosen, by_row(3 * half), by_row(half), whole(w.shape),
                      whole(gain_col.shape), whole(shift_col.shape)] + [anywhere] * len(after),
            out_specs=[whole((width, 3 * half)), whole((width, half)), whole((width, LANES)), whole((1, 3 * half))],
            scratch_shapes=[pltpu.VMEM((width, 3 * half), F32), pltpu.VMEM((width, half), F32),
                            pltpu.VMEM((1, 3 * half), F32)],
        ),
        out_shape=[
            jax.ShapeDtypeStruct((width, 3 * half), BF16),
            jax.ShapeDtypeStruct((width, half), BF16),
            jax.ShapeDtypeStruct((width, LANES), F32),
            jax.ShapeDtypeStruct((1, 3 * half), F32),
        ],
        compiler_params=params(),
        cost_estimate=long,
        name="weight_grads",
    )(which, x, dy, dproj, o, w, gain_col, shift_col, *after)


def join_kernel(*refs):
    out = refs[-1]
    at = 0
    for ref in refs[:-1]:
        out[:, at : at + ref.shape[1]] = ref[...]
        at += ref.shape[1]


def join(arrays):
    rows = arrays[0].shape[0]
    step = rows // 4
    widths = [array.shape[1] for array in arrays]
    by_row = lambda cols: pl.BlockSpec((step, cols), lambda i: (i, 0))
    return pl.pallas_call(
        join_kernel,
        grid=(4,),
        in_specs=[by_row(width) for width in widths],
        out_specs=by_row(sum(widths)),
        out_shape=jax.ShapeDtypeStruct((rows, sum(widths)), BF16),
        compiler_params=params(),
        cost_estimate=brief,
        name="join",
    )(*arrays)


def norm_back_kernel(which, x_ref, dy_ref, kept_ref, got_ref, *refs):
    out_ref = refs[-1]
    xhat, scale = normalise(x_ref[0].astype(F32))
    grad = kept_ref[...].astype(F32) + got_ref[...].astype(F32)
    centre = jnp.mean(grad, axis=-1, keepdims=True)
    along = jnp.mean(grad * xhat, axis=-1, keepdims=True)
    out_ref[...] = (dy_ref[0].astype(F32) + scale * (grad - centre - xhat * along)).astype(out_ref.dtype)


def norm_back(which, x, dy, kept, got, run, after=()):
    rows, width = got.shape
    step = min(256, rows)
    blocks = rows // step
    chosen = pl.BlockSpec(
        (1, step, width), lambda i, which: (which[0], (2 * run + which[1]) * blocks + i, 0)
    )
    return pl.pallas_call(
        norm_back_kernel,
        grid_spec=pltpu.PrefetchScalarGridSpec(
            num_scalar_prefetch=1,
            grid=(blocks,),
            in_specs=[chosen, chosen,
                      pl.BlockSpec((step, width), lambda i, *_: (run * blocks + i, 0)),
                      pl.BlockSpec((step, width), lambda i, *_: (i, 0))] + [anywhere] * len(after),
            out_specs=pl.BlockSpec((step, width), lambda i, *_: (i, 0)),
        ),
        out_shape=jax.ShapeDtypeStruct((rows, width), BF16),
        compiler_params=params(),
        cost_estimate=longest,
        name="norm_back",
    )(which, x, dy, kept, got, *after)


def finish_kernel(which, x_ref, kept_ref, got_ref, one_ref, two_ref, *refs):
    summed = kept_ref[...] + got_ref[...].astype(F32) + x_ref[0].astype(F32) + one_ref[...] + two_ref[...]
    refs[-1][...] = summed.astype(BF16)


def finish(which, x, kept, got, one, two, run, after=()):
    rows, width = got.shape
    step = min(256, rows)
    blocks = rows // step
    by_row = pl.BlockSpec((step, width), lambda i, *_: (i, 0))
    return pl.pallas_call(
        finish_kernel,
        grid_spec=pltpu.PrefetchScalarGridSpec(
            num_scalar_prefetch=1,
            grid=(blocks,),
            in_specs=[
                pl.BlockSpec((1, step, width), lambda i, which: (which[0], (2 * run + which[1]) * blocks + i, 0)),
                by_row, by_row, whole(one.shape), whole(two.shape),
            ] + [anywhere] * len(after),
            out_specs=by_row,
        ),
        out_shape=jax.ShapeDtypeStruct((rows, width), BF16),
        compiler_params=params(),
        cost_estimate=brief,
        name="finish",
    )(which, x, kept, got, one, two, *after)


def lay_kernel(early_ref, late_ref, *refs):
    out = refs[-1]
    run = pl.program_id(0) % 2

    @pl.when(run == 0)
    def _():
        out[0] = early_ref[...]

    @pl.when(run == 1)
    def _():
        out[0] = late_ref[...]


def lay_gathered(early, late, after=()):
    rows, width = early.shape[0] // 2, early.shape[1]
    half = pl.BlockSpec((rows, width), lambda i: (i // 2, 0))
    return pl.pallas_call(
        lay_kernel,
        grid=(4,),
        in_specs=[half, half] + [anywhere] * len(after),
        out_specs=pl.BlockSpec((1, rows, width), lambda i: (i // 2, i % 2, 0)),
        out_shape=jax.ShapeDtypeStruct((2, 2 * rows, width), BF16),
        compiler_params=params(),
        cost_estimate=brief,
        name="lay_gathered",
    )(early, late, *after)


STEPS = (0, 1, 2, 3, -1, -2, -3)


def lay_line_kernel(index, *refs):
    out, sem = refs[-2:]
    run, slot = pl.program_id(0) // 4, pl.program_id(0) % 4
    for j in range(2 * len(STEPS)):

        @pl.when((run == j // len(STEPS)) & (index[0] - slot == STEPS[j % len(STEPS)]))
        def _(j=j):
            copy = pltpu.make_async_copy(refs[j], out.at[0], sem)
            copy.start()
            copy.wait()


def lay_line(index, early, late):
    half, width = early[0].shape
    return pl.pallas_call(
        lay_line_kernel,
        grid_spec=pltpu.PrefetchScalarGridSpec(
            num_scalar_prefetch=1,
            grid=(8,),
            in_specs=[anywhere] * 14,
            out_specs=pl.BlockSpec((1, half, width), lambda i, *_: ((i % 4) // 2, 2 * (i // 4) + i % 2, 0)),
            scratch_shapes=[pltpu.SemaphoreType.DMA],
        ),
        out_shape=jax.ShapeDtypeStruct((2, 4 * half, width), BF16),
        compiler_params=params(),
        cost_estimate=brief,
        name="lay_line",
    )(index[None], *early, *late)


def sides_kernel(which, sums_ref, *refs, segments):
    keep_ref, send_ref = refs[-2:]
    near = which[0] == 0
    at = out = 0
    for cols in segments:
        one, two = sums_ref[:, at : at + cols], sums_ref[:, at + cols : at + 2 * cols]
        keep_ref[:, out : out + cols] = jnp.where(near, one, two)
        send_ref[:, out : out + cols] = jnp.where(near, two, one)
        at, out = at + 2 * cols, out + cols


def sides(which, sums, segments, after):
    rows = sums.shape[0]
    half = sum(segments)
    return pl.pallas_call(
        functools.partial(sides_kernel, segments=segments),
        grid_spec=pltpu.PrefetchScalarGridSpec(
            num_scalar_prefetch=1,
            grid=(1,),
            in_specs=[whole(sums.shape)] + [anywhere] * len(after),
            out_specs=[whole((rows, half))] * 2,
        ),
        out_shape=[jax.ShapeDtypeStruct((rows, half), BF16)] * 2,
        compiler_params=params(),
        cost_estimate=brief,
        name="sides",
    )(which, sums, *after)


def swap(values, axis):
    return lax.ppermute(values, axis, [(0, 1), (1, 0)])


def across(values, bit):
    return lax.ppermute(values, "dp", [(i, i ^ bit) for i in range(4)])


def gather_half(values, seq_first):
    values = jnp.concatenate([values[None], swap(values, "mh")[None]], axis=0)
    steps = [lambda v: swap(v, "seq"), lambda v: across(v, 2)]
    for step in steps if seq_first else steps[::-1]:
        values = jnp.concatenate([values, step(values)], axis=0)
    values = jnp.concatenate([values, across(values, 1)], axis=0)
    return values.reshape(8, 2, *values.shape[1:])


def line_mp(mine):
    axes = ("mh", "ml")
    before, behind = [mine], [mine]
    for _ in range(3):
        before.append(lax.ppermute(before[-1], axes, [(i, i + 1) for i in range(3)]))
        behind.append(lax.ppermute(behind[-1], axes, [(i + 1, i) for i in range(3)]))
    return before + behind[1:]


def rotation_tables(positions):
    half = ROT // 2
    frequency = jnp.power(F32(10000.0), -2.0 * jnp.arange(half, dtype=F32) / ROT)
    angles = frequency[:, None] * positions.astype(F32)[None, :]
    cosines, sines = lax.optimization_barrier((jnp.cos(angles), jnp.sin(angles)))
    cosines, sines = cosines.T, sines.T
    rows = positions.shape[0]
    rest = jnp.zeros((rows, HD - ROT), F32)
    blank = jnp.zeros((rows, half), F32)
    per_head = (
        jnp.concatenate([cosines, cosines, rest + 1.0], axis=1),
        jnp.concatenate([-sines, blank, rest], axis=1),
        jnp.concatenate([blank, sines, rest], axis=1),
    )
    return tuple(jnp.tile(table, (1, LANES // HD)) for table in per_head)


def body(
    tokens, places, w_qkv, b_qkv, w_dense, b_dense, w_up, b_up, w_down, b_down,
    norm1_gain, norm1_bias, norm2_gain, norm2_bias, out_grad, *, seq_size, owners,
):
    _, rows, width = tokens.shape
    share = width // owners
    heads = b_qkv.shape[1]
    cols = heads * HD
    units = w_up.shape[1]
    side, part = lax.axis_index("mh"), lax.axis_index("ml")
    index = (2 * side + part).astype(jnp.int32)
    owner = lax.axis_index("dp") * seq_size + lax.axis_index("seq")
    which = jnp.stack([side, part]).astype(jnp.int32)
    where = jnp.stack([side, owner]).astype(jnp.int32)

    run_rows = rows // 2
    held = places[:, ::run_rows] // run_rows

    def column(vector):
        vector = vector.reshape(-1)
        return jnp.pad(vector, (0, share - vector.shape[0]))[:, None]

    small = jnp.concatenate(
        [column(v) for v in (b_dense, b_down, norm1_gain, norm1_bias, norm2_gain, norm2_bias, b_qkv, b_up,
                            held.astype(BF16))],
        axis=1,
    )
    small = jnp.pad(small, ((0, 0), (0, LANES - small.shape[1])))
    one = w_qkv[:2].transpose(1, 0, 2).reshape(share, 2 * cols)
    two = jnp.concatenate([w_qkv[2], w_dense.T, small], axis=1)
    three, four = w_up, w_down.T
    first_widths = (6 * cols, 2 * cols, 2 * LANES)
    if owners == 8 and seq_size == 2:
        one, two = gather_half(one, True), gather_half(two, False)
        qkv_w, dense_w, small = place_first(where, one, two, first_widths, (BF16, BF16, F32))
        pack = lax.all_gather(jnp.concatenate([three, four], axis=1), ("dp", "seq", "mh"), axis=0, tiled=True)
        up_w, down_w = place_second(pack.reshape(owners, 2, share, 2 * units))
    else:

        def gather(values):
            values = lax.all_gather(values, ("dp", "seq", "mh"), axis=0, tiled=True)
            return values.reshape(owners, 2, share, -1).transpose(0, 2, 1, 3).reshape(width, 2, -1)

        one, two, three, four = gather(one), gather(two), gather(three), gather(four)
        qkv_w = jnp.concatenate([one[:, :, :cols], one[:, :, cols:], two[:, :, :cols]], axis=1)
        qkv_w, dense_w = qkv_w.reshape(width, 6 * cols), two[:, :, cols : 2 * cols].reshape(width, 2 * cols)
        small = two[:, :, 2 * cols :].reshape(width, 2 * LANES).astype(F32)
        up_w, down_w = three.reshape(width, 2 * units), four.reshape(width, 2 * units)
    vectors = small[:, :8]
    piece = HD // owners
    biases = small.reshape(owners, share, 2, LANES)
    qkv_b = biases[:, : 3 * heads * piece, :, 6].reshape(owners, 3, heads, piece, 2)
    qkv_b = qkv_b.transpose(1, 4, 2, 0, 3).reshape(1, 6 * cols)
    up_rows, up_cols = b_up.shape
    up_b = biases[..., 7].reshape(owners, up_rows, up_cols, 2).transpose(3, 1, 0, 2).reshape(1, 2 * units)
    by_row = vectors.T
    row_of = lambda at: by_row[at].reshape(1, width)
    column_of = lambda at: vectors[:, at].reshape(width, 1)

    my_places = lax.dynamic_index_in_dim(places, side, 0, keepdims=False)
    runs = lax.dynamic_index_in_dim(held, side, 0, keepdims=False)
    if owners == 8 and seq_size == 2:
        other = lax.dynamic_slice(small, ((owner ^ 1) * share + 2 * side, 8), (2, 1))[:, 0]
        all_runs = jnp.concatenate([runs, (other + 0.5).astype(jnp.int32)])
    elif seq_size == 2:
        all_runs = jnp.concatenate([runs, swap(runs, "seq")])
    else:
        all_runs = lax.all_gather(runs, "seq", axis=0, tiled=True)
    order = jnp.arange(2 * seq_size, dtype=jnp.int32)
    slots = jnp.sum(jnp.where(all_runs[None, :] == order[:, None], order[None, :], 0), axis=1)
    tables = rotation_tables(my_places)

    q, kv_most, kv_last, grad_o = front(
        which, tokens, out_grad, qkv_w, qkv_b, dense_w, row_of(2), row_of(3), tables
    )
    if seq_size == 2:
        kv_most, kv_last = (kv_most, swap(kv_most, "seq")), (kv_last, swap(kv_last, "seq"))
    else:
        kv_most = (lax.all_gather(kv_most, "seq", axis=0, tiled=True),)
        kv_last = (lax.all_gather(kv_last, "seq", axis=0, tiled=True),)
    pairs = q.shape[1] // LANES
    mlp_part, mlp_dx, act, mlp_grad = feed(which, tokens, out_grad, up_w, up_b, down_w, row_of(4), row_of(5))
    info = jnp.concatenate([runs, which[1:]])
    quarter = rows // 4

    def forward(kv_parts, prior, run, base, after):
        return attend(info, slots, q, grad_o, kv_parts, dense_w, prior, run, base, after)

    o_most_early, stat_most_early, summed_early = forward(kv_most, mlp_part, 0, 0, ())
    o_most_late, stat_most_late, summed_late = forward(kv_most, mlp_part, 1, 0, (o_most_early,))
    o_last_early, stat_last_early, send, keep_early = forward(kv_last, summed_early, 0, pairs - 1, (o_most_late,))
    got_early = swap(send, "ml")
    o_last_late, stat_last_late, send, keep_late = forward(kv_last, summed_late, 1, pairs - 1, (o_last_early,))
    got_late = swap(send, "ml")
    stats = jnp.concatenate(
        [
            jnp.concatenate([stat_most_early, stat_last_early], axis=0),
            jnp.concatenate([stat_most_late, stat_last_late], axis=0),
        ],
        axis=1,
    )
    attended = jnp.concatenate(
        [
            jnp.concatenate([o_most_early, o_last_early], axis=1),
            jnp.concatenate([o_most_late, o_last_late], axis=1),
        ],
        axis=0,
    )
    mixed_early = finish(which, tokens, keep_early, got_early, row_of(0), row_of(1), 0, (o_last_late,))
    after = (mixed_early,)
    mixed_early = lax.all_gather(mixed_early, ("mh", "ml"), axis=0, tiled=True)

    home = rows if seq_size == 2 else 0
    dq, dk, dv, got = [], [], [], []
    for pair in range(pairs):
        kv_parts, at = (kv_last, 0) if pair == pairs - 1 else (kv_most, pair)
        outs = attend_back(info, slots, q, grad_o, stats, kv_parts, pair, at, home, after)
        after = (outs[0],)
        dq.append(outs[0])
        if home:
            dk.append(outs[1])
            dv.append(outs[2])
            got.append(swap(outs[3], "seq"))
        else:
            both = jnp.concatenate([outs[1], outs[2]], axis=1).astype(BF16)
            got.append(lax.psum_scatter(both, "seq", scatter_dimension=0, tiled=True))
            dk.append(jnp.zeros((rows, LANES), F32))
            dv.append(jnp.zeros((rows, LANES), F32))
        if pair == 1:
            mixed_late = finish(which, tokens, keep_late, got_late, row_of(0), row_of(1), 1, (outs[0], got[0]))
            after = (outs[0], mixed_late)
            mixed_late = lax.all_gather(mixed_late, ("mh", "ml"), axis=0, tiled=True)
        elif pair > 1:
            after = (outs[0], got[pair - 1])
    feed_weights, mlp_vectors, grad_up_b = feed_grads(
        which, tokens, out_grad, act, mlp_grad, up_w, column_of(4), column_of(5), after + (mixed_early,)
    )
    dq = jnp.concatenate(dq, axis=1)
    dproj, send, keep = back(
        which, dq, dk, dv, got, qkv_w, row_of(2), mlp_dx, tables, (grad_up_b,)
    )
    mixed = lay_gathered(mixed_early, mixed_late, (dproj,))
    got = [swap(send[run * quarter : (run + 1) * quarter], "ml") for run in range(2)]
    grad_qkv, grad_dense, qkv_vectors, grad_qkv_b = weight_grads(
        which, tokens, out_grad, dproj, attended, qkv_w, column_of(2), column_of(3), (mixed_late,)
    )
    ties = ((grad_qkv_b,), (grad_qkv_b,))
    input_grad = [norm_back(which, tokens, out_grad, keep, got[run], run, ties[run]) for run in range(2)]
    travelled = [line_mp(rows_done) for rows_done in input_grad]
    input_grad = lay_line(index, *travelled)

    def scatter(grads):
        return lax.psum_scatter(grads, ("dp", "seq"), scatter_dimension=0, tiled=True)

    vector_grads = (mlp_vectors + qkv_vectors)[:, None, :5]
    vector_grads = jnp.broadcast_to(vector_grads, (width, 2, 5))
    bias_qkv = grad_qkv_b.reshape(3, 2, heads, owners, piece).transpose(3, 0, 2, 4, 1)
    bias_qkv = bias_qkv.reshape(owners, 3 * heads * piece, 2)
    bias_qkv = jnp.pad(bias_qkv, ((0, 0), (0, share - 3 * heads * piece), (0, 0))).reshape(width, 2, 1)
    bias_up = grad_up_b.reshape(2, up_rows, owners, up_cols).transpose(2, 1, 3, 0).reshape(width, 2, 1)
    tail = jnp.concatenate([vector_grads, bias_qkv, bias_up], axis=2)
    tail = jnp.pad(tail, ((0, 0), (0, 0), (0, LANES // 2 - 7))).astype(BF16).reshape(width, LANES)
    packed = scatter(join((grad_qkv, grad_dense, tail, feed_weights)))
    segments = (cols,) * 4 + (LANES // 2, units, units)
    kept, sent = sides(which, packed, segments, [travelled[1][at] for at in (2, 5)])
    owned = kept.astype(F32) + swap(sent, "mh").astype(F32)
    owned, owned_feed = owned[:, : 4 * cols + LANES // 2], owned[:, 4 * cols + LANES // 2 :]
    vectors = owned[:, 4 * cols :]
    norms = vectors[:, :5]
    norms = norms + swap(norms, "ml")
    bias_grad = norms[:, 0]
    return (
        mixed,
        input_grad,
        owned[:, : 3 * cols].reshape(share, 3, cols).transpose(1, 0, 2),
        vectors[: 3 * heads * piece, 5].reshape(b_qkv.shape),
        owned[:, 3 * cols : 4 * cols].T,
        bias_grad,
        owned_feed[:, :units],
        vectors[:, 6].reshape(b_up.shape),
        owned_feed[:, units:].T,
        bias_grad,
        norms[:, 1],
        norms[:, 2],
        norms[:, 3],
        norms[:, 4],
    )


def solution(mesh):
    dp, seq, mp = (mesh.shape[axis] for axis in ("dp", "seq", "mp"))
    split = Mesh(mesh.devices.reshape(dp, seq, 2, mp // 2), ("dp", "seq", "mh", "ml"))
    mp, owner = ("mh", "ml"), ("dp", "seq")
    row = P("dp", "seq", None)
    vector = P(owner)
    weights = (
        P(None, owner, mp), P(None, mp, owner), P(mp, owner), vector, P(owner, mp), P(mp, owner),
        P(mp, owner), vector, vector, vector, vector, vector,
    )
    return jax.shard_map(
        functools.partial(body, seq_size=seq, owners=dp * seq),
        mesh=split,
        in_specs=(row, P("dp", "seq")) + weights + (row,),
        out_specs=(row, row) + weights,
        check_vma=False,
    )
```
